32 devices in a mesh: stack: 8 (over z, y), azimuth: 2 (over x), range: 2 (over core).
Axes of the slice: x: 2, y: 2, z: 4, core: 2. Of those that a mesh axis runs over, the one named last changes fastest.
Arguments:
- phases: bfloat16 [1152, 4, 2048], P('stack', 'azimuth', 'range'), may hold values from -6 to 6
- ifg_pairs: int32 [1152, 2], replicated, may hold values from 0 to 599, as said below
- preconditioner: float32 [600, 600], replicated, as said below
- coherence: int32 [4, 2048], P('azimuth', ('range', 'stack')), may hold values 0 or 1
- geo_tiles: int32 [4, 2048], P('azimuth', ('range', 'stack')), may hold values from 0 to 15, as said below
Outputs:
- deramped: float32 [600, 4, 2048], P(None, 'azimuth', ('range', 'stack'))
The draws below stay inside these ranges and needn't reach their ends.
Inputs may be any that keep to these rules, and one draw needn't show every extreme that they name: `ifg_pairs`: each row names an earlier date first and a later date second. `preconditioner`: a symmetric matrix. geo_tiles[r, c] = min(max(floor((c + shift_r) / 128), 0), 15) with one integer shift_r per slab row, -32 <= shift_r <= 32; some row has shift -32 and another +32.
All inputs are finite; a program needn't handle non-finite values. No bound on the sum of `coherence` on one device may be relied on, other than what follows from the above.
Results may differ from the reference program's by a relative error of at most 0.002.
Values may be sent and summed in bfloat16 or wider, within the bound.
No kernel may reach another device: no remote copies, remote signals or barrier semaphores. Data moves between devices by JAX's collectives and lax.ppermute only.
A program may use at most 64 MiB of HBM per device.

```python
import jax
import jax.numpy as jnp
from jax import lax

IFG_COUNT = 1152
DATE_COUNT = 600
REWEIGHTS = 2
COL_DEV = 128
SKEW = 32
SLAB_ROWS = 4
SLAB_COLS = 2048
GEO_TILES = 16


def draw_ifg_pairs(key, part):
    key_start, key_gap = jax.random.split(jax.random.fold_in(key, 11))
    start_date = jax.random.randint(key_start, (IFG_COUNT,), 0, DATE_COUNT)
    gap_days = jax.random.randint(key_gap, (IFG_COUNT,), 1, DATE_COUNT)
    other_date = (start_date + gap_days) % DATE_COUNT
    earlier_date = jnp.minimum(start_date, other_date)
    later_date = jnp.maximum(start_date, other_date)
    row_ids = jnp.arange(IFG_COUNT, dtype=jnp.int32)
    earlier_date = jnp.where(row_ids == 0, 0, earlier_date)
    later_date = jnp.where(row_ids == 0, DATE_COUNT - 1, later_date)
    return jnp.stack([earlier_date, later_date], axis=1).astype(jnp.int32)


def draw_preconditioner(key, part):
    key_diag, key_noise = jax.random.split(jax.random.fold_in(key, 23))
    diagonal = jax.random.uniform(key_diag, (DATE_COUNT,), jnp.float32, 0.04, 0.06)
    noise = jax.random.normal(key_noise, (DATE_COUNT, DATE_COUNT), jnp.float32) * 0.0006
    symmetric = 0.5 * (noise + noise.T)
    return (symmetric + jnp.diag(diagonal)).astype(jnp.float32)


def draw_geo_tiles(key, part):
    row_shift = jax.random.randint(jax.random.fold_in(key, 37), (SLAB_ROWS,), -SKEW, SKEW + 1).astype(jnp.int32)
    row_ids = jnp.arange(SLAB_ROWS, dtype=jnp.int32)
    row_shift = jnp.where(row_ids == 0, -SKEW, row_shift)
    row_shift = jnp.where(row_ids == 1, SKEW, row_shift)
    col_ids = jnp.arange(SLAB_COLS, dtype=jnp.int32)
    tiles = jnp.floor_divide(col_ids[None, :] + row_shift[:, None], COL_DEV)
    return jnp.clip(tiles, 0, GEO_TILES - 1).astype(jnp.int32)


def place_ends(result, key, least, top_value):
    longest = result.shape.index(max(result.shape))
    spots = []
    for shift in (0, 1):
        where = [jax.random.randint(jax.random.fold_in(key, axis), (), 0, length) for axis, length in enumerate(result.shape)]
        where[longest] = (where[longest] + shift) % result.shape[longest]
        spots.append(tuple(where))
    return result.at[spots[0]].set(least).at[spots[1]].set(top_value)


def steps_of(own_key, dims, cuts, least, largest):
    loudness = 1.0
    for position, shards_of in cuts:
        heights = jax.random.uniform(jax.random.fold_in(jax.random.fold_in(own_key, 6), position), (shards_of,), jnp.float32, least / len(cuts), largest / len(cuts))
        loudness = loudness * jnp.repeat(jnp.exp(heights), dims[position] // shards_of).reshape((-1,) + (1,) * (len(dims) - 1 - position))
    return loudness


def gaussian(stream_key, dims, scale, most, cuts=(), kind=jnp.bfloat16):
    level = steps_of(stream_key, dims, cuts, -0.22, 0.18) if cuts else 1.0
    array = jax.random.normal(stream_key, dims, jnp.float32) * scale * level
    return jnp.minimum(jnp.maximum(array, -most), most).astype(kind)


def setup_inputs(seed: int = 0) -> dict:
    streams_of = jax.random.split(jax.random.key(seed), 6)
    return {
        "phases": gaussian(streams_of[0], (IFG_COUNT, SLAB_ROWS, SLAB_COLS), 1.0, 6.0, ((0, 8), (1, 2), (2, 2))),
        "ifg_pairs": draw_ifg_pairs(jax.random.fold_in(streams_of[5], 71), 0),
        "preconditioner": draw_preconditioner(jax.random.fold_in(streams_of[5], 71), 0),
        "coherence": place_ends((jax.random.randint(streams_of[3], (SLAB_ROWS, SLAB_COLS), 0, 4) < 3).astype(jnp.int32), jax.random.fold_in(streams_of[3], 1), 0, 1),
        "geo_tiles": draw_geo_tiles(jax.random.fold_in(streams_of[5], 71), 0),
    }


def plane_solve(gram_matrix, right_side):
    def entry(row_pos, col_pos):
        return gram_matrix[row_pos % 3, col_pos % 3]

    cofactors = [[entry(row_pos + 1, col_pos + 1) * entry(row_pos + 2, col_pos + 2) - entry(row_pos + 1, col_pos + 2) * entry(row_pos + 2, col_pos + 1) for col_pos in range(3)] for row_pos in range(3)]
    determinant = entry(0, 0) * cofactors[0][0] + entry(0, 1) * cofactors[0][1] + entry(0, 2) * cofactors[0][2]
    solution = [(cofactors[0][col_pos] * right_side[0] + cofactors[1][col_pos] * right_side[1] + cofactors[2][col_pos] * right_side[2]) / determinant for col_pos in range(3)]
    return jnp.stack(solution)


def invert_pixels(stack_data, coherence_row, incidence, incidence_half, earlier_date, later_date, preconditioner):
    normal_rhs = lax.dot_general(incidence_half, stack_data, (((0,), (0,)), ((), ())), preferred_element_type=jnp.float32)
    series = jnp.dot(preconditioner, normal_rhs, precision=lax.Precision.HIGHEST, preferred_element_type=jnp.float32)
    values = stack_data.astype(jnp.float32)
    for sweep in range(REWEIGHTS):
        residual = values - (series[later_date] - series[earlier_date])
        square = residual * residual
        robust_scale = jnp.mean(square, axis=0) + 1e-6
        shifted = square + robust_scale
        weight = coherence_row * (robust_scale * robust_scale) / (shifted * shifted)
        update = lax.dot_general(incidence, weight * residual, (((0,), (0,)), ((), ())), precision=lax.Precision.HIGHEST, preferred_element_type=jnp.float32)
        series = series + jnp.dot(preconditioner, update, precision=lax.Precision.HIGHEST, preferred_element_type=jnp.float32)
    return series


def reference(phases, ifg_pairs, preconditioner, coherence, geo_tiles):
    earlier_date = ifg_pairs[:, 0]
    later_date = ifg_pairs[:, 1]
    date_ids = jnp.arange(DATE_COUNT, dtype=jnp.int32)
    incidence = (later_date[:, None] == date_ids).astype(jnp.float32) - (earlier_date[:, None] == date_ids).astype(jnp.float32)
    incidence_half = incidence.astype(jnp.bfloat16)
    block_count = SLAB_COLS // COL_DEV
    row_coord = (jnp.arange(SLAB_ROWS, dtype=jnp.float32) + 0.5) / SLAB_ROWS - 0.5

    def block_basis(block_index):
        col_ids = block_index * COL_DEV + jnp.arange(COL_DEV, dtype=jnp.int32)
        col_coord = (col_ids.astype(jnp.float32) + 0.5) / SLAB_COLS - 0.5
        coord_u = jnp.broadcast_to(row_coord[:, None], (SLAB_ROWS, COL_DEV)).reshape(-1)
        coord_v = jnp.broadcast_to(col_coord[None, :], (SLAB_ROWS, COL_DEV)).reshape(-1)
        coherence_blk = lax.dynamic_slice_in_dim(coherence, block_index * COL_DEV, COL_DEV, 1).reshape(-1).astype(jnp.float32)
        tiles_blk = lax.dynamic_slice_in_dim(geo_tiles, block_index * COL_DEV, COL_DEV, 1).reshape(-1).astype(jnp.int32)
        return coord_u, coord_v, coherence_blk, tiles_blk

    def solve_block(block_index):
        stack_data = lax.dynamic_slice_in_dim(phases, block_index * COL_DEV, COL_DEV, 2).reshape(IFG_COUNT, SLAB_ROWS * COL_DEV)
        coord_u, coord_v, coherence_blk, tiles_blk = block_basis(block_index)
        return invert_pixels(stack_data, coherence_blk, incidence, incidence_half, earlier_date, later_date, preconditioner)

    block_ids = jnp.arange(block_count, dtype=jnp.int32)
    series_blocks = lax.map(solve_block, block_ids)

    def accumulate(totals, block_index):
        moments, gram_matrix = totals
        coord_u, coord_v, coherence_blk, tiles_blk = block_basis(block_index)
        basis = jnp.stack([jnp.ones_like(coord_u), coord_u, coord_v])
        weighted_basis = basis * coherence_blk[None, :]
        series = series_blocks[block_index]
        term = (weighted_basis[:, None, :] * series[None, :, :]).transpose(2, 0, 1)
        moments = moments + jax.ops.segment_sum(term, tiles_blk, num_segments=GEO_TILES)
        products = (weighted_basis[:, None, :] * basis[None, :, :]).transpose(2, 0, 1)
        gram_matrix = gram_matrix + jax.ops.segment_sum(products, tiles_blk, num_segments=GEO_TILES)
        return (moments, gram_matrix), None

    start_totals = (jnp.zeros((GEO_TILES, 3, DATE_COUNT), jnp.float32), jnp.zeros((GEO_TILES, 3, 3), jnp.float32))
    (moments, gram_matrix), unused = lax.scan(accumulate, start_totals, block_ids)
    moments = moments.transpose(1, 2, 0)
    gram_matrix = gram_matrix.transpose(1, 2, 0) + jnp.eye(3, dtype=jnp.float32)[:, :, None]
    plane_coefs = plane_solve(gram_matrix, moments)

    def deramp_block(block_index):
        coord_u, coord_v, coherence_blk, tiles_blk = block_basis(block_index)
        picked = jnp.take(plane_coefs, tiles_blk, axis=2)
        return series_blocks[block_index] - (picked[0] + picked[1] * coord_u + picked[2] * coord_v)

    out_blocks = lax.map(deramp_block, block_ids)
    out_blocks = out_blocks.reshape(block_count, DATE_COUNT, SLAB_ROWS, COL_DEV).transpose(1, 2, 0, 3)
    return out_blocks.reshape(DATE_COUNT, SLAB_ROWS, SLAB_COLS)
```

```python
import functools

import jax
import jax.numpy as jnp
from jax import lax
from jax.experimental import pallas as pl
from jax.experimental.pallas import tpu as pltpu
from jax.sharding import PartitionSpec as P

REWEIGHTS = 2
LANES = 128
VMEM_LIMIT = 48 * 1024 * 1024
ROWS_A = 384
ROWS_B = 128


def halves(value):
    top = value.astype(jnp.bfloat16)
    return top, (value - top.astype(jnp.float32)).astype(jnp.bfloat16)


def product(left, right, dims=(((1,), (0,)), ((), ()))):
    return lax.dot_general(left, right, dims, preferred_element_type=jnp.float32)


def prepare_kernel(pairs_ref, prec_ref, hat_top, hat_low, gain_top, gain_low, *, date_pad):
    ifg_total = pairs_ref.shape[1]
    date_total = prec_ref.shape[0]
    pairs = pairs_ref[...]
    date_ids = lax.broadcasted_iota(jnp.int32, (date_total, ifg_total), 0)
    incidence_t = (
        jnp.where(date_ids == pairs[1:2], 1.0, 0.0) - jnp.where(date_ids == pairs[0:1], 1.0, 0.0)
    ).astype(jnp.bfloat16)
    prec = prec_ref[...]
    top, rest = halves(prec)
    middle, low = halves(prec - top.astype(jnp.float32))
    gain = product(top, incidence_t) + (product(middle, incidence_t) + product(low, incidence_t))
    gain_a, gain_b = halves(gain)
    gain_top[pl.ds(0, date_total), :] = gain_a
    gain_low[pl.ds(0, date_total), :] = gain_b
    zeros = jnp.zeros((date_pad - date_total, ifg_total), jnp.bfloat16)
    gain_top[pl.ds(date_total, date_pad - date_total), :] = zeros
    gain_low[pl.ds(date_total, date_pad - date_total), :] = zeros
    incidence = incidence_t.T
    for start in range(0, ifg_total, ROWS_A):
        rows = incidence[start : start + ROWS_A]
        hat = product(rows, gain_a) + product(rows, gain_b)
        hat_a, hat_b = halves(hat)
        hat_top[pl.ds(start, ROWS_A), :] = hat_a
        hat_low[pl.ds(start, ROWS_A), :] = hat_b


def prepare(pairs_t, preconditioner, date_pad):
    ifg_total = pairs_t.shape[1]
    shapes = [(ifg_total, ifg_total)] * 2 + [(date_pad, ifg_total)] * 2
    return pl.pallas_call(
        functools.partial(prepare_kernel, date_pad=date_pad),
        out_shape=[jax.ShapeDtypeStruct(shape, jnp.bfloat16) for shape in shapes],
        compiler_params=pltpu.CompilerParams(vmem_limit_bytes=VMEM_LIMIT),
        name="prepare",
    )(pairs_t, preconditioner)


def invert_kernel(
    data_ref, hat_top, hat_low, gain_top, gain_low, coherence_ref, weighted_ref, basis_ref,
    series_ref, moments_ref, wide, data, residual, moved, *, row_local, date_total,
):
    ifg_total, pixel_count = data.shape
    date_pad = gain_top.shape[0]
    col_local = pixel_count // row_local
    wide[...] = data_ref[...].astype(jnp.float32)
    for row in range(row_local):
        part = wide[pl.ds(row, ifg_total, stride=row_local), :]
        data[:, row * col_local : (row + 1) * col_local] = part.astype(jnp.bfloat16)
    coherence = coherence_ref[...]

    def folded(square):
        return jnp.sum(square.reshape(-1, 8, pixel_count), axis=0)

    def robust(total):
        return jnp.sum(total, axis=0, keepdims=True) / ifg_total + 1e-06

    total = jnp.zeros((8, pixel_count), jnp.float32)
    for start in range(0, ifg_total, ROWS_A):
        rows = pl.ds(start, ROWS_A)
        fit = product(hat_top[rows, :], data[...]) + product(hat_low[rows, :], data[...])
        left = data[rows, :].astype(jnp.float32) - fit
        residual[rows, :] = left
        total = total + folded(left * left)
    for sweep in range(REWEIGHTS):
        scale = robust(total)
        for start in range(0, ifg_total, ROWS_B):
            rows = pl.ds(start, ROWS_B)
            left = residual[rows, :]
            ratio = scale / (left * left + scale)
            moved[rows, :] = (coherence * (ratio * ratio) * left).astype(jnp.bfloat16)
        source = data if sweep == 0 else None
        for start in range(0, date_pad, ROWS_B):
            rows = pl.ds(start, ROWS_B)
            part = product(gain_top[rows, :], moved[...]) + product(gain_low[rows, :], moved[...])
            if sweep == 0:
                part = part + (
                    product(gain_top[rows, :], data[...]) + product(gain_low[rows, :], data[...])
                )
            else:
                part = part + series_ref[rows, :]
            series_ref[rows, :] = part
        if sweep + 1 < REWEIGHTS:
            total = jnp.zeros((8, pixel_count), jnp.float32)
            for start in range(0, ifg_total, ROWS_A):
                rows = pl.ds(start, ROWS_A)
                left = residual[rows, :] - product(hat_top[rows, :], moved[...])
                residual[rows, :] = left
                total = total + folded(left * left)
    series_ref[pl.ds(date_total, 8), :] = basis_ref[...]
    series_top, series_low = halves(series_ref[...])
    weighted_top, weighted_low = halves(weighted_ref[...])
    across = (((1,), (1,)), ((), ()))
    moments_ref[...] = product(weighted_top, series_top, across) + (
        product(weighted_low, series_top, across) + product(weighted_top, series_low, across)
    )


def invert(data, hats, coherence, weighted, basis, row_local, date_total):
    hat_top, hat_low, gain_top, gain_low = hats
    ifg_total = hat_top.shape[0]
    date_pad = gain_top.shape[0]
    pixel_count = coherence.shape[1]
    return pl.pallas_call(
        functools.partial(invert_kernel, row_local=row_local, date_total=date_total),
        out_shape=[
            jax.ShapeDtypeStruct((date_pad, pixel_count), jnp.float32),
            jax.ShapeDtypeStruct((weighted.shape[0], date_pad), jnp.float32),
        ],
        scratch_shapes=[
            pltpu.VMEM(data.shape, jnp.float32),
            pltpu.VMEM((ifg_total, pixel_count), jnp.bfloat16),
            pltpu.VMEM((ifg_total, pixel_count), jnp.float32),
            pltpu.VMEM((ifg_total, pixel_count), jnp.bfloat16),
        ],
        compiler_params=pltpu.CompilerParams(vmem_limit_bytes=VMEM_LIMIT),
        name="invert",
    )(data, *hats, coherence, weighted, basis)


def plane_solve(gram_matrix, right_side):

    def entry(row_pos, col_pos):
        return gram_matrix[row_pos % 3][col_pos % 3]

    cofactors = [
        [
            entry(row_pos + 1, col_pos + 1) * entry(row_pos + 2, col_pos + 2)
            - entry(row_pos + 1, col_pos + 2) * entry(row_pos + 2, col_pos + 1)
            for col_pos in range(3)
        ]
        for row_pos in range(3)
    ]
    determinant = (
        entry(0, 0) * cofactors[0][0]
        + entry(0, 1) * cofactors[0][1]
        + entry(0, 2) * cofactors[0][2]
    )
    return [
        (
            (cofactors[0][col_pos] / determinant) * right_side[0]
            + (cofactors[1][col_pos] / determinant) * right_side[1]
            + (cofactors[2][col_pos] / determinant) * right_side[2]
        )
        for col_pos in range(3)
    ]


def deramp_kernel(first_ref, *refs, row_local, date_total):
    *others, series_ref, member_ref, out_ref = refs
    totals = first_ref[...]
    for other in others:
        totals = totals + other[...]
    planes = []
    for base in (0, 3, 8, 11):
        gram = [
            [
                totals[base + k : base + k + 1, date_total + m : date_total + m + 1]
                + (1.0 if k == m else 0.0)
                for m in range(3)
            ]
            for k in range(3)
        ]
        planes += plane_solve(gram, [totals[base + k : base + k + 1, :] for k in range(3)])
        if base in (3, 11):
            planes += [jnp.zeros_like(planes[0])] * 2
    planes_top, planes_low = halves(jnp.concatenate(planes, axis=0))
    member_top, member_low = halves(member_ref[...])
    ramp = product(
        jnp.concatenate([planes_top, planes_low, planes_top], axis=0),
        jnp.concatenate([member_top, member_top, member_low], axis=0),
        (((0,), (0,)), ((), ())),
    )
    flat = series_ref[pl.ds(0, date_total), :] - ramp[:date_total]
    col_local = flat.shape[1] // row_local
    for row in range(row_local):
        out_ref[pl.ds(row, date_total, stride=row_local), :] = flat[
            :, row * col_local : (row + 1) * col_local
        ]


def deramp(parts, series, member, row_local, date_total):
    col_local = series.shape[1] // row_local
    return pl.pallas_call(
        functools.partial(deramp_kernel, row_local=row_local, date_total=date_total),
        out_shape=jax.ShapeDtypeStruct((date_total * row_local, col_local), jnp.float32),
        compiler_params=pltpu.CompilerParams(vmem_limit_bytes=VMEM_LIMIT),
        name="deramp",
    )(*parts, series, member)


def swap(value, axes, pairs):
    both = [(i, j) for i, j in pairs] + [(j, i) for i, j in pairs]
    return lax.ppermute(value, axes, both)


def local(phases, ifg_pairs, preconditioner, coherence, geo_tiles):
    stack_size = lax.axis_size("stack")
    range_size = lax.axis_size("range")
    azimuth_size = lax.axis_size("azimuth")
    ifg_local, row_local, col_range = phases.shape
    col_local = col_range // stack_size
    pixel_count = row_local * col_local
    date_total = preconditioner.shape[0]
    date_pad = -(-(date_total + 8) // LANES) * LANES
    stack_pos = lax.axis_index("stack")
    block_index = lax.axis_index("range") * stack_size + stack_pos

    blocks = phases.reshape(ifg_local, row_local, stack_size, col_local).transpose(2, 0, 1, 3)
    stacked = lax.all_to_all(blocks, "stack", split_axis=0, concat_axis=0, tiled=True)
    data = stacked.reshape(stack_size * ifg_local * row_local, col_local)

    hats = prepare(ifg_pairs.T, preconditioner, date_pad)

    row_ids = lax.axis_index("azimuth") * row_local + jnp.arange(row_local, dtype=jnp.int32)
    col_ids = block_index * col_local + jnp.arange(col_local, dtype=jnp.int32)
    row_coord = (row_ids.astype(jnp.float32) + 0.5) / (row_local * azimuth_size) - 0.5
    col_coord = (col_ids.astype(jnp.float32) + 0.5) / (col_range * range_size) - 0.5
    shape = (row_local, col_local)
    coord_u = jnp.broadcast_to(row_coord[:, None], shape).reshape(1, pixel_count)
    coord_v = jnp.broadcast_to(col_coord[None, :], shape).reshape(1, pixel_count)
    basis = jnp.concatenate([jnp.ones_like(coord_u), coord_u, coord_v], axis=0)
    coherence_f = coherence.astype(jnp.float32).reshape(1, pixel_count)
    tiles = geo_tiles.reshape(1, pixel_count)

    node = block_index // 2
    even = node % 2 == 0
    first_tile = jnp.where(even, 2 * node + 1, 2 * node - 1)
    second_tile = jnp.where(even, 2 * node - 1, 2 * node + 1)
    spare = jnp.zeros((2, pixel_count), jnp.float32)
    member_rows = []
    for base in (first_tile, second_tile):
        for step in range(2):
            member_rows.append(basis * (tiles == base + step).astype(jnp.float32))
        member_rows.append(spare)
    member = jnp.concatenate(member_rows, axis=0)
    weighted = member * coherence_f
    basis8 = jnp.concatenate([basis, jnp.zeros((5, pixel_count), jnp.float32)], axis=0)

    series, moments = invert(
        data, hats, coherence_f, weighted, basis8, row_local, date_total
    )

    def place(block):
        return (block % stack_size) * range_size + block // stack_size

    block_count = stack_size * range_size
    inner = [
        (place(block), place(block + 2)) for block in range(block_count - 2) if block // 2 % 2 == 0
    ]
    outer = [
        (place(block), place(block + 2)) for block in range(block_count - 2) if block // 2 % 2 == 1
    ]
    axes = ("stack", "range")
    second = swap(moments[8:], axes, outer)
    first = swap(moments[:8], axes, inner)
    moments = moments + jnp.concatenate([first, second], axis=0)
    pairs = [(i, i + 1) for i in range(0, stack_size, 2)]
    crossed = [
        (i * azimuth_size + a, (i + 1) * azimuth_size + (azimuth_size - 1 - a))
        for i in range(0, stack_size, 2)
        for a in range(azimuth_size)
    ]
    parts = [
        moments,
        swap(moments, "azimuth", [(0, 1)]),
        swap(moments, "stack", pairs),
        swap(moments, ("stack", "azimuth"), crossed),
    ]
    flat = deramp(parts, series, member, row_local, date_total)
    return flat.reshape(date_total, row_local, col_local)


def solution(mesh):
    return jax.shard_map(
        local,
        mesh=mesh,
        in_specs=(
            P("stack", "azimuth", "range"),
            P(),
            P(),
            P("azimuth", ("range", "stack")),
            P("azimuth", ("range", "stack")),
        ),
        out_specs=P(None, "azimuth", ("range", "stack")),
        check_vma=False,
    )
```

```python
import functools

import jax
import jax.numpy as jnp
from jax import lax
from jax.experimental import pallas as pl
from jax.experimental.pallas import tpu as pltpu
from jax.sharding import PartitionSpec as P

REWEIGHTS = 2
LANES = 128
VMEM_LIMIT = 24 * 1024 * 1024
ROWS_A = 128
ROWS_B = 128
ARRIVAL = (0, 1, 4, 5, 2, 6, 7, 3)
EARLY = 6


def halves(value):
    top = value.astype(jnp.bfloat16)
    return top, (value - top.astype(jnp.float32)).astype(jnp.bfloat16)


def product(left, right, dims=(((1,), (0,)), ((), ()))):
    return lax.dot_general(left, right, dims, preferred_element_type=jnp.float32)


def prepare_kernel(place_ref, pairs_ref, prec_ref, incidence_ref, gain_top, gain_low, pairs, *, order):
    chunk = pairs_ref.shape[2]
    date_total = prec_ref.shape[0]
    date_pad, ifg_total = gain_top.shape
    place = place_ref[0]
    for position, mask in enumerate(order):
        pairs[:, position * chunk : (position + 1) * chunk] = pairs_ref[place ^ mask]
    date_ids = lax.broadcasted_iota(jnp.int32, (date_pad, ifg_total), 0)
    incidence_t = (
        jnp.where(date_ids == pairs[1:2, :], 1.0, 0.0)
        - jnp.where(date_ids == pairs[0:1, :], 1.0, 0.0)
    ).astype(jnp.bfloat16)
    incidence_ref[...] = incidence_t.T
    prec = prec_ref[...]
    top, rest = halves(prec)
    middle, low = halves(prec - top.astype(jnp.float32))
    used = incidence_t[:date_total]
    gain = product(top, used) + (product(middle, used) + product(low, used))
    gain_a, gain_b = halves(gain)
    zeros = jnp.zeros((date_pad - date_total, ifg_total), jnp.bfloat16)
    gain_top[...] = jnp.concatenate([gain_a, zeros], axis=0)
    gain_low[...] = jnp.concatenate([gain_b, zeros], axis=0)


def prepare(place, pairs, preconditioner, date_pad, order):
    ifg_total = pairs.shape[0] * pairs.shape[2]
    shapes = [(ifg_total, date_pad)] + [(date_pad, ifg_total)] * 2
    whole = pl.BlockSpec(memory_space=pltpu.VMEM)
    return pl.pallas_call(
        functools.partial(prepare_kernel, order=order),
        out_shape=[jax.ShapeDtypeStruct(shape, jnp.bfloat16) for shape in shapes],
        in_specs=[pl.BlockSpec(memory_space=pltpu.SMEM), whole, whole],
        out_specs=[whole] * 3,
        scratch_shapes=[pltpu.VMEM((2, ifg_total), jnp.int32)],
        compiler_params=pltpu.CompilerParams(vmem_limit_bytes=VMEM_LIMIT),
        name="prepare",
    )(place, pairs, preconditioner)


def unpack(chunk_refs, wide, data, row_local):
    start = 0
    col_local = chunk_refs[0].shape[1]
    for ref in chunk_refs:
        count = ref.shape[0] // row_local
        wide[pl.ds(0, ref.shape[0]), :] = ref[...].astype(jnp.float32)
        for row in range(row_local):
            data[pl.ds(start, count), row * col_local : (row + 1) * col_local] = wide[
                pl.ds(row, count, stride=row_local), :
            ].astype(jnp.bfloat16)
        start += count


def gained(gain_top, gain_low, rows, columns, value):
    part = product(gain_top[rows, columns], value)
    if gain_low is not None:
        part = part + product(gain_low[rows, columns], value)
    return part


def early_kernel(*refs, row_local):
    *chunk_refs, gain_top, gain_low, data_ref, series_ref, wide = refs
    unpack(chunk_refs, wide, data_ref, row_local)
    columns = pl.ds(0, data_ref.shape[0] // 256 * 256)
    for start in range(0, series_ref.shape[0], ROWS_B):
        rows = pl.ds(start, ROWS_B)
        series_ref[rows, :] = gained(gain_top, gain_low, rows, columns, data_ref[columns, :])


def early_fit(chunks, gains, row_local):
    count = sum(chunk.shape[0] for chunk in chunks) // row_local
    pixel_count = chunks[0].shape[1] * row_local
    return pl.pallas_call(
        functools.partial(early_kernel, row_local=row_local),
        out_shape=[
            jax.ShapeDtypeStruct((count, pixel_count), jnp.bfloat16),
            jax.ShapeDtypeStruct((gains[0].shape[0], pixel_count), jnp.float32),
        ],
        scratch_shapes=[pltpu.VMEM(chunks[0].shape, jnp.float32)],
        compiler_params=pltpu.CompilerParams(vmem_limit_bytes=VMEM_LIMIT),
        name="early_fit",
    )(*chunks, *gains)


def invert_kernel(*refs, row_local, date_total, late):
    (
        *chunk_refs, incidence, gain_top, gain_low, coherence_ref, weighted_ref, basis_ref,
        series_ref, moments_ref, wide, data, residual, moved,
    ) = refs
    ifg_total, pixel_count = data.shape
    date_pad = gain_top.shape[0]
    late_refs, early_refs = chunk_refs[:late], chunk_refs[late:]
    done = 0
    if early_refs:
        early_data, early_series = early_refs
        held = early_data.shape[0]
        done = held // 256 * 256
        data[pl.ds(0, held), :] = early_data[...]
        unpack(late_refs, wide, data.at[pl.ds(held, ifg_total - held)], row_local)
    else:
        unpack(late_refs, wide, data, row_local)
    coherence = coherence_ref[...]
    date_tiles = [pl.ds(start, ROWS_B) for start in range(0, date_pad, ROWS_B)]
    ifg_tiles = [pl.ds(start, ROWS_A) for start in range(0, ifg_total, ROWS_A)]
    everything = slice(None)

    def folded(square):
        return jnp.sum(square.reshape(-1, 8, pixel_count), axis=0)

    def reweighted(total):
        scale = jnp.sum(total, axis=0, keepdims=True) / ifg_total + 1e-06
        for rows in ifg_tiles:
            left = residual[rows, :]
            ratio = scale / (left * left + scale)
            moved[rows, :] = (coherence * (ratio * ratio) * left).astype(jnp.bfloat16)

    left_columns = pl.ds(done, ifg_total - done)
    tops, lows = [], []
    for rows in date_tiles:
        part = gained(gain_top, gain_low, rows, left_columns, data[left_columns, :])
        if early_refs:
            part = part + early_series[rows, :]
        series_ref[rows, :] = part
        top, low = halves(part)
        tops.append(top)
        lows.append(low)
    top, low = jnp.concatenate(tops, axis=0), jnp.concatenate(lows, axis=0)
    total = jnp.zeros((8, pixel_count), jnp.float32)
    for rows in ifg_tiles:
        fit = product(incidence[rows, :], top) + product(incidence[rows, :], low)
        left = data[rows, :].astype(jnp.float32) - fit
        residual[rows, :] = left
        total = total + folded(left * left)
    reweighted(total)
    for sweep in range(1, REWEIGHTS):
        steps = []
        for rows in date_tiles:
            part = gained(gain_top, gain_low, rows, everything, moved[...])
            steps.append(part.astype(jnp.bfloat16))
            series_ref[rows, :] = series_ref[rows, :] + part
        step = jnp.concatenate(steps, axis=0)
        total = jnp.zeros((8, pixel_count), jnp.float32)
        for rows in ifg_tiles:
            left = residual[rows, :] - product(incidence[rows, :], step)
            residual[rows, :] = left
            total = total + folded(left * left)
        reweighted(total)
    for rows in date_tiles:
        part = gained(gain_top, None, rows, everything, moved[...])
        series_ref[rows, :] = series_ref[rows, :] + part
    series_ref[pl.ds(date_total, 8), :] = basis_ref[...]
    series_top, series_low = halves(series_ref[...])
    weighted_top, weighted_low = halves(weighted_ref[...])
    across = (((1,), (1,)), ((), ()))
    moments_ref[...] = product(weighted_top, series_top, across) + (
        product(weighted_low, series_top, across) + product(weighted_top, series_low, across)
    )


def invert(late_chunks, early, incidence, gains, coherence, weighted, basis, row_local, date_total):
    ifg_total = incidence.shape[0]
    date_pad = gains[0].shape[0]
    pixel_count = coherence.shape[1]
    return pl.pallas_call(
        functools.partial(
            invert_kernel, row_local=row_local, date_total=date_total, late=len(late_chunks)
        ),
        out_shape=[
            jax.ShapeDtypeStruct((date_pad, pixel_count), jnp.float32),
            jax.ShapeDtypeStruct((weighted.shape[0], date_pad), jnp.float32),
        ],
        scratch_shapes=[
            pltpu.VMEM(late_chunks[0].shape, jnp.float32),
            pltpu.VMEM((ifg_total, pixel_count), jnp.bfloat16),
            pltpu.VMEM((ifg_total, pixel_count), jnp.float32),
            pltpu.VMEM((ifg_total, pixel_count), jnp.bfloat16),
        ],
        compiler_params=pltpu.CompilerParams(vmem_limit_bytes=VMEM_LIMIT),
        name="invert",
    )(*late_chunks, *early, incidence, *gains, coherence, weighted, basis)


def exchange(phases, stack_pos, stack_size):
    ifg_local, row_local, col_range = phases.shape
    col_local = col_range // stack_size
    if stack_size != 8:
        blocks = phases.reshape(ifg_local, row_local, stack_size, col_local).transpose(2, 0, 1, 3)
        stacked = lax.all_to_all(blocks, "stack", split_axis=0, concat_axis=0, tiled=True)
        return [stacked.reshape(-1, col_local)], []
    blocks = [
        lax.dynamic_slice_in_dim(phases, (stack_pos ^ mask) * col_local, col_local, axis=2)
        for mask in range(stack_size)
    ]
    found = {0: blocks[0]}

    def send(mask, after=None):
        block = blocks[mask]
        if after is not None:
            block, found[after] = lax.optimization_barrier((block, found[after]))
        found[mask] = lax.ppermute(block, "stack", [(i, i ^ mask) for i in range(stack_size)])

    for mask, after in ((4, None), (5, None), (1, None), (6, None), (2, None), (7, 1), (3, 2)):
        send(mask, after)
    return [found[mask].reshape(-1, col_local) for mask in ARRIVAL], ARRIVAL


def plane_solve(gram_matrix, right_side):

    def entry(row_pos, col_pos):
        return gram_matrix[row_pos % 3][col_pos % 3]

    cofactors = [
        [
            entry(row_pos + 1, col_pos + 1) * entry(row_pos + 2, col_pos + 2)
            - entry(row_pos + 1, col_pos + 2) * entry(row_pos + 2, col_pos + 1)
            for col_pos in range(3)
        ]
        for row_pos in range(3)
    ]
    determinant = (
        entry(0, 0) * cofactors[0][0]
        + entry(0, 1) * cofactors[0][1]
        + entry(0, 2) * cofactors[0][2]
    )
    return [
        (
            (cofactors[0][col_pos] / determinant) * right_side[0]
            + (cofactors[1][col_pos] / determinant) * right_side[1]
            + (cofactors[2][col_pos] / determinant) * right_side[2]
        )
        for col_pos in range(3)
    ]


def deramp_kernel(first_ref, *refs, row_local, date_total):
    *others, series_ref, member_ref, out_ref = refs
    totals = first_ref[...]
    for other in others:
        totals = totals + other[...]
    planes = []
    for base in (0, 3, 8, 11):
        gram = [
            [
                totals[base + k : base + k + 1, date_total + m : date_total + m + 1]
                + (1.0 if k == m else 0.0)
                for m in range(3)
            ]
            for k in range(3)
        ]
        planes += plane_solve(gram, [totals[base + k : base + k + 1, :] for k in range(3)])
        if base in (3, 11):
            planes += [jnp.zeros_like(planes[0])] * 2
    planes_top, planes_low = halves(jnp.concatenate(planes, axis=0))
    member_top, member_low = halves(member_ref[...])
    ramp = product(
        jnp.concatenate([planes_top, planes_low, planes_top], axis=0),
        jnp.concatenate([member_top, member_top, member_low], axis=0),
        (((0,), (0,)), ((), ())),
    )
    flat = series_ref[pl.ds(0, date_total), :] - ramp[:date_total]
    col_local = flat.shape[1] // row_local
    for row in range(row_local):
        out_ref[pl.ds(row, date_total, stride=row_local), :] = flat[
            :, row * col_local : (row + 1) * col_local
        ]


def deramp(parts, series, member, row_local, date_total):
    col_local = series.shape[1] // row_local
    return pl.pallas_call(
        functools.partial(deramp_kernel, row_local=row_local, date_total=date_total),
        out_shape=jax.ShapeDtypeStruct((date_total * row_local, col_local), jnp.float32),
        compiler_params=pltpu.CompilerParams(vmem_limit_bytes=VMEM_LIMIT),
        name="deramp",
    )(*parts, series, member)


def swap(value, axes, pairs):
    both = [(i, j) for i, j in pairs] + [(j, i) for i, j in pairs]
    return lax.ppermute(value, axes, both)


def local(phases, ifg_pairs, preconditioner, coherence, geo_tiles):
    stack_size = lax.axis_size("stack")
    range_size = lax.axis_size("range")
    azimuth_size = lax.axis_size("azimuth")
    ifg_local, row_local, col_range = phases.shape
    col_local = col_range // stack_size
    pixel_count = row_local * col_local
    date_total = preconditioner.shape[0]
    date_pad = -(-(date_total + 8) // LANES) * LANES
    stack_pos = lax.axis_index("stack")
    block_index = lax.axis_index("range") * stack_size + stack_pos

    chunks, order = exchange(phases, stack_pos, stack_size)
    pairs = ifg_pairs.T.reshape(2, stack_size, ifg_local).transpose(1, 0, 2)
    place = stack_pos
    if not order:
        pairs = ifg_pairs.T[None]
        place, order = jnp.int32(0), [0]
    incidence, *gains = prepare(
        place.astype(jnp.int32).reshape(1), pairs, preconditioner, date_pad, order
    )
    early = []
    if len(chunks) > EARLY:
        early = early_fit(chunks[:EARLY], gains, row_local)
        chunks = chunks[EARLY:]

    row_ids = lax.axis_index("azimuth") * row_local + jnp.arange(row_local, dtype=jnp.int32)
    col_ids = block_index * col_local + jnp.arange(col_local, dtype=jnp.int32)
    row_coord = (row_ids.astype(jnp.float32) + 0.5) / (row_local * azimuth_size) - 0.5
    col_coord = (col_ids.astype(jnp.float32) + 0.5) / (col_range * range_size) - 0.5
    shape = (row_local, col_local)
    coord_u = jnp.broadcast_to(row_coord[:, None], shape).reshape(1, pixel_count)
    coord_v = jnp.broadcast_to(col_coord[None, :], shape).reshape(1, pixel_count)
    basis = jnp.concatenate([jnp.ones_like(coord_u), coord_u, coord_v], axis=0)
    coherence_f = coherence.astype(jnp.float32).reshape(1, pixel_count)
    tiles = geo_tiles.reshape(1, pixel_count)

    node = block_index // 2
    even = node % 2 == 0
    first_tile = jnp.where(even, 2 * node + 1, 2 * node - 1)
    second_tile = jnp.where(even, 2 * node - 1, 2 * node + 1)
    spare = jnp.zeros((2, pixel_count), jnp.float32)
    member_rows = []
    for base in (first_tile, second_tile):
        for step in range(2):
            member_rows.append(basis * (tiles == base + step).astype(jnp.float32))
        member_rows.append(spare)
    member = jnp.concatenate(member_rows, axis=0)
    weighted = member * coherence_f
    basis8 = jnp.concatenate([basis, jnp.zeros((5, pixel_count), jnp.float32)], axis=0)

    series, moments = invert(
        chunks, early, incidence, gains, coherence_f, weighted, basis8, row_local, date_total
    )

    def place(block):
        return (block % stack_size) * range_size + block // stack_size

    block_count = stack_size * range_size
    inner = [
        (place(block), place(block + 2)) for block in range(block_count - 2) if block // 2 % 2 == 0
    ]
    outer = [
        (place(block), place(block + 2)) for block in range(block_count - 2) if block // 2 % 2 == 1
    ]
    axes = ("stack", "range")
    second = swap(moments[8:], axes, outer)
    first = swap(moments[:8], axes, inner)
    moments = moments + jnp.concatenate([first, second], axis=0)
    pairs = [(i, i + 1) for i in range(0, stack_size, 2)]
    crossed = [
        (i * azimuth_size + a, (i + 1) * azimuth_size + (azimuth_size - 1 - a))
        for i in range(0, stack_size, 2)
        for a in range(azimuth_size)
    ]
    parts = [
        moments,
        swap(moments, "azimuth", [(0, 1)]),
        swap(moments, "stack", pairs),
        swap(moments, ("stack", "azimuth"), crossed),
    ]
    flat = deramp(parts, series, member, row_local, date_total)
    return flat.reshape(date_total, row_local, col_local)


def solution(mesh):
    return jax.shard_map(
        local,
        mesh=mesh,
        in_specs=(
            P("stack", "azimuth", "range"),
            P(),
            P(),
            P("azimuth", ("range", "stack")),
            P("azimuth", ("range", "stack")),
        ),
        out_specs=P(None, "azimuth", ("range", "stack")),
        check_vma=False,
    )
```

```python
import functools

import jax
import jax.numpy as jnp
from jax import lax
from jax.experimental import pallas as pl
from jax.experimental.pallas import tpu as pltpu
from jax.sharding import PartitionSpec as P

REWEIGHTS = 2
LANES = 128
VMEM_LIMIT = 24 * 1024 * 1024
ROWS_A = 128
ROWS_B = 320
APPROX = False
ARRIVAL = (0, 1, 4, 5, 2, 6, 7, 3)
EARLY = 6
OUT_PARTS = 5


def halves(value):
    top = value.astype(jnp.bfloat16)
    return top, (value - top.astype(jnp.float32)).astype(jnp.bfloat16)


def product(left, right, dims=(((1,), (0,)), ((), ()))):
    return lax.dot_general(left, right, dims, preferred_element_type=jnp.float32)


def prepare_kernel(
    pairs_ref, prec_ref, coherence_ref, tiles_ref, incidence_ref, gain_top, gain_low, member_ref,
    weighted_ref, basis_ref, pairs, *, order, col_total, row_total,
):
    chunk = pairs_ref.shape[2]
    date_total = prec_ref.shape[0]
    date_pad, ifg_total = gain_top.shape
    place = lax.axis_index("stack") if len(order) > 1 else 0
    for position, mask in enumerate(order):
        pairs[:, position * chunk : (position + 1) * chunk] = pairs_ref[place ^ mask]
    date_ids = lax.broadcasted_iota(jnp.int32, (date_pad, ifg_total), 0)
    incidence_t = (
        jnp.where(date_ids == pairs[1:2, :], 1.0, 0.0)
        - jnp.where(date_ids == pairs[0:1, :], 1.0, 0.0)
    ).astype(jnp.bfloat16)
    incidence_ref[...] = incidence_t.T
    prec = prec_ref[...]
    prec = prec - jnp.sum(prec, axis=1, keepdims=True) / date_total
    top, low = halves(prec)
    used = incidence_t[:date_total]
    gain_a, gain_b = halves(product(top, used) + product(low, used))
    zeros = jnp.zeros((date_pad - date_total, ifg_total), jnp.bfloat16)
    gain_top[...] = jnp.concatenate([gain_a, zeros], axis=0)
    gain_low[...] = jnp.concatenate([gain_b, zeros], axis=0)

    row_local, col_local = coherence_ref.shape
    pixel_count = row_local * col_local
    stack_size = lax.axis_size("stack")
    block = lax.axis_index("range") * stack_size + lax.axis_index("stack")
    node = block // 2
    even = node % 2 == 0

    def flat(ref):
        return jnp.concatenate([ref[row : row + 1, :] for row in range(row_local)], axis=1)

    coherence = flat(coherence_ref).astype(jnp.float32)
    tiles = flat(tiles_ref)
    pixel = lax.broadcasted_iota(jnp.int32, (1, pixel_count), 1)
    row = jnp.zeros_like(pixel)
    for step in range(1, row_local):
        row = row + (pixel >= step * col_local).astype(jnp.int32)
    column = block * col_local + (pixel - row * col_local)
    row = row + lax.axis_index("azimuth") * row_local
    coord_u = (row.astype(jnp.float32) + 0.5) / row_total - 0.5
    coord_v = (column.astype(jnp.float32) + 0.5) / col_total - 0.5
    basis = jnp.concatenate([jnp.ones_like(coord_u), coord_u, coord_v], axis=0)
    spare = jnp.zeros((2, pixel_count), jnp.float32)
    lines = []
    for base in (jnp.where(even, 2 * node + 1, 2 * node - 1), jnp.where(even, 2 * node - 1, 2 * node + 1)):
        for step in range(2):
            lines.append(basis * (tiles == base + step).astype(jnp.float32))
        lines.append(spare)
    member = jnp.concatenate(lines, axis=0)
    member_ref[...] = member
    weighted_ref[...] = member * coherence
    basis_ref[...] = jnp.concatenate([basis, coherence, jnp.zeros((4, pixel_count), jnp.float32)], axis=0)


def prepare(pairs, preconditioner, coherence, tiles, date_pad, order, col_total, row_total):
    ifg_total = pairs.shape[0] * pairs.shape[2]
    pixel_count = coherence.size
    shapes = [((ifg_total, date_pad), jnp.bfloat16)] + [((date_pad, ifg_total), jnp.bfloat16)] * 2
    shapes += [((rows, pixel_count), jnp.float32) for rows in (16, 16, 8)]
    whole = pl.BlockSpec(memory_space=pltpu.VMEM)
    return pl.pallas_call(
        functools.partial(prepare_kernel, order=order, col_total=col_total, row_total=row_total),
        out_shape=[jax.ShapeDtypeStruct(shape, dtype) for shape, dtype in shapes],
        in_specs=[whole] * 4,
        out_specs=[whole] * 6,
        scratch_shapes=[pltpu.VMEM((2, ifg_total), jnp.int32)],
        compiler_params=pltpu.CompilerParams(vmem_limit_bytes=VMEM_LIMIT),
        name="prepare",
    )(pairs, preconditioner, coherence, tiles)


def unpack(chunk_refs, wide, data, row_local):
    start = 0
    col_local = chunk_refs[0].shape[1]
    for ref in chunk_refs:
        count = ref.shape[0] // row_local
        wide[pl.ds(0, ref.shape[0]), :] = ref[...].astype(jnp.float32)
        for row in range(row_local):
            data[pl.ds(start, count), row * col_local : (row + 1) * col_local] = wide[
                pl.ds(row, count, stride=row_local), :
            ].astype(jnp.bfloat16)
        start += count


def gained(gain_top, gain_low, rows, columns, value):
    part = product(gain_top[rows, columns], value)
    if gain_low is not None:
        part = part + product(gain_low[rows, columns], value)
    return part


def early_kernel(*refs, row_local):
    *chunk_refs, gain_top, gain_low, data_ref, series_ref, wide = refs
    unpack(chunk_refs, wide, data_ref, row_local)
    columns = pl.ds(0, data_ref.shape[0] // 256 * 256)
    for start in range(0, series_ref.shape[0], ROWS_B):
        rows = pl.ds(start, ROWS_B)
        series_ref[rows, :] = gained(gain_top, gain_low, rows, columns, data_ref[columns, :])


def early_fit(chunks, gains, row_local):
    count = sum(chunk.shape[0] for chunk in chunks) // row_local
    pixel_count = chunks[0].shape[1] * row_local
    return pl.pallas_call(
        functools.partial(early_kernel, row_local=row_local),
        out_shape=[
            jax.ShapeDtypeStruct((count, pixel_count), jnp.bfloat16),
            jax.ShapeDtypeStruct((gains[0].shape[0], pixel_count), jnp.float32),
        ],
        scratch_shapes=[pltpu.VMEM(chunks[0].shape, jnp.float32)],
        compiler_params=pltpu.CompilerParams(vmem_limit_bytes=VMEM_LIMIT),
        name="early_fit",
    )(*chunks, *gains)


def invert_kernel(*refs, row_local, date_total, late):
    (
        *chunk_refs, incidence, gain_top, gain_low, weighted_ref, basis_ref, series_ref,
        moments_ref, wide, data, residual, moved,
    ) = refs
    ifg_total, pixel_count = data.shape
    date_pad = gain_top.shape[0]
    late_refs, early_refs = chunk_refs[:late], chunk_refs[late:]
    done = 0
    if early_refs:
        early_data, early_series = early_refs
        held = early_data.shape[0]
        done = held // 256 * 256
        data[pl.ds(0, held), :] = early_data[...]
        unpack(late_refs, wide, data.at[pl.ds(held, ifg_total - held)], row_local)
    else:
        unpack(late_refs, wide, data, row_local)
    coherence = basis_ref[3:4, :]
    date_tiles = [pl.ds(start, ROWS_B) for start in range(0, date_pad, ROWS_B)]
    ifg_tiles = [pl.ds(start, ROWS_A) for start in range(0, ifg_total, ROWS_A)]
    everything = slice(None)

    def folded(square):
        return jnp.sum(square.reshape(-1, 8, pixel_count), axis=0)

    def reweighted(total):
        scale = jnp.sum(total, axis=0, keepdims=True) / ifg_total + 1e-06
        strength = coherence * (scale * scale)
        for rows in ifg_tiles:
            left = residual[rows, :]
            inverse = pl.reciprocal(left * left + scale, approx=APPROX)
            moved[rows, :] = ((inverse * left) * (inverse * strength)).astype(jnp.bfloat16)

    left_columns = pl.ds(done, ifg_total - done)
    tops, lows = [], []
    for rows in date_tiles:
        part = gained(gain_top, gain_low, rows, left_columns, data[left_columns, :])
        if early_refs:
            part = part + early_series[rows, :]
        series_ref[rows, :] = part
        top, low = halves(part)
        tops.append(top)
        lows.append(low)
    top, low = jnp.concatenate(tops, axis=0), jnp.concatenate(lows, axis=0)
    total = jnp.zeros((8, pixel_count), jnp.float32)
    for rows in ifg_tiles:
        fit = product(incidence[rows, :], top) + product(incidence[rows, :], low)
        left = data[rows, :].astype(jnp.float32) - fit
        residual[rows, :] = left
        total = total + folded(left * left)
    reweighted(total)
    for sweep in range(1, REWEIGHTS):
        steps = []
        for rows in date_tiles:
            part = gained(gain_top, gain_low, rows, everything, moved[...])
            steps.append(part.astype(jnp.bfloat16))
            series_ref[rows, :] = series_ref[rows, :] + part
        step = jnp.concatenate(steps, axis=0)
        total = jnp.zeros((8, pixel_count), jnp.float32)
        for rows in ifg_tiles:
            left = residual[rows, :] - product(incidence[rows, :], step)
            residual[rows, :] = left
            total = total + folded(left * left)
        reweighted(total)
    for rows in date_tiles:
        part = gained(gain_top, None, rows, everything, moved[...])
        series_ref[rows, :] = series_ref[rows, :] + part
    series_ref[pl.ds(date_total, 8), :] = basis_ref[...]
    series_top, series_low = halves(series_ref[...])
    weighted_top, weighted_low = halves(weighted_ref[...])
    across = (((1,), (1,)), ((), ()))
    moments_ref[...] = product(weighted_top, series_top, across) + (
        product(weighted_low, series_top, across) + product(weighted_top, series_low, across)
    )


def invert(late_chunks, early, incidence, gains, weighted, basis, row_local, date_total):
    ifg_total = incidence.shape[0]
    date_pad = gains[0].shape[0]
    pixel_count = weighted.shape[1]
    return pl.pallas_call(
        functools.partial(
            invert_kernel, row_local=row_local, date_total=date_total, late=len(late_chunks)
        ),
        out_shape=[
            jax.ShapeDtypeStruct((date_pad, pixel_count), jnp.float32),
            jax.ShapeDtypeStruct((weighted.shape[0], date_pad), jnp.float32),
        ],
        scratch_shapes=[
            pltpu.VMEM(late_chunks[0].shape, jnp.float32),
            pltpu.VMEM((ifg_total, pixel_count), jnp.bfloat16),
            pltpu.VMEM((ifg_total, pixel_count), jnp.float32),
            pltpu.VMEM((ifg_total, pixel_count), jnp.bfloat16),
        ],
        compiler_params=pltpu.CompilerParams(vmem_limit_bytes=VMEM_LIMIT),
        name="invert",
    )(*late_chunks, *early, incidence, *gains, weighted, basis)


def exchange(phases, stack_pos, stack_size):
    ifg_local, row_local, col_range = phases.shape
    col_local = col_range // stack_size
    if stack_size != 8:
        blocks = phases.reshape(ifg_local, row_local, stack_size, col_local).transpose(2, 0, 1, 3)
        stacked = lax.all_to_all(blocks, "stack", split_axis=0, concat_axis=0, tiled=True)
        return [stacked.reshape(-1, col_local)], []
    def block_for(array, mask):
        return lax.dynamic_slice_in_dim(array, (stack_pos ^ mask) * col_local, col_local, axis=2)

    first = block_for(phases, 4)
    phases, first = lax.optimization_barrier((phases, first))
    blocks = [first if mask == 4 else block_for(phases, mask) for mask in range(stack_size)]
    found = {0: blocks[0]}

    def send(mask, after=None):
        block = blocks[mask]
        if after is not None:
            block, found[after] = lax.optimization_barrier((block, found[after]))
        found[mask] = lax.ppermute(block, "stack", [(i, i ^ mask) for i in range(stack_size)])

    for mask, after in ((4, None), (5, None), (1, None), (6, None), (2, None), (7, 1), (3, 2)):
        send(mask, after)
    return [found[mask].reshape(-1, col_local) for mask in ARRIVAL], ARRIVAL


def plane_solve(gram_matrix, right_side):

    def entry(row_pos, col_pos):
        return gram_matrix[row_pos % 3][col_pos % 3]

    cofactors = [
        [
            entry(row_pos + 1, col_pos + 1) * entry(row_pos + 2, col_pos + 2)
            - entry(row_pos + 1, col_pos + 2) * entry(row_pos + 2, col_pos + 1)
            for col_pos in range(3)
        ]
        for row_pos in range(3)
    ]
    determinant = (
        entry(0, 0) * cofactors[0][0]
        + entry(0, 1) * cofactors[0][1]
        + entry(0, 2) * cofactors[0][2]
    )
    return [
        (
            (cofactors[0][col_pos] / determinant) * right_side[0]
            + (cofactors[1][col_pos] / determinant) * right_side[1]
            + (cofactors[2][col_pos] / determinant) * right_side[2]
        )
        for col_pos in range(3)
    ]


def deramp_kernel(first_ref, *refs, row_local, date_total):
    *others, series_ref, member_ref, out_ref, staged, sems = refs
    totals = first_ref[...]
    for other in others:
        totals = totals + other[...]
    planes = []
    for base in (0, 3, 8, 11):
        gram = [
            [
                totals[base + k : base + k + 1, date_total + m : date_total + m + 1]
                + (1.0 if k == m else 0.0)
                for m in range(3)
            ]
            for k in range(3)
        ]
        planes += plane_solve(gram, [totals[base + k : base + k + 1, :] for k in range(3)])
        if base in (3, 11):
            planes += [jnp.zeros_like(planes[0])] * 2
    planes_top, planes_low = halves(jnp.concatenate(planes, axis=0))
    member_top, member_low = halves(member_ref[...])
    ramp = product(
        jnp.concatenate([planes_top, planes_low, planes_top], axis=0),
        jnp.concatenate([member_top, member_top, member_low], axis=0),
        (((0,), (0,)), ((), ())),
    )
    col_local = series_ref.shape[1] // row_local
    copies = []
    step = date_total // OUT_PARTS
    for part in range(OUT_PARTS):
        start = part * step
        flat = series_ref[pl.ds(start, step), :] - ramp[start : start + step]
        for row in range(row_local):
            staged[pl.ds(start * row_local + row, step, stride=row_local), :] = flat[
                :, row * col_local : (row + 1) * col_local
            ]
        rows = pl.ds(start * row_local, step * row_local)
        copy = pltpu.make_async_copy(staged.at[rows], out_ref.at[rows], sems.at[part])
        copy.start()
        copies.append(copy)
    for copy in copies:
        copy.wait()


def deramp(parts, series, member, row_local, date_total):
    col_local = series.shape[1] // row_local
    shape = (date_total * row_local, col_local)
    whole = pl.BlockSpec(memory_space=pltpu.VMEM)
    return pl.pallas_call(
        functools.partial(deramp_kernel, row_local=row_local, date_total=date_total),
        out_shape=jax.ShapeDtypeStruct(shape, jnp.float32),
        in_specs=[whole] * (len(parts) + 2),
        out_specs=pl.BlockSpec(memory_space=pl.ANY),
        scratch_shapes=[pltpu.VMEM(shape, jnp.float32), pltpu.SemaphoreType.DMA((OUT_PARTS,))],
        compiler_params=pltpu.CompilerParams(vmem_limit_bytes=VMEM_LIMIT),
        name="deramp",
    )(*parts, series, member)


def swap(value, axes, pairs):
    both = [(i, j) for i, j in pairs] + [(j, i) for i, j in pairs]
    return lax.ppermute(value, axes, both)


def local(phases, ifg_pairs, preconditioner, coherence, geo_tiles):
    stack_size = lax.axis_size("stack")
    range_size = lax.axis_size("range")
    azimuth_size = lax.axis_size("azimuth")
    ifg_local, row_local, col_range = phases.shape
    date_total = preconditioner.shape[0]
    date_pad = -(-(date_total + 8) // LANES) * LANES
    stack_pos = lax.axis_index("stack")

    chunks, order = exchange(phases, stack_pos, stack_size)
    pairs = ifg_pairs.T.reshape(2, stack_size, ifg_local).transpose(1, 0, 2)
    if not order:
        pairs, order = ifg_pairs.T[None], (0,)
    incidence, *gains, member, weighted, basis = prepare(
        pairs, preconditioner, coherence, geo_tiles, date_pad, order,
        col_range * range_size, row_local * azimuth_size,
    )
    early = []
    if len(chunks) > EARLY:
        early = early_fit(chunks[:EARLY], gains, row_local)
        chunks = chunks[EARLY:]

    series, moments = invert(
        chunks, early, incidence, gains, weighted, basis, row_local, date_total
    )

    def place(block):
        return (block % stack_size) * range_size + block // stack_size

    block_count = stack_size * range_size
    inner = [
        (place(block), place(block + 2)) for block in range(block_count - 2) if block // 2 % 2 == 0
    ]
    outer = [
        (place(block), place(block + 2)) for block in range(block_count - 2) if block // 2 % 2 == 1
    ]
    axes = ("stack", "range")
    second = swap(moments[8:], axes, outer)
    first = swap(moments[:8], axes, inner)
    moments = moments + jnp.concatenate([first, second], axis=0)
    pairs = [(i, i + 1) for i in range(0, stack_size, 2)]
    crossed = [
        (i * azimuth_size + a, (i + 1) * azimuth_size + (azimuth_size - 1 - a))
        for i in range(0, stack_size, 2)
        for a in range(azimuth_size)
    ]
    parts = [
        moments,
        swap(moments, "azimuth", [(0, 1)]),
        swap(moments, "stack", pairs),
        swap(moments, ("stack", "azimuth"), crossed),
    ]
    flat = deramp(parts, series, member, row_local, date_total)
    return flat.reshape(date_total, row_local, -1)


def solution(mesh):
    return jax.shard_map(
        local,
        mesh=mesh,
        in_specs=(
            P("stack", "azimuth", "range"),
            P(),
            P(),
            P("azimuth", ("range", "stack")),
            P("azimuth", ("range", "stack")),
        ),
        out_specs=P(None, "azimuth", ("range", "stack")),
        check_vma=False,
    )
```

```python
import functools

import jax
import jax.numpy as jnp
from jax import lax
from jax.experimental import pallas as pl
from jax.experimental.pallas import tpu as pltpu
from jax.sharding import PartitionSpec as P

REWEIGHTS = 2
LANES = 128
VMEM_LIMIT = 24 * 1024 * 1024
ROWS_A = 128
ROWS_B = 320
APPROX = False
ARRIVAL = (0, 1, 4, 5, 2, 6, 7, 3)
EARLY = 6
OUT_PARTS = 5


def halves(value):
    top = value.astype(jnp.bfloat16)
    return top, (value - top.astype(jnp.float32)).astype(jnp.bfloat16)


def product(left, right, dims=(((1,), (0,)), ((), ()))):
    return lax.dot_general(left, right, dims, preferred_element_type=jnp.float32)


def prepare_kernel(
    pairs_hbm, prec_hbm, coherence_hbm, tiles_hbm, incidence_ref, gain_top, gain_low, member_ref,
    weighted_ref, basis_ref, pairs_ref, prec_ref, coherence_ref, tiles_ref, pairs, sems, *, order,
    col_total, row_total,
):
    copies = [
        pltpu.make_async_copy(source, target, sems.at[index])
        for index, (source, target) in enumerate(
            (
                (pairs_hbm, pairs_ref),
                (prec_hbm, prec_ref),
                (coherence_hbm, coherence_ref),
                (tiles_hbm, tiles_ref),
            )
        )
    ]
    for copy in copies:
        copy.start()
    copies[0].wait()
    chunk = pairs_ref.shape[1] // len(order)
    date_total = prec_ref.shape[0]
    date_pad, ifg_total = gain_top.shape
    for position, mask in enumerate(order):
        moved = pairs_ref[...]
        if len(order) > 1:
            back = (len(order) - (lax.axis_index("stack") ^ mask)) % len(order)
            moved = pltpu.roll(moved, back * chunk, 1)
        pairs[:, position * chunk : (position + 1) * chunk] = moved[:, :chunk]
    date_ids = lax.broadcasted_iota(jnp.int32, (date_pad, ifg_total), 0)
    incidence_t = (
        jnp.where(date_ids == pairs[1:2, :], 1.0, 0.0)
        - jnp.where(date_ids == pairs[0:1, :], 1.0, 0.0)
    ).astype(jnp.bfloat16)
    incidence_ref[...] = incidence_t.T
    for copy in copies[1:]:
        copy.wait()
    prec = prec_ref[...]
    prec = prec - jnp.sum(prec, axis=1, keepdims=True) / date_total
    top, low = halves(prec)
    used = incidence_t[:date_total]
    gain_a, gain_b = halves(product(top, used) + product(low, used))
    zeros = jnp.zeros((date_pad - date_total, ifg_total), jnp.bfloat16)
    gain_top[...] = jnp.concatenate([gain_a, zeros], axis=0)
    gain_low[...] = jnp.concatenate([gain_b, zeros], axis=0)

    row_local, col_local = coherence_ref.shape
    pixel_count = row_local * col_local
    stack_size = lax.axis_size("stack")
    block = lax.axis_index("range") * stack_size + lax.axis_index("stack")
    node = block // 2
    even = node % 2 == 0

    def flat(ref):
        return jnp.concatenate([ref[row : row + 1, :] for row in range(row_local)], axis=1)

    coherence = flat(coherence_ref).astype(jnp.float32)
    tiles = flat(tiles_ref)
    pixel = lax.broadcasted_iota(jnp.int32, (1, pixel_count), 1)
    row = jnp.zeros_like(pixel)
    for step in range(1, row_local):
        row = row + (pixel >= step * col_local).astype(jnp.int32)
    column = block * col_local + (pixel - row * col_local)
    row = row + lax.axis_index("azimuth") * row_local
    coord_u = (row.astype(jnp.float32) + 0.5) / row_total - 0.5
    coord_v = (column.astype(jnp.float32) + 0.5) / col_total - 0.5
    basis = jnp.concatenate([jnp.ones_like(coord_u), coord_u, coord_v], axis=0)
    spare = jnp.zeros((2, pixel_count), jnp.float32)
    lines = []
    for base in (jnp.where(even, 2 * node + 1, 2 * node - 1), jnp.where(even, 2 * node - 1, 2 * node + 1)):
        for step in range(2):
            lines.append(basis * (tiles == base + step).astype(jnp.float32))
        lines.append(spare)
    member = jnp.concatenate(lines, axis=0)
    member_ref[...] = member
    weighted_ref[...] = member * coherence
    basis_ref[...] = jnp.concatenate([basis, coherence, jnp.zeros((4, pixel_count), jnp.float32)], axis=0)


def prepare(pairs, preconditioner, coherence, tiles, date_pad, order, col_total, row_total):
    ifg_total = pairs.shape[1]
    pixel_count = coherence.size
    arguments = (pairs, preconditioner, coherence, tiles)
    shapes = [((ifg_total, date_pad), jnp.bfloat16)] + [((date_pad, ifg_total), jnp.bfloat16)] * 2
    shapes += [((rows, pixel_count), jnp.float32) for rows in (16, 16, 8)]
    whole = pl.BlockSpec(memory_space=pltpu.VMEM)
    return pl.pallas_call(
        functools.partial(prepare_kernel, order=order, col_total=col_total, row_total=row_total),
        out_shape=[jax.ShapeDtypeStruct(shape, dtype) for shape, dtype in shapes],
        in_specs=[pl.BlockSpec(memory_space=pltpu.HBM)] * 4,
        out_specs=[whole] * 6,
        scratch_shapes=[
            *(pltpu.VMEM(value.shape, value.dtype) for value in arguments),
            pltpu.VMEM(pairs.shape, jnp.int32),
            pltpu.SemaphoreType.DMA((4,)),
        ],
        compiler_params=pltpu.CompilerParams(vmem_limit_bytes=VMEM_LIMIT),
        name="prepare",
    )(*(pltpu.with_memory_space_constraint(value, pltpu.HBM) for value in arguments))


def unpack(chunk_refs, wide, data, row_local):
    start = 0
    col_local = chunk_refs[0].shape[1]
    for ref in chunk_refs:
        count = ref.shape[0] // row_local
        wide[pl.ds(0, ref.shape[0]), :] = ref[...].astype(jnp.float32)
        for row in range(row_local):
            data[pl.ds(start, count), row * col_local : (row + 1) * col_local] = wide[
                pl.ds(row, count, stride=row_local), :
            ].astype(jnp.bfloat16)
        start += count


def gained(gain_top, gain_low, rows, columns, value):
    part = product(gain_top[rows, columns], value)
    if gain_low is not None:
        part = part + product(gain_low[rows, columns], value)
    return part


def early_kernel(*refs, row_local):
    *chunk_refs, gain_top, gain_low, data_ref, series_ref, wide = refs
    unpack(chunk_refs, wide, data_ref, row_local)
    columns = pl.ds(0, data_ref.shape[0] // 256 * 256)
    for start in range(0, series_ref.shape[0], ROWS_B):
        rows = pl.ds(start, ROWS_B)
        series_ref[rows, :] = gained(gain_top, gain_low, rows, columns, data_ref[columns, :])


def early_fit(chunks, gains, row_local):
    count = sum(chunk.shape[0] for chunk in chunks) // row_local
    pixel_count = chunks[0].shape[1] * row_local
    return pl.pallas_call(
        functools.partial(early_kernel, row_local=row_local),
        out_shape=[
            jax.ShapeDtypeStruct((count, pixel_count), jnp.bfloat16),
            jax.ShapeDtypeStruct((gains[0].shape[0], pixel_count), jnp.float32),
        ],
        scratch_shapes=[pltpu.VMEM(chunks[0].shape, jnp.float32)],
        compiler_params=pltpu.CompilerParams(vmem_limit_bytes=VMEM_LIMIT),
        name="early_fit",
    )(*chunks, *gains)


def invert_kernel(*refs, row_local, date_total, late):
    (
        *chunk_refs, incidence, gain_top, gain_low, weighted_ref, basis_ref, series_ref,
        moments_ref, wide, data, residual, moved,
    ) = refs
    ifg_total, pixel_count = data.shape
    date_pad = gain_top.shape[0]
    late_refs, early_refs = chunk_refs[:late], chunk_refs[late:]
    done = 0
    if early_refs:
        early_data, early_series = early_refs
        held = early_data.shape[0]
        done = held // 256 * 256
        data[pl.ds(0, held), :] = early_data[...]
        unpack(late_refs, wide, data.at[pl.ds(held, ifg_total - held)], row_local)
    else:
        unpack(late_refs, wide, data, row_local)
    coherence = basis_ref[3:4, :]
    date_tiles = [pl.ds(start, ROWS_B) for start in range(0, date_pad, ROWS_B)]
    ifg_tiles = [pl.ds(start, ROWS_A) for start in range(0, ifg_total, ROWS_A)]
    everything = slice(None)

    def folded(square):
        return jnp.sum(square.reshape(-1, 8, pixel_count), axis=0)

    def reweighted(total):
        scale = jnp.sum(total, axis=0, keepdims=True) / ifg_total + 1e-06
        strength = coherence * (scale * scale)
        for rows in ifg_tiles:
            left = residual[rows, :]
            inverse = pl.reciprocal(left * left + scale, approx=APPROX)
            moved[rows, :] = ((inverse * left) * (inverse * strength)).astype(jnp.bfloat16)

    left_columns = pl.ds(done, ifg_total - done)
    tops, lows = [], []
    for rows in date_tiles:
        part = gained(gain_top, gain_low, rows, left_columns, data[left_columns, :])
        if early_refs:
            part = part + early_series[rows, :]
        series_ref[rows, :] = part
        top, low = halves(part)
        tops.append(top)
        lows.append(low)
    top, low = jnp.concatenate(tops, axis=0), jnp.concatenate(lows, axis=0)
    total = jnp.zeros((8, pixel_count), jnp.float32)
    for rows in ifg_tiles:
        fit = product(incidence[rows, :], top) + product(incidence[rows, :], low)
        left = data[rows, :].astype(jnp.float32) - fit
        residual[rows, :] = left
        total = total + folded(left * left)
    reweighted(total)
    for sweep in range(1, REWEIGHTS):
        steps = []
        for rows in date_tiles:
            part = gained(gain_top, gain_low, rows, everything, moved[...])
            steps.append(part.astype(jnp.bfloat16))
            series_ref[rows, :] = series_ref[rows, :] + part
        step = jnp.concatenate(steps, axis=0)
        total = jnp.zeros((8, pixel_count), jnp.float32)
        for rows in ifg_tiles:
            left = residual[rows, :] - product(incidence[rows, :], step)
            residual[rows, :] = left
            total = total + folded(left * left)
        reweighted(total)
    for rows in date_tiles:
        part = gained(gain_top, None, rows, everything, moved[...])
        series_ref[rows, :] = series_ref[rows, :] + part
    series_ref[pl.ds(date_total, 8), :] = basis_ref[...]
    series_top, series_low = halves(series_ref[...])
    weighted_top, weighted_low = halves(weighted_ref[...])
    across = (((1,), (1,)), ((), ()))
    moments_ref[...] = product(weighted_top, series_top, across) + (
        product(weighted_low, series_top, across) + product(weighted_top, series_low, across)
    )


def invert(late_chunks, early, incidence, gains, weighted, basis, row_local, date_total):
    ifg_total = incidence.shape[0]
    date_pad = gains[0].shape[0]
    pixel_count = weighted.shape[1]
    return pl.pallas_call(
        functools.partial(
            invert_kernel, row_local=row_local, date_total=date_total, late=len(late_chunks)
        ),
        out_shape=[
            jax.ShapeDtypeStruct((date_pad, pixel_count), jnp.float32),
            jax.ShapeDtypeStruct((weighted.shape[0], date_pad), jnp.float32),
        ],
        scratch_shapes=[
            pltpu.VMEM(late_chunks[0].shape, jnp.float32),
            pltpu.VMEM((ifg_total, pixel_count), jnp.bfloat16),
            pltpu.VMEM((ifg_total, pixel_count), jnp.float32),
            pltpu.VMEM((ifg_total, pixel_count), jnp.bfloat16),
        ],
        compiler_params=pltpu.CompilerParams(vmem_limit_bytes=VMEM_LIMIT),
        name="invert",
    )(*late_chunks, *early, incidence, *gains, weighted, basis)


def cut_kernel(source, *refs):
    *targets, sems = refs
    copies = [
        pltpu.make_async_copy(
            source.at[:, lax.axis_index("stack") ^ mask], target, sems.at[mask]
        )
        for mask, target in enumerate(targets)
    ]
    for copy in copies:
        copy.start()
    for copy in copies:
        copy.wait()


def cut(phases, col_local):
    ifg_local, row_local, col_range = phases.shape
    count = col_range // col_local
    view = phases.reshape(ifg_local, row_local, count, col_local).transpose(0, 2, 1, 3)
    return pl.pallas_call(
        cut_kernel,
        out_shape=[jax.ShapeDtypeStruct((ifg_local, row_local, col_local), phases.dtype)] * count,
        in_specs=[pl.BlockSpec(memory_space=pltpu.HBM)],
        out_specs=[pl.BlockSpec(memory_space=pltpu.VMEM)] * count,
        scratch_shapes=[pltpu.SemaphoreType.DMA((count,))],
        compiler_params=pltpu.CompilerParams(vmem_limit_bytes=8 * 1024 * 1024),
        name="cut",
    )(pltpu.with_memory_space_constraint(view, pltpu.HBM))


def exchange(phases, stack_size):
    ifg_local, row_local, col_range = phases.shape
    col_local = col_range // stack_size
    if stack_size != 8:
        blocks = phases.reshape(ifg_local, row_local, stack_size, col_local).transpose(2, 0, 1, 3)
        stacked = lax.all_to_all(blocks, "stack", split_axis=0, concat_axis=0, tiled=True)
        return [stacked.reshape(-1, col_local)], (0,)
    blocks = cut(phases, col_local)
    found = {0: blocks[0]}

    def send(mask, after=None):
        block = blocks[mask]
        if after is not None:
            block, found[after] = lax.optimization_barrier((block, found[after]))
        found[mask] = lax.ppermute(block, "stack", [(i, i ^ mask) for i in range(stack_size)])

    for mask, after in ((4, None), (5, None), (1, None), (6, None), (2, None), (7, 1), (3, 2)):
        send(mask, after)
    return [found[mask].reshape(-1, col_local) for mask in ARRIVAL], ARRIVAL


def plane_solve(gram_matrix, right_side):

    def entry(row_pos, col_pos):
        return gram_matrix[row_pos % 3][col_pos % 3]

    cofactors = [
        [
            entry(row_pos + 1, col_pos + 1) * entry(row_pos + 2, col_pos + 2)
            - entry(row_pos + 1, col_pos + 2) * entry(row_pos + 2, col_pos + 1)
            for col_pos in range(3)
        ]
        for row_pos in range(3)
    ]
    determinant = (
        entry(0, 0) * cofactors[0][0]
        + entry(0, 1) * cofactors[0][1]
        + entry(0, 2) * cofactors[0][2]
    )
    return [
        (
            (cofactors[0][col_pos] / determinant) * right_side[0]
            + (cofactors[1][col_pos] / determinant) * right_side[1]
            + (cofactors[2][col_pos] / determinant) * right_side[2]
        )
        for col_pos in range(3)
    ]


def deramp_kernel(first_ref, *refs, row_local, date_total):
    *others, series_ref, member_ref, out_ref, staged, sems = refs
    totals = first_ref[...]
    for other in others:
        totals = totals + other[...]
    planes = []
    for base in (0, 3, 8, 11):
        gram = [
            [
                totals[base + k : base + k + 1, date_total + m : date_total + m + 1]
                + (1.0 if k == m else 0.0)
                for m in range(3)
            ]
            for k in range(3)
        ]
        planes += plane_solve(gram, [totals[base + k : base + k + 1, :] for k in range(3)])
        if base in (3, 11):
            planes += [jnp.zeros_like(planes[0])] * 2
    planes_top, planes_low = halves(jnp.concatenate(planes, axis=0))
    member_top, member_low = halves(member_ref[...])
    ramp = product(
        jnp.concatenate([planes_top, planes_low, planes_top], axis=0),
        jnp.concatenate([member_top, member_top, member_low], axis=0),
        (((0,), (0,)), ((), ())),
    )
    col_local = series_ref.shape[1] // row_local
    copies = []
    step = date_total // OUT_PARTS
    for part in range(OUT_PARTS):
        start = part * step
        flat = series_ref[pl.ds(start, step), :] - ramp[start : start + step]
        for row in range(row_local):
            staged[pl.ds(start * row_local + row, step, stride=row_local), :] = flat[
                :, row * col_local : (row + 1) * col_local
            ]
        rows = pl.ds(start * row_local, step * row_local)
        copy = pltpu.make_async_copy(staged.at[rows], out_ref.at[rows], sems.at[part])
        copy.start()
        copies.append(copy)
    for copy in copies:
        copy.wait()


def deramp(parts, series, member, row_local, date_total):
    col_local = series.shape[1] // row_local
    shape = (date_total * row_local, col_local)
    whole = pl.BlockSpec(memory_space=pltpu.VMEM)
    return pl.pallas_call(
        functools.partial(deramp_kernel, row_local=row_local, date_total=date_total),
        out_shape=jax.ShapeDtypeStruct(shape, jnp.float32),
        in_specs=[whole] * (len(parts) + 2),
        out_specs=pl.BlockSpec(memory_space=pl.ANY),
        scratch_shapes=[pltpu.VMEM(shape, jnp.float32), pltpu.SemaphoreType.DMA((OUT_PARTS,))],
        compiler_params=pltpu.CompilerParams(vmem_limit_bytes=VMEM_LIMIT),
        name="deramp",
    )(*parts, series, member)


def swap(value, axes, pairs):
    both = [(i, j) for i, j in pairs] + [(j, i) for i, j in pairs]
    return lax.ppermute(value, axes, both)


def local(phases, ifg_pairs, preconditioner, coherence, geo_tiles):
    stack_size = lax.axis_size("stack")
    range_size = lax.axis_size("range")
    azimuth_size = lax.axis_size("azimuth")
    ifg_local, row_local, col_range = phases.shape
    date_total = preconditioner.shape[0]
    date_pad = -(-(date_total + 8) // LANES) * LANES

    chunks, order = exchange(phases, stack_size)
    incidence, *gains, member, weighted, basis = prepare(
        ifg_pairs.T, preconditioner, coherence, geo_tiles, date_pad, order,
        col_range * range_size, row_local * azimuth_size,
    )
    early = []
    if len(chunks) > EARLY:
        early = early_fit(chunks[:EARLY], gains, row_local)
        chunks = chunks[EARLY:]

    series, moments = invert(
        chunks, early, incidence, gains, weighted, basis, row_local, date_total
    )

    def place(block):
        return (block % stack_size) * range_size + block // stack_size

    block_count = stack_size * range_size
    inner = [
        (place(block), place(block + 2)) for block in range(block_count - 2) if block // 2 % 2 == 0
    ]
    outer = [
        (place(block), place(block + 2)) for block in range(block_count - 2) if block // 2 % 2 == 1
    ]
    axes = ("stack", "range")
    second = swap(moments[8:], axes, outer)
    first = swap(moments[:8], axes, inner)
    moments = moments + jnp.concatenate([first, second], axis=0)
    pairs = [(i, i + 1) for i in range(0, stack_size, 2)]
    crossed = [
        (i * azimuth_size + a, (i + 1) * azimuth_size + (azimuth_size - 1 - a))
        for i in range(0, stack_size, 2)
        for a in range(azimuth_size)
    ]
    parts = [
        moments,
        swap(moments, "azimuth", [(0, 1)]),
        swap(moments, "stack", pairs),
        swap(moments, ("stack", "azimuth"), crossed),
    ]
    flat = deramp(parts, series, member, row_local, date_total)
    return flat.reshape(date_total, row_local, -1)


def solution(mesh):
    return jax.shard_map(
        local,
        mesh=mesh,
        in_specs=(
            P("stack", "azimuth", "range"),
            P(),
            P(),
            P("azimuth", ("range", "stack")),
            P("azimuth", ("range", "stack")),
        ),
        out_specs=P(None, "azimuth", ("range", "stack")),
        check_vma=False,
    )
```

```python
import functools

import jax
import jax.numpy as jnp
from jax import lax
from jax.experimental import pallas as pl
from jax.experimental.pallas import tpu as pltpu
from jax.sharding import PartitionSpec as P

REWEIGHTS = 2
LANES = 128
VMEM_LIMIT = 24 * 1024 * 1024
ROWS_A = 192
ROWS_B = 320
APPROX = False
ARRIVAL = (0, 1, 2, 4, 5, 6, 7, 3)
EARLY = (4, 6)
OUT_PARTS = 5


def halves(value):
    top = value.astype(jnp.bfloat16)
    return top, (value - top.astype(jnp.float32)).astype(jnp.bfloat16)


def product(left, right, dims=(((1,), (0,)), ((), ()))):
    return lax.dot_general(left, right, dims, preferred_element_type=jnp.float32)


def prepare_kernel(
    pairs_hbm, prec_hbm, coherence_hbm, tiles_hbm, incidence_ref, gain_top, gain_low, member_ref,
    weighted_ref, basis_ref, pairs_ref, prec_ref, coherence_ref, tiles_ref, pairs, sems, *, order,
    col_total, row_total,
):
    copies = [
        pltpu.make_async_copy(source, target, sems.at[index])
        for index, (source, target) in enumerate(
            (
                (pairs_hbm, pairs_ref),
                (prec_hbm, prec_ref),
                (coherence_hbm, coherence_ref),
                (tiles_hbm, tiles_ref),
            )
        )
    ]
    for copy in copies:
        copy.start()
    copies[0].wait()
    chunk = pairs_ref.shape[1] // len(order)
    date_total = prec_ref.shape[0]
    date_pad, ifg_total = gain_top.shape
    for position, mask in enumerate(order):
        moved = pairs_ref[...]
        if len(order) > 1:
            back = (len(order) - (lax.axis_index("stack") ^ mask)) % len(order)
            moved = pltpu.roll(moved, back * chunk, 1)
        pairs[:, position * chunk : (position + 1) * chunk] = moved[:, :chunk]
    date_ids = lax.broadcasted_iota(jnp.int32, (date_pad, ifg_total), 0)
    incidence_t = (
        jnp.where(date_ids == pairs[1:2, :], 1.0, 0.0)
        - jnp.where(date_ids == pairs[0:1, :], 1.0, 0.0)
    ).astype(jnp.bfloat16)
    incidence_ref[...] = incidence_t.T
    for copy in copies[1:]:
        copy.wait()
    prec = prec_ref[...]
    prec = prec - jnp.sum(prec, axis=1, keepdims=True) / date_total
    top, low = halves(prec)
    used = incidence_t[:date_total]
    gain_a, gain_b = halves(product(top, used) + product(low, used))
    zeros = jnp.zeros((date_pad - date_total, ifg_total), jnp.bfloat16)
    gain_top[...] = jnp.concatenate([gain_a, zeros], axis=0)
    gain_low[...] = jnp.concatenate([gain_b, zeros], axis=0)

    row_local, col_local = coherence_ref.shape
    pixel_count = row_local * col_local
    stack_size = lax.axis_size("stack")
    block = lax.axis_index("range") * stack_size + lax.axis_index("stack")
    node = block // 2
    even = node % 2 == 0

    def flat(ref):
        return jnp.concatenate([ref[row : row + 1, :] for row in range(row_local)], axis=1)

    coherence = flat(coherence_ref).astype(jnp.float32)
    tiles = flat(tiles_ref)
    pixel = lax.broadcasted_iota(jnp.int32, (1, pixel_count), 1)
    row = jnp.zeros_like(pixel)
    for step in range(1, row_local):
        row = row + (pixel >= step * col_local).astype(jnp.int32)
    column = block * col_local + (pixel - row * col_local)
    row = row + lax.axis_index("azimuth") * row_local
    coord_u = (row.astype(jnp.float32) + 0.5) / row_total - 0.5
    coord_v = (column.astype(jnp.float32) + 0.5) / col_total - 0.5
    basis = jnp.concatenate([jnp.ones_like(coord_u), coord_u, coord_v], axis=0)
    spare = jnp.zeros((2, pixel_count), jnp.float32)
    lines = []
    for base in (jnp.where(even, 2 * node - 1, 2 * node + 1), jnp.where(even, 2 * node + 1, 2 * node - 1)):
        for step in range(2):
            lines.append(basis * (tiles == base + step).astype(jnp.float32))
        lines.append(spare)
    member = jnp.concatenate(lines, axis=0)
    member_ref[...] = member
    weighted_ref[...] = member * coherence
    basis_ref[...] = jnp.concatenate([basis, coherence, jnp.zeros((4, pixel_count), jnp.float32)], axis=0)


def prepare(pairs, preconditioner, coherence, tiles, date_pad, order, col_total, row_total):
    ifg_total = pairs.shape[1]
    pixel_count = coherence.size
    arguments = (pairs, preconditioner, coherence, tiles)
    shapes = [((ifg_total, date_pad), jnp.bfloat16)] + [((date_pad, ifg_total), jnp.bfloat16)] * 2
    shapes += [((rows, pixel_count), jnp.float32) for rows in (16, 16, 8)]
    whole = pl.BlockSpec(memory_space=pltpu.VMEM)
    return pl.pallas_call(
        functools.partial(prepare_kernel, order=order, col_total=col_total, row_total=row_total),
        out_shape=[jax.ShapeDtypeStruct(shape, dtype) for shape, dtype in shapes],
        in_specs=[pl.BlockSpec(memory_space=pltpu.HBM)] * 4,
        out_specs=[whole] * 6,
        scratch_shapes=[
            *(pltpu.VMEM(value.shape, value.dtype) for value in arguments),
            pltpu.VMEM(pairs.shape, jnp.int32),
            pltpu.SemaphoreType.DMA((4,)),
        ],
        compiler_params=pltpu.CompilerParams(vmem_limit_bytes=VMEM_LIMIT),
        name="prepare",
    )(*(pltpu.with_memory_space_constraint(value, pltpu.HBM) for value in arguments))


def unpack(chunk_refs, wide, data, row_local):
    start = 0
    col_local = chunk_refs[0].shape[1]
    for ref in chunk_refs:
        count = ref.shape[0] // row_local
        wide[pl.ds(0, ref.shape[0]), :] = ref[...].astype(jnp.float32)
        for row in range(row_local):
            data[pl.ds(start, count), row * col_local : (row + 1) * col_local] = wide[
                pl.ds(row, count, stride=row_local), :
            ].astype(jnp.bfloat16)
        start += count


def gained(gain_top, gain_low, rows, columns, value):
    part = product(gain_top[rows, columns], value)
    if gain_low is not None:
        part = part + product(gain_low[rows, columns], value)
    return part


def early_kernel(*refs, row_local, start, end, late):
    *chunk_refs, gain_top, gain_low, data_ref, series_ref, wide = refs
    unpack(chunk_refs[:late], wide, data_ref, row_local)
    before = chunk_refs[late:]
    columns = pl.ds(start, end - start)
    value = data_ref[...]
    if before:
        held = before[0].shape[0] - start
        value = jnp.concatenate([before[0][pl.ds(start, held), :], value[: end - start - held]], axis=0)
    else:
        value = value[:end]
    for first in range(0, series_ref.shape[0], ROWS_B):
        rows = pl.ds(first, ROWS_B)
        part = gained(gain_top, gain_low, rows, columns, value)
        series_ref[rows, :] = part + before[1][rows, :] if before else part


def early_fit(chunks, before, gains, row_local, start, end):
    count = sum(chunk.shape[0] for chunk in chunks) // row_local
    pixel_count = chunks[0].shape[1] * row_local
    return pl.pallas_call(
        functools.partial(
            early_kernel, row_local=row_local, start=start, end=end, late=len(chunks)
        ),
        out_shape=[
            jax.ShapeDtypeStruct((count, pixel_count), jnp.bfloat16),
            jax.ShapeDtypeStruct((gains[0].shape[0], pixel_count), jnp.float32),
        ],
        scratch_shapes=[pltpu.VMEM(chunks[0].shape, jnp.float32)],
        compiler_params=pltpu.CompilerParams(vmem_limit_bytes=VMEM_LIMIT),
        name="early_fit",
    )(*chunks, *before, *gains)


def invert_kernel(*refs, row_local, date_total, late):
    (
        *chunk_refs, incidence, gain_top, gain_low, weighted_ref, basis_ref, series_ref,
        moments_ref, wide, data, residual, moved,
    ) = refs
    ifg_total, pixel_count = moved.shape
    date_pad = gain_top.shape[0]
    late_refs, early_refs = chunk_refs[:late], chunk_refs[late:]
    done = 0
    pieces = []
    if early_refs:
        *early_data, early_series = early_refs
        for ref in early_data:
            count = ref.shape[0]
            used = min(count, (done + count) // 128 * 128 - done) if ref is early_data[-1] else count
            pieces.append((ref, done, used))
            done += used
        data[pl.ds(0, count - used), :] = early_data[-1][pl.ds(used, count - used), :]
        unpack(late_refs, wide, data.at[pl.ds(count - used, ifg_total - done - count + used)], row_local)
    else:
        unpack(late_refs, wide, data, row_local)
    pieces.append((data, done, ifg_total - done))

    def observed(rows):
        parts = []
        for ref, first, count in pieces:
            low, high = max(rows.start, first), min(rows.start + rows.size, first + count)
            if low < high:
                parts.append(ref[pl.ds(low - first, high - low), :])
        return parts[0] if len(parts) == 1 else jnp.concatenate(parts, axis=0)

    coherence = basis_ref[3:4, :]
    date_tiles = [pl.ds(start, ROWS_B) for start in range(0, date_pad, ROWS_B)]
    ifg_tiles = [pl.ds(start, ROWS_A) for start in range(0, ifg_total, ROWS_A)]
    everything = slice(None)

    def folded(square):
        return jnp.sum(square.reshape(-1, 8, pixel_count), axis=0)

    def reweighted(total):
        scale = jnp.sum(total, axis=0, keepdims=True) / ifg_total + 1e-06
        strength = coherence * (scale * scale)
        for rows in ifg_tiles:
            left = residual[rows, :]
            inverse = pl.reciprocal(left * left + scale, approx=APPROX)
            moved[rows, :] = ((inverse * left) * (inverse * strength)).astype(jnp.bfloat16)

    left_columns = pl.ds(done, ifg_total - done)
    tops, lows = [], []
    for rows in date_tiles:
        part = gained(gain_top, gain_low, rows, left_columns, data[...])
        if early_refs:
            part = part + early_series[rows, :]
        series_ref[rows, :] = part
        top, low = halves(part)
        tops.append(top)
        lows.append(low)
    top, low = jnp.concatenate(tops, axis=0), jnp.concatenate(lows, axis=0)
    total = jnp.zeros((8, pixel_count), jnp.float32)
    for rows in ifg_tiles:
        fit = product(incidence[rows, :], top) + product(incidence[rows, :], low)
        left = observed(rows).astype(jnp.float32) - fit
        residual[rows, :] = left
        total = total + folded(left * left)
    reweighted(total)
    for sweep in range(1, REWEIGHTS):
        steps = []
        for rows in date_tiles:
            part = gained(gain_top, None, rows, everything, moved[...])
            steps.append(part.astype(jnp.bfloat16))
            series_ref[rows, :] = series_ref[rows, :] + part
        step = jnp.concatenate(steps, axis=0)
        total = jnp.zeros((8, pixel_count), jnp.float32)
        for rows in ifg_tiles:
            left = residual[rows, :] - product(incidence[rows, :], step)
            residual[rows, :] = left
            total = total + folded(left * left)
        held = moved[...]
        for rows in date_tiles:
            series_ref[rows, :] = series_ref[rows, :] + product(gain_low[rows, :], held)
        reweighted(total)
    for rows in date_tiles:
        part = gained(gain_top, None, rows, everything, moved[...])
        series_ref[rows, :] = series_ref[rows, :] + part
    series_ref[pl.ds(date_total, 8), :] = basis_ref[...]
    series_top, series_low = halves(series_ref[...])
    weighted_top, weighted_low = halves(weighted_ref[...])
    across = (((1,), (1,)), ((), ()))
    moments_ref[...] = product(weighted_top, series_top, across) + (
        product(weighted_low, series_top, across) + product(weighted_top, series_low, across)
    )


def invert(late_chunks, early, incidence, gains, weighted, basis, row_local, date_total):
    ifg_total = incidence.shape[0]
    kept = sum(value.shape[0] for value in early[:-1]) // 128 * 128
    date_pad = gains[0].shape[0]
    pixel_count = weighted.shape[1]
    return pl.pallas_call(
        functools.partial(
            invert_kernel, row_local=row_local, date_total=date_total, late=len(late_chunks)
        ),
        out_shape=[
            jax.ShapeDtypeStruct((date_pad, pixel_count), jnp.float32),
            jax.ShapeDtypeStruct((weighted.shape[0], date_pad), jnp.float32),
        ],
        scratch_shapes=[
            pltpu.VMEM(late_chunks[0].shape, jnp.float32),
            pltpu.VMEM((ifg_total - kept, pixel_count), jnp.bfloat16),
            pltpu.VMEM((ifg_total, pixel_count), jnp.float32),
            pltpu.VMEM((ifg_total, pixel_count), jnp.bfloat16),
        ],
        compiler_params=pltpu.CompilerParams(vmem_limit_bytes=VMEM_LIMIT),
        name="invert",
    )(*late_chunks, *early, incidence, *gains, weighted, basis)


def cut_kernel(source, *refs):
    *targets, sems = refs
    copies = [
        pltpu.make_async_copy(
            source.at[:, lax.axis_index("stack") ^ mask], target, sems.at[mask]
        )
        for mask, target in enumerate(targets)
    ]
    for copy in copies:
        copy.start()
    for copy in copies:
        copy.wait()


def cut(phases, col_local):
    ifg_local, row_local, col_range = phases.shape
    count = col_range // col_local
    view = phases.reshape(ifg_local, row_local, count, col_local).transpose(0, 2, 1, 3)
    return pl.pallas_call(
        cut_kernel,
        out_shape=[jax.ShapeDtypeStruct((ifg_local, row_local, col_local), phases.dtype)] * count,
        in_specs=[pl.BlockSpec(memory_space=pltpu.HBM)],
        out_specs=[pl.BlockSpec(memory_space=pltpu.VMEM)] * count,
        scratch_shapes=[pltpu.SemaphoreType.DMA((count,))],
        compiler_params=pltpu.CompilerParams(vmem_limit_bytes=8 * 1024 * 1024),
        name="cut",
    )(pltpu.with_memory_space_constraint(view, pltpu.HBM))


def exchange(phases, stack_size):
    ifg_local, row_local, col_range = phases.shape
    col_local = col_range // stack_size
    if stack_size != 8:
        blocks = phases.reshape(ifg_local, row_local, stack_size, col_local).transpose(2, 0, 1, 3)
        stacked = lax.all_to_all(blocks, "stack", split_axis=0, concat_axis=0, tiled=True)
        return [stacked.reshape(-1, col_local)], (0,)
    blocks = cut(phases, col_local)
    found = {0: blocks[0]}

    def send(mask, after=None):
        block = blocks[mask]
        if after is not None:
            block, found[after] = lax.optimization_barrier((block, found[after]))
        found[mask] = lax.ppermute(block, "stack", [(i, i ^ mask) for i in range(stack_size)])

    for mask, after in ((4, None), (5, None), (1, None), (6, None), (2, None), (7, 1), (3, 2)):
        send(mask, after)
    return [found[mask].reshape(-1, col_local) for mask in ARRIVAL], ARRIVAL


def plane_solve(gram_matrix, right_side):

    def entry(row_pos, col_pos):
        return gram_matrix[row_pos % 3][col_pos % 3]

    cofactors = [
        [
            entry(row_pos + 1, col_pos + 1) * entry(row_pos + 2, col_pos + 2)
            - entry(row_pos + 1, col_pos + 2) * entry(row_pos + 2, col_pos + 1)
            for col_pos in range(3)
        ]
        for row_pos in range(3)
    ]
    determinant = (
        entry(0, 0) * cofactors[0][0]
        + entry(0, 1) * cofactors[0][1]
        + entry(0, 2) * cofactors[0][2]
    )
    return [
        (
            (cofactors[0][col_pos] / determinant) * right_side[0]
            + (cofactors[1][col_pos] / determinant) * right_side[1]
            + (cofactors[2][col_pos] / determinant) * right_side[2]
        )
        for col_pos in range(3)
    ]


def deramp_kernel(first_ref, *refs, row_local, date_total):
    *others, series_ref, member_ref, out_ref, staged, sems = refs
    totals = first_ref[...]
    for other in others:
        totals = totals + other[...]
    planes = []
    for base in (0, 3, 8, 11):
        gram = [
            [
                totals[base + k : base + k + 1, date_total + m : date_total + m + 1]
                + (1.0 if k == m else 0.0)
                for m in range(3)
            ]
            for k in range(3)
        ]
        planes += plane_solve(gram, [totals[base + k : base + k + 1, :] for k in range(3)])
        if base in (3, 11):
            planes += [jnp.zeros_like(planes[0])] * 2
    planes_top, planes_low = halves(jnp.concatenate(planes, axis=0))
    member_top, member_low = halves(member_ref[...])
    ramp = product(
        jnp.concatenate([planes_top, planes_low, planes_top], axis=0),
        jnp.concatenate([member_top, member_top, member_low], axis=0),
        (((0,), (0,)), ((), ())),
    )
    col_local = series_ref.shape[1] // row_local
    copies = []
    step = date_total // OUT_PARTS
    for part in range(OUT_PARTS):
        start = part * step
        flat = series_ref[pl.ds(start, step), :] - ramp[start : start + step]
        for row in range(row_local):
            staged[pl.ds(start * row_local + row, step, stride=row_local), :] = flat[
                :, row * col_local : (row + 1) * col_local
            ]
        rows = pl.ds(start * row_local, step * row_local)
        copy = pltpu.make_async_copy(staged.at[rows], out_ref.at[rows], sems.at[part])
        copy.start()
        copies.append(copy)
    for copy in copies:
        copy.wait()


def deramp(parts, series, member, row_local, date_total):
    col_local = series.shape[1] // row_local
    shape = (date_total * row_local, col_local)
    whole = pl.BlockSpec(memory_space=pltpu.VMEM)
    return pl.pallas_call(
        functools.partial(deramp_kernel, row_local=row_local, date_total=date_total),
        out_shape=jax.ShapeDtypeStruct(shape, jnp.float32),
        in_specs=[whole] * (len(parts) + 2),
        out_specs=pl.BlockSpec(memory_space=pl.ANY),
        scratch_shapes=[pltpu.VMEM(shape, jnp.float32), pltpu.SemaphoreType.DMA((OUT_PARTS,))],
        compiler_params=pltpu.CompilerParams(vmem_limit_bytes=VMEM_LIMIT),
        name="deramp",
    )(*parts, series, member)


def swap(value, axes, pairs):
    both = [(i, j) for i, j in pairs] + [(j, i) for i, j in pairs]
    return lax.ppermute(value, axes, both)


def local(phases, ifg_pairs, preconditioner, coherence, geo_tiles):
    stack_size = lax.axis_size("stack")
    range_size = lax.axis_size("range")
    azimuth_size = lax.axis_size("azimuth")
    ifg_local, row_local, col_range = phases.shape
    date_total = preconditioner.shape[0]
    date_pad = -(-(date_total + 8) // LANES) * LANES

    chunks, order = exchange(phases, stack_size)
    incidence, *gains, member, weighted, basis = prepare(
        ifg_pairs.T, preconditioner, coherence, geo_tiles, date_pad, order,
        col_range * range_size, row_local * azimuth_size,
    )
    early = []
    if len(chunks) > 1:
        first, second = EARLY
        count = ifg_local * first // 256 * 256
        data_a, series_a = early_fit(chunks[:first], [], gains, row_local, 0, count)
        data_b, series_b = early_fit(
            chunks[first:second], [data_a, series_a], gains, row_local, count,
            ifg_local * second // 128 * 128,
        )
        early = [data_a, data_b, series_b]
        chunks = chunks[second:]

    series, moments = invert(
        chunks, early, incidence, gains, weighted, basis, row_local, date_total
    )

    def place(block):
        return (block % stack_size) * range_size + block // stack_size

    block_count = stack_size * range_size
    inner = [
        (place(block), place(block + 2)) for block in range(block_count - 2) if block // 2 % 2 == 0
    ]
    outer = [
        (place(block), place(block + 2)) for block in range(block_count - 2) if block // 2 % 2 == 1
    ]
    axes = ("stack", "range")
    first = swap(moments[:8], axes, outer)
    second = swap(moments[8:], axes, inner)
    moments = moments + jnp.concatenate([first, second], axis=0)
    pairs = [(i, i + 1) for i in range(0, stack_size, 2)]
    crossed = [
        (i * azimuth_size + a, (i + 1) * azimuth_size + (azimuth_size - 1 - a))
        for i in range(0, stack_size, 2)
        for a in range(azimuth_size)
    ]
    parts = [
        moments,
        swap(moments, "azimuth", [(0, 1)]),
        swap(moments, "stack", pairs),
        swap(moments, ("stack", "azimuth"), crossed),
    ]
    flat = deramp(parts, series, member, row_local, date_total)
    return flat.reshape(date_total, row_local, -1)


def solution(mesh):
    return jax.shard_map(
        local,
        mesh=mesh,
        in_specs=(
            P("stack", "azimuth", "range"),
            P(),
            P(),
            P("azimuth", ("range", "stack")),
            P("azimuth", ("range", "stack")),
        ),
        out_specs=P(None, "azimuth", ("range", "stack")),
        check_vma=False,
    )
```

```python
import functools

import jax
import jax.numpy as jnp
from jax import lax
from jax.experimental import pallas as pl
from jax.experimental.pallas import tpu as pltpu
from jax.sharding import PartitionSpec as P

REWEIGHTS = 2
LANES = 128
VMEM_LIMIT = 24 * 1024 * 1024
ROWS_A = 192
ROWS_B = 320
APPROX = False
ARRIVAL = (0, 1, 2, 4, 5, 6, 7, 3)
EARLY = (4, 6)
OUT_PARTS = 5


def halves(value):
    top = value.astype(jnp.bfloat16)
    return top, (value - top.astype(jnp.float32)).astype(jnp.bfloat16)


def product(left, right, dims=(((1,), (0,)), ((), ()))):
    return lax.dot_general(left, right, dims, preferred_element_type=jnp.float32)


def prepare_kernel(
    pairs_hbm, prec_hbm, coherence_hbm, tiles_hbm, incidence_ref, gain_top, gain_low, member_ref,
    weighted_ref, basis_ref, pairs_ref, prec_ref, coherence_ref, tiles_ref, pairs, sems, *, order,
    col_total, row_total,
):
    copies = [
        pltpu.make_async_copy(source, target, sems.at[index])
        for index, (source, target) in enumerate(
            (
                (pairs_hbm, pairs_ref),
                (prec_hbm, prec_ref),
                (coherence_hbm, coherence_ref),
                (tiles_hbm, tiles_ref),
            )
        )
    ]
    for copy in copies:
        copy.start()
    copies[0].wait()
    chunk = pairs_ref.shape[1] // len(order)
    date_total = prec_ref.shape[0]
    date_pad, ifg_total = gain_top.shape
    for position, mask in enumerate(order):
        moved = pairs_ref[...]
        if len(order) > 1:
            back = (len(order) - (lax.axis_index("stack") ^ mask)) % len(order)
            moved = pltpu.roll(moved, back * chunk, 1)
        pairs[:, position * chunk : (position + 1) * chunk] = moved[:, :chunk]
    date_ids = lax.broadcasted_iota(jnp.int32, (date_pad, ifg_total), 0)
    incidence_t = (
        jnp.where(date_ids == pairs[1:2, :], 1.0, 0.0)
        - jnp.where(date_ids == pairs[0:1, :], 1.0, 0.0)
    ).astype(jnp.bfloat16)
    incidence_ref[...] = incidence_t.T
    for copy in copies[1:]:
        copy.wait()
    prec = prec_ref[...]
    prec = prec - jnp.sum(prec, axis=1, keepdims=True) / date_total
    top, low = halves(prec)
    used = incidence_t[:date_total]
    gain_a, gain_b = halves(product(top, used) + product(low, used))
    zeros = jnp.zeros((date_pad - date_total, ifg_total), jnp.bfloat16)
    gain_top[...] = jnp.concatenate([gain_a, zeros], axis=0)
    gain_low[...] = jnp.concatenate([gain_b, zeros], axis=0)

    row_local, col_local = coherence_ref.shape
    pixel_count = row_local * col_local
    stack_size = lax.axis_size("stack")
    block = lax.axis_index("range") * stack_size + lax.axis_index("stack")
    node = block // 2
    even = node % 2 == 0

    def flat(ref):
        return jnp.concatenate([ref[row : row + 1, :] for row in range(row_local)], axis=1)

    coherence = flat(coherence_ref).astype(jnp.float32)
    tiles = flat(tiles_ref)
    pixel = lax.broadcasted_iota(jnp.int32, (1, pixel_count), 1)
    row = jnp.zeros_like(pixel)
    for step in range(1, row_local):
        row = row + (pixel >= step * col_local).astype(jnp.int32)
    column = block * col_local + (pixel - row * col_local)
    row = row + lax.axis_index("azimuth") * row_local
    coord_u = (row.astype(jnp.float32) + 0.5) / row_total - 0.5
    coord_v = (column.astype(jnp.float32) + 0.5) / col_total - 0.5
    basis = jnp.concatenate([jnp.ones_like(coord_u), coord_u, coord_v], axis=0)
    spare = jnp.zeros((2, pixel_count), jnp.float32)
    lines = []
    for base in (jnp.where(even, 2 * node - 1, 2 * node + 1), jnp.where(even, 2 * node + 1, 2 * node - 1)):
        for step in range(2):
            lines.append(basis * (tiles == base + step).astype(jnp.float32))
        lines.append(spare)
    member = jnp.concatenate(lines, axis=0)
    member_ref[...] = member
    weighted_ref[...] = member * coherence
    basis_ref[...] = jnp.concatenate([basis, coherence, jnp.zeros((4, pixel_count), jnp.float32)], axis=0)


def prepare(pairs, preconditioner, coherence, tiles, date_pad, order, col_total, row_total):
    ifg_total = pairs.shape[1]
    pixel_count = coherence.size
    arguments = (pairs, preconditioner, coherence, tiles)
    shapes = [((ifg_total, date_pad), jnp.bfloat16)] + [((date_pad, ifg_total), jnp.bfloat16)] * 2
    shapes += [((rows, pixel_count), jnp.float32) for rows in (16, 16, 8)]
    whole = pl.BlockSpec(memory_space=pltpu.VMEM)
    return pl.pallas_call(
        functools.partial(prepare_kernel, order=order, col_total=col_total, row_total=row_total),
        out_shape=[jax.ShapeDtypeStruct(shape, dtype) for shape, dtype in shapes],
        in_specs=[pl.BlockSpec(memory_space=pltpu.HBM)] * 4,
        out_specs=[whole] * 6,
        scratch_shapes=[
            *(pltpu.VMEM(value.shape, value.dtype) for value in arguments),
            pltpu.VMEM(pairs.shape, jnp.int32),
            pltpu.SemaphoreType.DMA((4,)),
        ],
        compiler_params=pltpu.CompilerParams(vmem_limit_bytes=VMEM_LIMIT),
        name="prepare",
    )(*(pltpu.with_memory_space_constraint(value, pltpu.HBM) for value in arguments))


def unpack(chunk_refs, wide, data, row_local):
    start = 0
    col_local = chunk_refs[0].shape[1]
    for ref in chunk_refs:
        count = ref.shape[0] // row_local
        wide[pl.ds(0, ref.shape[0]), :] = ref[...].astype(jnp.float32)
        for row in range(row_local):
            data[pl.ds(start, count), row * col_local : (row + 1) * col_local] = wide[
                pl.ds(row, count, stride=row_local), :
            ].astype(jnp.bfloat16)
        start += count


def gained(gain_top, gain_low, rows, columns, value):
    part = product(gain_top[rows, columns], value)
    if gain_low is not None:
        part = part + product(gain_low[rows, columns], value)
    return part


def early_kernel(*refs, row_local, start, end, late):
    *chunk_refs, gain_top, gain_low, data_ref, series_ref, wide = refs
    unpack(chunk_refs[:late], wide, data_ref, row_local)
    before = chunk_refs[late:]
    columns = pl.ds(start, end - start)
    value = data_ref[...]
    if before:
        held = before[0].shape[0] - start
        value = jnp.concatenate([before[0][pl.ds(start, held), :], value[: end - start - held]], axis=0)
    else:
        value = value[:end]
    for first in range(0, series_ref.shape[0], ROWS_B):
        rows = pl.ds(first, ROWS_B)
        part = gained(gain_top, gain_low, rows, columns, value)
        series_ref[rows, :] = part + before[1][rows, :] if before else part


def early_fit(chunks, before, gains, row_local, start, end):
    count = sum(chunk.shape[0] for chunk in chunks) // row_local
    pixel_count = chunks[0].shape[1] * row_local
    return pl.pallas_call(
        functools.partial(
            early_kernel, row_local=row_local, start=start, end=end, late=len(chunks)
        ),
        out_shape=[
            jax.ShapeDtypeStruct((count, pixel_count), jnp.bfloat16),
            jax.ShapeDtypeStruct((gains[0].shape[0], pixel_count), jnp.float32),
        ],
        scratch_shapes=[pltpu.VMEM(chunks[0].shape, jnp.float32)],
        compiler_params=pltpu.CompilerParams(vmem_limit_bytes=VMEM_LIMIT),
        name="early_fit",
    )(*chunks, *before, *gains)


def invert_kernel(*refs, row_local, date_total, late):
    (
        *chunk_refs, incidence, gain_top, gain_low, weighted_ref, basis_ref, series_ref,
        moments_ref, wide, data, residual, moved,
    ) = refs
    ifg_total, pixel_count = moved.shape
    date_pad = gain_top.shape[0]
    late_refs, early_refs = chunk_refs[:late], chunk_refs[late:]
    done = 0
    pieces = []
    if early_refs:
        *early_data, early_series = early_refs
        for ref in early_data:
            count = ref.shape[0]
            used = min(count, (done + count) // 128 * 128 - done) if ref is early_data[-1] else count
            pieces.append((ref, done, used))
            done += used
        data[pl.ds(0, count - used), :] = early_data[-1][pl.ds(used, count - used), :]
        unpack(late_refs, wide, data.at[pl.ds(count - used, ifg_total - done - count + used)], row_local)
    else:
        unpack(late_refs, wide, data, row_local)
    pieces.append((data, done, ifg_total - done))

    def observed(rows):
        parts = []
        for ref, first, count in pieces:
            low, high = max(rows.start, first), min(rows.start + rows.size, first + count)
            if low < high:
                parts.append(ref[pl.ds(low - first, high - low), :])
        return parts[0] if len(parts) == 1 else jnp.concatenate(parts, axis=0)

    coherence = basis_ref[3:4, :]
    date_tiles = [pl.ds(start, ROWS_B) for start in range(0, date_pad, ROWS_B)]
    ifg_tiles = [pl.ds(start, ROWS_A) for start in range(0, ifg_total, ROWS_A)]
    everything = slice(None)

    def folded(square):
        return jnp.sum(square.reshape(-1, 8, pixel_count), axis=0)

    def reweighted(total):
        scale = jnp.sum(total, axis=0, keepdims=True) / ifg_total + 1e-06
        strength = coherence * (scale * scale)
        for rows in ifg_tiles:
            left = residual[rows, :]
            inverse = pl.reciprocal(left * left + scale, approx=APPROX)
            moved[rows, :] = ((inverse * left) * (inverse * strength)).astype(jnp.bfloat16)

    left_columns = pl.ds(done, ifg_total - done)
    tops, lows = [], []
    for rows in date_tiles:
        part = gained(gain_top, gain_low, rows, left_columns, data[...])
        if early_refs:
            part = part + early_series[rows, :]
        series_ref[rows, :] = part
        top, low = halves(part)
        tops.append(top)
        lows.append(low)
    top, low = jnp.concatenate(tops, axis=0), jnp.concatenate(lows, axis=0)
    total = jnp.zeros((8, pixel_count), jnp.float32)
    for rows in ifg_tiles:
        fit = product(incidence[rows, :], top) + product(incidence[rows, :], low)
        left = observed(rows).astype(jnp.float32) - fit
        residual[rows, :] = left
        total = total + folded(left * left)
    reweighted(total)
    for sweep in range(1, REWEIGHTS):
        steps = []
        for rows in date_tiles:
            part = gained(gain_top, None, rows, everything, moved[...])
            steps.append(part.astype(jnp.bfloat16))
            series_ref[rows, :] = series_ref[rows, :] + part
        step = jnp.concatenate(steps, axis=0)
        total = jnp.zeros((8, pixel_count), jnp.float32)
        for rows in ifg_tiles:
            left = residual[rows, :] - product(incidence[rows, :], step)
            residual[rows, :] = left
            total = total + folded(left * left)
        held = moved[...]
        for rows in date_tiles:
            series_ref[rows, :] = series_ref[rows, :] + product(gain_low[rows, :], held)
        reweighted(total)
    for rows in date_tiles:
        part = gained(gain_top, None, rows, everything, moved[...])
        series_ref[rows, :] = series_ref[rows, :] + part
    series_ref[pl.ds(date_total, 8), :] = basis_ref[...]
    series_top, series_low = halves(series_ref[...])
    weighted_top, weighted_low = halves(weighted_ref[...])
    across = (((1,), (1,)), ((), ()))
    moments_ref[...] = product(weighted_top, series_top, across) + (
        product(weighted_low, series_top, across) + product(weighted_top, series_low, across)
    )


def invert(late_chunks, early, incidence, gains, weighted, basis, row_local, date_total):
    ifg_total = incidence.shape[0]
    kept = sum(value.shape[0] for value in early[:-1]) // 128 * 128
    date_pad = gains[0].shape[0]
    pixel_count = weighted.shape[1]
    return pl.pallas_call(
        functools.partial(
            invert_kernel, row_local=row_local, date_total=date_total, late=len(late_chunks)
        ),
        out_shape=[
            jax.ShapeDtypeStruct((date_pad, pixel_count), jnp.float32),
            jax.ShapeDtypeStruct((weighted.shape[0], date_pad), jnp.float32),
        ],
        scratch_shapes=[
            pltpu.VMEM(late_chunks[0].shape, jnp.float32),
            pltpu.VMEM((ifg_total - kept, pixel_count), jnp.bfloat16),
            pltpu.VMEM((ifg_total, pixel_count), jnp.float32),
            pltpu.VMEM((ifg_total, pixel_count), jnp.bfloat16),
        ],
        compiler_params=pltpu.CompilerParams(vmem_limit_bytes=VMEM_LIMIT),
        name="invert",
    )(*late_chunks, *early, incidence, *gains, weighted, basis)


def cut_kernel(source, *refs):
    *targets, sems = refs
    copies = [
        pltpu.make_async_copy(
            source.at[:, lax.axis_index("stack") ^ mask], target, sems.at[mask]
        )
        for mask, target in enumerate(targets)
    ]
    for copy in copies:
        copy.start()
    for copy in copies:
        copy.wait()


def cut(phases, col_local):
    ifg_local, row_local, col_range = phases.shape
    count = col_range // col_local
    view = phases.reshape(ifg_local, row_local, count, col_local).transpose(0, 2, 1, 3)
    return pl.pallas_call(
        cut_kernel,
        out_shape=[jax.ShapeDtypeStruct((ifg_local, row_local, col_local), phases.dtype)] * count,
        in_specs=[pl.BlockSpec(memory_space=pltpu.HBM)],
        out_specs=[pl.BlockSpec(memory_space=pltpu.VMEM)] * count,
        scratch_shapes=[pltpu.SemaphoreType.DMA((count,))],
        compiler_params=pltpu.CompilerParams(vmem_limit_bytes=8 * 1024 * 1024),
        name="cut",
    )(pltpu.with_memory_space_constraint(view, pltpu.HBM))


def exchange(phases, stack_size):
    ifg_local, row_local, col_range = phases.shape
    col_local = col_range // stack_size
    if stack_size != 8:
        blocks = phases.reshape(ifg_local, row_local, stack_size, col_local).transpose(2, 0, 1, 3)
        stacked = lax.all_to_all(blocks, "stack", split_axis=0, concat_axis=0, tiled=True)
        return [stacked.reshape(-1, col_local)], (0,)
    blocks = cut(phases, col_local)
    found = {0: blocks[0]}

    def send(mask, after=None):
        block = blocks[mask]
        if after is not None:
            block, found[after] = lax.optimization_barrier((block, found[after]))
        found[mask] = lax.ppermute(block, "stack", [(i, i ^ mask) for i in range(stack_size)])

    for mask, after in ((4, None), (5, None), (1, None), (6, None), (2, None), (7, 1), (3, 2)):
        send(mask, after)
    return [found[mask].reshape(-1, col_local) for mask in ARRIVAL], ARRIVAL


def plane_solve(gram_matrix, right_side):

    def entry(row_pos, col_pos):
        return gram_matrix[row_pos % 3][col_pos % 3]

    cofactors = [
        [
            entry(row_pos + 1, col_pos + 1) * entry(row_pos + 2, col_pos + 2)
            - entry(row_pos + 1, col_pos + 2) * entry(row_pos + 2, col_pos + 1)
            for col_pos in range(3)
        ]
        for row_pos in range(3)
    ]
    determinant = (
        entry(0, 0) * cofactors[0][0]
        + entry(0, 1) * cofactors[0][1]
        + entry(0, 2) * cofactors[0][2]
    )
    return [
        (
            (cofactors[0][col_pos] / determinant) * right_side[0]
            + (cofactors[1][col_pos] / determinant) * right_side[1]
            + (cofactors[2][col_pos] / determinant) * right_side[2]
        )
        for col_pos in range(3)
    ]


def deramp_kernel(first_ref, *refs, row_local, date_total):
    *others, series_ref, member_ref, out_ref, staged, sems = refs
    totals = first_ref[...]
    for other in others:
        totals = totals + other[...]
    planes = []
    for base in (0, 3, 8, 11):
        gram = [
            [
                totals[base + k : base + k + 1, date_total + m : date_total + m + 1]
                + (1.0 if k == m else 0.0)
                for m in range(3)
            ]
            for k in range(3)
        ]
        planes += plane_solve(gram, [totals[base + k : base + k + 1, :] for k in range(3)])
        if base in (3, 11):
            planes += [jnp.zeros_like(planes[0])] * 2
    planes_top, planes_low = halves(jnp.concatenate(planes, axis=0))
    member_top, member_low = halves(member_ref[...])
    ramp = product(
        jnp.concatenate([planes_top, planes_low, planes_top], axis=0),
        jnp.concatenate([member_top, member_top, member_low], axis=0),
        (((0,), (0,)), ((), ())),
    )
    col_local = series_ref.shape[1] // row_local
    copies = []
    step = date_total // OUT_PARTS
    for part in range(OUT_PARTS):
        start = part * step
        flat = series_ref[pl.ds(start, step), :] - ramp[start : start + step]
        for row in range(row_local):
            staged[pl.ds(start * row_local + row, step, stride=row_local), :] = flat[
                :, row * col_local : (row + 1) * col_local
            ]
        rows = pl.ds(start * row_local, step * row_local)
        copy = pltpu.make_async_copy(staged.at[rows], out_ref.at[rows], sems.at[part])
        copy.start()
        copies.append(copy)
    for copy in copies:
        copy.wait()


def deramp(parts, series, member, row_local, date_total):
    col_local = series.shape[1] // row_local
    shape = (date_total * row_local, col_local)
    whole = pl.BlockSpec(memory_space=pltpu.VMEM)
    return pl.pallas_call(
        functools.partial(deramp_kernel, row_local=row_local, date_total=date_total),
        out_shape=jax.ShapeDtypeStruct(shape, jnp.float32),
        in_specs=[whole] * (len(parts) + 2),
        out_specs=pl.BlockSpec(memory_space=pl.ANY),
        scratch_shapes=[pltpu.VMEM(shape, jnp.float32), pltpu.SemaphoreType.DMA((OUT_PARTS,))],
        compiler_params=pltpu.CompilerParams(vmem_limit_bytes=VMEM_LIMIT),
        name="deramp",
    )(*parts, series, member)


def swap(value, axes, pairs):
    both = [(i, j) for i, j in pairs] + [(j, i) for i, j in pairs]
    return lax.ppermute(value, axes, both)


def local(phases, ifg_pairs, preconditioner, coherence, geo_tiles):
    stack_size = lax.axis_size("stack")
    range_size = lax.axis_size("range")
    azimuth_size = lax.axis_size("azimuth")
    ifg_local, row_local, col_range = phases.shape
    date_total = preconditioner.shape[0]
    date_pad = -(-(date_total + 8) // LANES) * LANES

    chunks, order = exchange(phases, stack_size)
    incidence, *gains, member, weighted, basis = prepare(
        ifg_pairs.T, preconditioner, coherence, geo_tiles, date_pad, order,
        col_range * range_size, row_local * azimuth_size,
    )
    early = []
    if len(chunks) > 1:
        first, second = EARLY
        count = ifg_local * first // 256 * 256
        data_a, series_a = early_fit(chunks[:first], [], gains, row_local, 0, count)
        data_b, series_b = early_fit(
            chunks[first:second], [data_a, series_a], gains, row_local, count,
            ifg_local * second // 128 * 128,
        )
        early = [data_a, data_b, series_b]
        chunks = chunks[second:]

    series, moments = invert(
        chunks, early, incidence, gains, weighted, basis, row_local, date_total
    )

    def place(block):
        return (block % stack_size) * range_size + block // stack_size

    block_count = stack_size * range_size
    inner = [
        (place(block), place(block + 2)) for block in range(block_count - 2) if block // 2 % 2 == 0
    ]
    outer = [
        (place(block), place(block + 2)) for block in range(block_count - 2) if block // 2 % 2 == 1
    ]
    axes = ("stack", "range")
    outer += [(place(0), place(1)), (place(block_count - 2), place(block_count - 1))]
    first = swap(moments[:8], axes, outer)
    node = (lax.axis_index("range") * stack_size + lax.axis_index("stack")) // 2
    first = jnp.where((node > 0) & (node < block_count // 2 - 1), first, 0.0)
    second = swap(moments[8:], axes, inner)
    moments = moments + jnp.concatenate([first, second], axis=0)
    pairs = [(i, i + 1) for i in range(0, stack_size, 2)]
    crossed = [
        (i * azimuth_size + a, (i + 1) * azimuth_size + (azimuth_size - 1 - a))
        for i in range(0, stack_size, 2)
        for a in range(azimuth_size)
    ]
    parts = [
        moments,
        swap(moments, "azimuth", [(0, 1)]),
        swap(moments, "stack", pairs),
        swap(moments, ("stack", "azimuth"), crossed),
    ]
    flat = deramp(parts, series, member, row_local, date_total)
    return flat.reshape(date_total, row_local, -1)


def solution(mesh):
    return jax.shard_map(
        local,
        mesh=mesh,
        in_specs=(
            P("stack", "azimuth", "range"),
            P(),
            P(),
            P("azimuth", ("range", "stack")),
            P("azimuth", ("range", "stack")),
        ),
        out_specs=P(None, "azimuth", ("range", "stack")),
        check_vma=False,
    )
```

```python
import functools

import jax
import jax.numpy as jnp
from jax import lax
from jax.experimental import pallas as pl
from jax.experimental.pallas import tpu as pltpu
from jax.sharding import PartitionSpec as P

REWEIGHTS = 2
LANES = 128
VMEM_LIMIT = 24 * 1024 * 1024
ROWS_A = 192
APPROX = False
ARRIVAL = (0, 1, 2, 4, 5, 6, 7, 3)
EARLY = (4, 6)
OUT_PARTS = 5


def halves(value):
    top = value.astype(jnp.bfloat16)
    return top, (value - top.astype(jnp.float32)).astype(jnp.bfloat16)


def product(left, right, dims=(((1,), (0,)), ((), ()))):
    return lax.dot_general(left, right, dims, preferred_element_type=jnp.float32)


def prepare_kernel(
    pairs_hbm, prec_hbm, coherence_hbm, tiles_hbm, incidence_ref, gain_top, gain_low, member_ref,
    weighted_ref, basis_ref, pairs_ref, prec_ref, coherence_ref, tiles_ref, pairs, sems, *, order,
    col_total, row_total,
):
    copies = [
        pltpu.make_async_copy(source, target, sems.at[index])
        for index, (source, target) in enumerate(
            (
                (pairs_hbm, pairs_ref),
                (prec_hbm, prec_ref),
                (coherence_hbm, coherence_ref),
                (tiles_hbm, tiles_ref),
            )
        )
    ]
    for copy in copies:
        copy.start()
    copies[0].wait()
    chunk = pairs_ref.shape[1] // len(order)
    date_total = prec_ref.shape[0]
    ifg_total = gain_top.shape[1]
    date_pad = incidence_ref.shape[1] // 2
    for position, mask in enumerate(order):
        moved = pairs_ref[...]
        if len(order) > 1:
            back = (len(order) - (lax.axis_index("stack") ^ mask)) % len(order)
            moved = pltpu.roll(moved, back * chunk, 1)
        pairs[:, position * chunk : (position + 1) * chunk] = moved[:, :chunk]
    date_ids = lax.broadcasted_iota(jnp.int32, (date_pad, ifg_total), 0)
    incidence_t = (
        jnp.where(date_ids == pairs[1:2, :], 1.0, 0.0)
        - jnp.where(date_ids == pairs[0:1, :], 1.0, 0.0)
    ).astype(jnp.bfloat16)
    incidence = incidence_t.T
    incidence_ref[:, :date_pad] = incidence
    incidence_ref[:, date_pad:] = incidence
    for copy in copies[1:]:
        copy.wait()
    prec = prec_ref[...]
    prec = prec - jnp.sum(prec, axis=1, keepdims=True) / date_total
    top, low = halves(prec)
    used = incidence_t[:date_total]
    gain_a, gain_b = halves(product(top, used) + product(low, used))
    zeros = jnp.zeros((gain_top.shape[0] - date_total, ifg_total), jnp.bfloat16)
    gain_top[...] = jnp.concatenate([gain_a, zeros], axis=0)
    gain_low[...] = jnp.concatenate([gain_b, zeros], axis=0)

    row_local, col_local = coherence_ref.shape
    pixel_count = row_local * col_local
    stack_size = lax.axis_size("stack")
    block = lax.axis_index("range") * stack_size + lax.axis_index("stack")
    node = block // 2
    even = node % 2 == 0

    def flat(ref):
        return jnp.concatenate([ref[row : row + 1, :] for row in range(row_local)], axis=1)

    coherence = flat(coherence_ref).astype(jnp.float32)
    tiles = flat(tiles_ref)
    pixel = lax.broadcasted_iota(jnp.int32, (1, pixel_count), 1)
    row = jnp.zeros_like(pixel)
    for step in range(1, row_local):
        row = row + (pixel >= step * col_local).astype(jnp.int32)
    column = block * col_local + (pixel - row * col_local)
    row = row + lax.axis_index("azimuth") * row_local
    coord_u = (row.astype(jnp.float32) + 0.5) / row_total - 0.5
    coord_v = (column.astype(jnp.float32) + 0.5) / col_total - 0.5
    basis = jnp.concatenate([jnp.ones_like(coord_u), coord_u, coord_v], axis=0)
    spare = jnp.zeros((2, pixel_count), jnp.float32)
    lines, inside = [], []
    for base in (jnp.where(even, 2 * node - 1, 2 * node + 1), jnp.where(even, 2 * node + 1, 2 * node - 1)):
        held = [(tiles == base + step).astype(jnp.float32) for step in range(2)]
        for line in range(3):
            lines += [basis[line : line + 1] * each for each in held]
        lines.append(spare)
        inside += held
    weighted_ref[...] = jnp.concatenate(lines, axis=0) * coherence
    member_ref[...] = jnp.concatenate(
        [basis[line : line + 1] * each for line in range(3) for each in inside] + [spare, spare], axis=0
    )
    basis_ref[...] = jnp.concatenate([basis, coherence, jnp.zeros((4, pixel_count), jnp.float32)], axis=0)


def prepare(pairs, preconditioner, coherence, tiles, date_pad, date_rows, order, col_total, row_total):
    ifg_total = pairs.shape[1]
    pixel_count = coherence.size
    arguments = (pairs, preconditioner, coherence, tiles)
    shapes = [((ifg_total, 2 * date_pad), jnp.bfloat16)]
    shapes += [((date_rows, ifg_total), jnp.bfloat16)] * 2
    shapes += [((rows, pixel_count), jnp.float32) for rows in (16, 16, 8)]
    whole = pl.BlockSpec(memory_space=pltpu.VMEM)
    return pl.pallas_call(
        functools.partial(prepare_kernel, order=order, col_total=col_total, row_total=row_total),
        out_shape=[jax.ShapeDtypeStruct(shape, dtype) for shape, dtype in shapes],
        in_specs=[pl.BlockSpec(memory_space=pltpu.HBM)] * 4,
        out_specs=[whole] * 6,
        scratch_shapes=[
            *(pltpu.VMEM(value.shape, value.dtype) for value in arguments),
            pltpu.VMEM(pairs.shape, jnp.int32),
            pltpu.SemaphoreType.DMA((4,)),
        ],
        compiler_params=pltpu.CompilerParams(vmem_limit_bytes=VMEM_LIMIT),
        name="prepare",
    )(*(pltpu.with_memory_space_constraint(value, pltpu.HBM) for value in arguments))


def unpack(chunk_refs, wide, data, row_local):
    start = 0
    col_local = chunk_refs[0].shape[1]
    for ref in chunk_refs:
        count = ref.shape[0] // row_local
        wide[pl.ds(0, ref.shape[0]), :] = ref[...].astype(jnp.float32)
        for row in range(row_local):
            data[pl.ds(start, count), row * col_local : (row + 1) * col_local] = wide[
                pl.ds(row, count, stride=row_local), :
            ].astype(jnp.bfloat16)
        start += count


def gained(gain_top, gain_low, rows, columns, value):
    part = product(gain_top[rows, columns], value)
    if gain_low is not None:
        part = part + product(gain_low[rows, columns], value)
    return part


def early_kernel(*refs, row_local, start, end, late):
    *chunk_refs, gain_top, gain_low, data_ref, series_ref, wide = refs
    unpack(chunk_refs[:late], wide, data_ref, row_local)
    before = chunk_refs[late:]
    columns = pl.ds(start, end - start)
    value = data_ref[...]
    if before:
        held = before[0].shape[0] - start
        value = jnp.concatenate([before[0][pl.ds(start, held), :], value[: end - start - held]], axis=0)
    else:
        value = value[:end]
    half = series_ref.shape[0] // 2
    for first in (0, half):
        rows = pl.ds(first, half)
        part = gained(gain_top, gain_low, rows, columns, value)
        series_ref[rows, :] = part + before[1][rows, :] if before else part


def early_fit(chunks, before, gains, row_local, start, end):
    count = sum(chunk.shape[0] for chunk in chunks) // row_local
    pixel_count = chunks[0].shape[1] * row_local
    return pl.pallas_call(
        functools.partial(
            early_kernel, row_local=row_local, start=start, end=end, late=len(chunks)
        ),
        out_shape=[
            jax.ShapeDtypeStruct((count, pixel_count), jnp.bfloat16),
            jax.ShapeDtypeStruct((gains[0].shape[0], pixel_count), jnp.float32),
        ],
        scratch_shapes=[pltpu.VMEM(chunks[0].shape, jnp.float32)],
        compiler_params=pltpu.CompilerParams(vmem_limit_bytes=VMEM_LIMIT),
        name="early_fit",
    )(*chunks, *before, *gains)


def invert_kernel(*refs, row_local, date_total, late):
    (
        *chunk_refs, incidence, gain_top, gain_low, weighted_ref, basis_ref, series_ref,
        moments_ref, wide, data, residual, moved,
    ) = refs
    ifg_total, pixel_count = moved.shape
    date_rows = gain_top.shape[0]
    date_pad = incidence.shape[1] // 2
    late_refs, early_refs = chunk_refs[:late], chunk_refs[late:]
    done = 0
    pieces = []
    if early_refs:
        *early_data, early_series = early_refs
        for ref in early_data:
            count = ref.shape[0]
            used = min(count, (done + count) // 128 * 128 - done) if ref is early_data[-1] else count
            pieces.append((ref, done, used))
            done += used
        data[pl.ds(0, count - used), :] = early_data[-1][pl.ds(used, count - used), :]
        unpack(late_refs, wide, data.at[pl.ds(count - used, ifg_total - done - count + used)], row_local)
    else:
        unpack(late_refs, wide, data, row_local)
    pieces.append((data, done, ifg_total - done))

    def observed(rows):
        parts = []
        for ref, first, count in pieces:
            low, high = max(rows.start, first), min(rows.start + rows.size, first + count)
            if low < high:
                parts.append(ref[pl.ds(low - first, high - low), :])
        return parts[0] if len(parts) == 1 else jnp.concatenate(parts, axis=0)

    coherence = basis_ref[3:4, :]
    date_tiles = [pl.ds(start, date_rows // 2) for start in (0, date_rows // 2)]
    spare = [jnp.zeros((date_pad - date_rows, pixel_count), jnp.bfloat16)]
    ifg_tiles = [pl.ds(start, ROWS_A) for start in range(0, ifg_total, ROWS_A)]
    everything = slice(None)

    def folded(square):
        return jnp.sum(square.reshape(-1, 8, pixel_count), axis=0)

    def reweighted(total):
        scale = jnp.sum(total, axis=0, keepdims=True) / ifg_total + 1e-06
        strength = coherence * (scale * scale)
        for rows in ifg_tiles:
            left = residual[rows, :]
            inverse = pl.reciprocal(left * left + scale, approx=APPROX)
            moved[rows, :] = ((inverse * left) * (inverse * strength)).astype(jnp.bfloat16)

    left_columns = pl.ds(done, ifg_total - done)
    tops, lows = [], []
    for rows in date_tiles:
        part = gained(gain_top, gain_low, rows, left_columns, data[...])
        if early_refs:
            part = part + early_series[rows, :]
        series_ref[rows, :] = part
        top, low = halves(part)
        tops.append(top)
        lows.append(low)
    both = jnp.concatenate(tops + spare + lows + spare, axis=0)
    total = jnp.zeros((8, pixel_count), jnp.float32)
    for rows in ifg_tiles:
        left = observed(rows).astype(jnp.float32) - product(incidence[rows, :], both)
        residual[rows, :] = left
        total = total + folded(left * left)
    reweighted(total)
    for sweep in range(1, REWEIGHTS):
        steps = []
        for rows in date_tiles:
            part = gained(gain_top, None, rows, everything, moved[...])
            steps.append(part.astype(jnp.bfloat16))
            series_ref[rows, :] = series_ref[rows, :] + part
        step = jnp.concatenate(steps + spare, axis=0)
        total = jnp.zeros((8, pixel_count), jnp.float32)
        for rows in ifg_tiles:
            left = residual[rows, :] - product(incidence[rows, :date_pad], step)
            residual[rows, :] = left
            total = total + folded(left * left)
        held = moved[...]
        for rows in date_tiles:
            series_ref[rows, :] = series_ref[rows, :] + product(gain_low[rows, :], held)
        reweighted(total)
    for rows in date_tiles:
        part = gained(gain_top, None, rows, everything, moved[...])
        series_ref[rows, :] = series_ref[rows, :] + part
    series_ref[pl.ds(date_total, 8), :] = basis_ref[...]
    series_top, series_low = halves(series_ref[...])
    weighted_top, weighted_low = halves(weighted_ref[...])
    across = (((1,), (1,)), ((), ()))
    moments_ref[...] = product(weighted_top, series_top, across) + (
        product(weighted_low, series_top, across) + product(weighted_top, series_low, across)
    )


def invert(late_chunks, early, incidence, gains, weighted, basis, row_local, date_total):
    ifg_total = incidence.shape[0]
    kept = sum(value.shape[0] for value in early[:-1]) // 128 * 128
    date_rows = gains[0].shape[0]
    pixel_count = weighted.shape[1]
    return pl.pallas_call(
        functools.partial(
            invert_kernel, row_local=row_local, date_total=date_total, late=len(late_chunks)
        ),
        out_shape=[
            jax.ShapeDtypeStruct((date_rows, pixel_count), jnp.float32),
            jax.ShapeDtypeStruct((weighted.shape[0], date_rows), jnp.float32),
        ],
        scratch_shapes=[
            pltpu.VMEM(late_chunks[0].shape, jnp.float32),
            pltpu.VMEM((ifg_total - kept, pixel_count), jnp.bfloat16),
            pltpu.VMEM((ifg_total, pixel_count), jnp.float32),
            pltpu.VMEM((ifg_total, pixel_count), jnp.bfloat16),
        ],
        compiler_params=pltpu.CompilerParams(vmem_limit_bytes=VMEM_LIMIT),
        name="invert",
    )(*late_chunks, *early, incidence, *gains, weighted, basis)


def cut_kernel(source, *refs):
    *targets, sems = refs
    copies = [
        pltpu.make_async_copy(
            source.at[:, lax.axis_index("stack") ^ mask], target, sems.at[mask]
        )
        for mask, target in enumerate(targets)
    ]
    for copy in copies:
        copy.start()
    for copy in copies:
        copy.wait()


def cut(phases, col_local):
    ifg_local, row_local, col_range = phases.shape
    count = col_range // col_local
    view = phases.reshape(ifg_local, row_local, count, col_local).transpose(0, 2, 1, 3)
    return pl.pallas_call(
        cut_kernel,
        out_shape=[jax.ShapeDtypeStruct((ifg_local, row_local, col_local), phases.dtype)] * count,
        in_specs=[pl.BlockSpec(memory_space=pltpu.HBM)],
        out_specs=[pl.BlockSpec(memory_space=pltpu.VMEM)] * count,
        scratch_shapes=[pltpu.SemaphoreType.DMA((count,))],
        compiler_params=pltpu.CompilerParams(vmem_limit_bytes=8 * 1024 * 1024),
        name="cut",
    )(pltpu.with_memory_space_constraint(view, pltpu.HBM))


def exchange(phases, stack_size):
    ifg_local, row_local, col_range = phases.shape
    col_local = col_range // stack_size
    if stack_size != 8:
        blocks = phases.reshape(ifg_local, row_local, stack_size, col_local).transpose(2, 0, 1, 3)
        stacked = lax.all_to_all(blocks, "stack", split_axis=0, concat_axis=0, tiled=True)
        return [stacked.reshape(-1, col_local)], (0,)
    blocks = cut(phases, col_local)
    found = {0: blocks[0]}

    def send(mask, after=None):
        block = blocks[mask]
        if after is not None:
            block, found[after] = lax.optimization_barrier((block, found[after]))
        found[mask] = lax.ppermute(block, "stack", [(i, i ^ mask) for i in range(stack_size)])

    for mask, after in ((4, None), (5, None), (1, None), (6, None), (2, None), (7, 1), (3, 2)):
        send(mask, after)
    return [found[mask].reshape(-1, col_local) for mask in ARRIVAL], ARRIVAL


def plane_solve(gram_matrix, right_side):

    def entry(row_pos, col_pos):
        return gram_matrix[row_pos % 3][col_pos % 3]

    cofactors = [
        [
            entry(row_pos + 1, col_pos + 1) * entry(row_pos + 2, col_pos + 2)
            - entry(row_pos + 1, col_pos + 2) * entry(row_pos + 2, col_pos + 1)
            for col_pos in range(3)
        ]
        for row_pos in range(3)
    ]
    determinant = (
        entry(0, 0) * cofactors[0][0]
        + entry(0, 1) * cofactors[0][1]
        + entry(0, 2) * cofactors[0][2]
    )
    return [
        (
            (cofactors[0][col_pos] / determinant) * right_side[0]
            + (cofactors[1][col_pos] / determinant) * right_side[1]
            + (cofactors[2][col_pos] / determinant) * right_side[2]
        )
        for col_pos in range(3)
    ]


def deramp_kernel(first_ref, *refs, row_local, date_total):
    *others, series_ref, member_ref, out_ref, staged, sems = refs
    totals = first_ref[...]
    for other in others:
        totals = totals + other[...]
    sums = [
        jnp.concatenate([totals[2 * k : 2 * k + 2], totals[8 + 2 * k : 10 + 2 * k]], axis=0)
        for k in range(3)
    ]
    gram = [
        [sums[k][:, date_total + m : date_total + m + 1] + (1.0 if k == m else 0.0) for m in range(3)]
        for k in range(3)
    ]
    planes = plane_solve(gram, sums)
    planes.append(jnp.zeros_like(planes[0]))
    planes_top, planes_low = halves(jnp.concatenate(planes, axis=0))
    member_top, member_low = halves(member_ref[...])
    ramp = product(
        jnp.concatenate([planes_top, planes_low, planes_top], axis=0),
        jnp.concatenate([member_top, member_top, member_low], axis=0),
        (((0,), (0,)), ((), ())),
    )
    col_local = series_ref.shape[1] // row_local
    copies = []
    step = date_total // OUT_PARTS
    for part in range(OUT_PARTS):
        start = part * step
        flat = series_ref[pl.ds(start, step), :] - ramp[start : start + step]
        for row in range(row_local):
            staged[pl.ds(start * row_local + row, step, stride=row_local), :] = flat[
                :, row * col_local : (row + 1) * col_local
            ]
        rows = pl.ds(start * row_local, step * row_local)
        copy = pltpu.make_async_copy(staged.at[rows], out_ref.at[rows], sems.at[part])
        copy.start()
        copies.append(copy)
    for copy in copies:
        copy.wait()


def deramp(parts, series, member, row_local, date_total):
    col_local = series.shape[1] // row_local
    shape = (date_total * row_local, col_local)
    whole = pl.BlockSpec(memory_space=pltpu.VMEM)
    return pl.pallas_call(
        functools.partial(deramp_kernel, row_local=row_local, date_total=date_total),
        out_shape=jax.ShapeDtypeStruct(shape, jnp.float32),
        in_specs=[whole] * (len(parts) + 2),
        out_specs=pl.BlockSpec(memory_space=pl.ANY),
        scratch_shapes=[pltpu.VMEM(shape, jnp.float32), pltpu.SemaphoreType.DMA((OUT_PARTS,))],
        compiler_params=pltpu.CompilerParams(vmem_limit_bytes=VMEM_LIMIT),
        name="deramp",
    )(*parts, series, member)


def swap(value, axes, pairs):
    both = [(i, j) for i, j in pairs] + [(j, i) for i, j in pairs]
    return lax.ppermute(value, axes, both)


def local(phases, ifg_pairs, preconditioner, coherence, geo_tiles):
    stack_size = lax.axis_size("stack")
    range_size = lax.axis_size("range")
    azimuth_size = lax.axis_size("azimuth")
    ifg_local, row_local, col_range = phases.shape
    date_total = preconditioner.shape[0]
    date_rows = -(-(date_total + 8) // 32) * 32
    date_pad = -(-date_rows // LANES) * LANES

    chunks, order = exchange(phases, stack_size)
    incidence, *gains, member, weighted, basis = prepare(
        ifg_pairs.T, preconditioner, coherence, geo_tiles, date_pad, date_rows, order,
        col_range * range_size, row_local * azimuth_size,
    )
    early = []
    if len(chunks) > 1:
        first, second = EARLY
        count = ifg_local * first // 256 * 256
        data_a, series_a = early_fit(chunks[:first], [], gains, row_local, 0, count)
        data_b, series_b = early_fit(
            chunks[first:second], [data_a, series_a], gains, row_local, count,
            ifg_local * second // 128 * 128,
        )
        early = [data_a, data_b, series_b]
        chunks = chunks[second:]

    series, moments = invert(
        chunks, early, incidence, gains, weighted, basis, row_local, date_total
    )

    def place(block):
        return (block % stack_size) * range_size + block // stack_size

    block_count = stack_size * range_size
    inner = [
        (place(block), place(block + 2)) for block in range(block_count - 2) if block // 2 % 2 == 0
    ]
    outer = [
        (place(block), place(block + 2)) for block in range(block_count - 2) if block // 2 % 2 == 1
    ]
    axes = ("stack", "range")
    outer += [(place(0), place(1)), (place(block_count - 2), place(block_count - 1))]
    first = swap(moments[:8], axes, outer)
    node = (lax.axis_index("range") * stack_size + lax.axis_index("stack")) // 2
    first = jnp.where((node > 0) & (node < block_count // 2 - 1), first, 0.0)
    second = swap(moments[8:], axes, inner)
    moments = moments + jnp.concatenate([first, second], axis=0)
    pairs = [(i, i + 1) for i in range(0, stack_size, 2)]
    crossed = [
        (i * azimuth_size + a, (i + 1) * azimuth_size + (azimuth_size - 1 - a))
        for i in range(0, stack_size, 2)
        for a in range(azimuth_size)
    ]
    parts = [
        moments,
        swap(moments, "azimuth", [(0, 1)]),
        swap(moments, "stack", pairs),
        swap(moments, ("stack", "azimuth"), crossed),
    ]
    flat = deramp(parts, series, member, row_local, date_total)
    return flat.reshape(date_total, row_local, -1)


def solution(mesh):
    return jax.shard_map(
        local,
        mesh=mesh,
        in_specs=(
            P("stack", "azimuth", "range"),
            P(),
            P(),
            P("azimuth", ("range", "stack")),
            P("azimuth", ("range", "stack")),
        ),
        out_specs=P(None, "azimuth", ("range", "stack")),
        check_vma=False,
    )
```

```python
import functools

import jax
import jax.numpy as jnp
from jax import lax
from jax.experimental import pallas as pl
from jax.experimental.pallas import tpu as pltpu
from jax.sharding import PartitionSpec as P

REWEIGHTS = 2
LANES = 128
VMEM_LIMIT = 24 * 1024 * 1024
ROWS_A = 192
APPROX = False
ARRIVAL = (0, 1, 2, 4, 5, 6, 7, 3)
EARLY = (4, 6)
OUT_PARTS = 5


def halves(value):
    top = value.astype(jnp.bfloat16)
    return top, (value - top.astype(jnp.float32)).astype(jnp.bfloat16)


def product(left, right, dims=(((1,), (0,)), ((), ()))):
    return lax.dot_general(left, right, dims, preferred_element_type=jnp.float32)


def prepare_kernel(
    pairs_hbm, prec_hbm, coherence_hbm, tiles_hbm, incidence_ref, gain_top, gain_low, member_ref,
    weighted_ref, basis_ref, pairs_ref, prec_ref, coherence_ref, tiles_ref, pairs, sems, *, order,
    col_total, row_total,
):
    copies = [
        pltpu.make_async_copy(source, target, sems.at[index])
        for index, (source, target) in enumerate(
            (
                (pairs_hbm, pairs_ref),
                (prec_hbm, prec_ref),
                (coherence_hbm, coherence_ref),
                (tiles_hbm, tiles_ref),
            )
        )
    ]
    for copy in copies:
        copy.start()
    copies[0].wait()
    chunk = pairs_ref.shape[1] // len(order)
    date_total = prec_ref.shape[0]
    ifg_total = gain_top.shape[1]
    date_pad = incidence_ref.shape[1] // 2
    for position, mask in enumerate(order):
        moved = pairs_ref[...]
        if len(order) > 1:
            back = (len(order) - (lax.axis_index("stack") ^ mask)) % len(order)
            moved = pltpu.roll(moved, back * chunk, 1)
        pairs[:, position * chunk : (position + 1) * chunk] = moved[:, :chunk]
    date_ids = lax.broadcasted_iota(jnp.int32, (date_pad, ifg_total), 0)
    incidence_t = (
        jnp.where(date_ids == pairs[1:2, :], 1.0, 0.0)
        - jnp.where(date_ids == pairs[0:1, :], 1.0, 0.0)
    ).astype(jnp.bfloat16)
    incidence = incidence_t.T
    incidence_ref[:, :date_pad] = incidence
    incidence_ref[:, date_pad:] = incidence
    for copy in copies[1:]:
        copy.wait()
    prec = prec_ref[...]
    prec = prec - jnp.sum(prec, axis=1, keepdims=True) / date_total
    top, low = halves(prec)
    used = incidence_t[:date_total]
    gain_a, gain_b = halves(product(top, used) + product(low, used))
    zeros = jnp.zeros((gain_top.shape[0] - date_total, ifg_total), jnp.bfloat16)
    gain_top[...] = jnp.concatenate([gain_a, zeros], axis=0)
    gain_low[...] = jnp.concatenate([gain_b, zeros], axis=0)

    row_local, col_local = coherence_ref.shape
    pixel_count = row_local * col_local
    stack_size = lax.axis_size("stack")
    block = lax.axis_index("range") * stack_size + lax.axis_index("stack")
    node = block // 2
    even = node % 2 == 0

    def flat(ref):
        return jnp.concatenate([ref[row : row + 1, :] for row in range(row_local)], axis=1)

    coherence = flat(coherence_ref).astype(jnp.float32)
    tiles = flat(tiles_ref)
    pixel = lax.broadcasted_iota(jnp.int32, (1, pixel_count), 1)
    row = jnp.zeros_like(pixel)
    for step in range(1, row_local):
        row = row + (pixel >= step * col_local).astype(jnp.int32)
    column = block * col_local + (pixel - row * col_local)
    row = row + lax.axis_index("azimuth") * row_local
    coord_u = (row.astype(jnp.float32) + 0.5) / row_total - 0.5
    coord_v = (column.astype(jnp.float32) + 0.5) / col_total - 0.5
    basis = jnp.concatenate([jnp.ones_like(coord_u), coord_u, coord_v], axis=0)
    spare = jnp.zeros((2, pixel_count), jnp.float32)
    lines, inside = [], []
    for base in (jnp.where(even, 2 * node - 1, 2 * node + 1), jnp.where(even, 2 * node + 1, 2 * node - 1)):
        held = [(tiles == base + step).astype(jnp.float32) for step in range(2)]
        for line in range(3):
            lines += [basis[line : line + 1] * each for each in held]
        lines.append(spare)
        inside += held
    weighted_ref[...] = jnp.concatenate(lines, axis=0) * coherence
    member_ref[...] = jnp.concatenate(
        [basis[line : line + 1] * each for line in range(3) for each in inside] + [spare, spare], axis=0
    )
    basis_ref[...] = jnp.concatenate([basis, coherence, jnp.zeros((4, pixel_count), jnp.float32)], axis=0)


def prepare(pairs, preconditioner, coherence, tiles, date_pad, date_rows, order, col_total, row_total):
    ifg_total = pairs.shape[1]
    pixel_count = coherence.size
    arguments = (pairs, preconditioner, coherence, tiles)
    shapes = [((ifg_total, 2 * date_pad), jnp.bfloat16)]
    shapes += [((date_rows, ifg_total), jnp.bfloat16)] * 2
    shapes += [((rows, pixel_count), jnp.float32) for rows in (16, 16, 8)]
    whole = pl.BlockSpec(memory_space=pltpu.VMEM)
    return pl.pallas_call(
        functools.partial(prepare_kernel, order=order, col_total=col_total, row_total=row_total),
        out_shape=[jax.ShapeDtypeStruct(shape, dtype) for shape, dtype in shapes],
        in_specs=[pl.BlockSpec(memory_space=pltpu.HBM)] * 4,
        out_specs=[whole] * 6,
        scratch_shapes=[
            *(pltpu.VMEM(value.shape, value.dtype) for value in arguments),
            pltpu.VMEM(pairs.shape, jnp.int32),
            pltpu.SemaphoreType.DMA((4,)),
        ],
        compiler_params=pltpu.CompilerParams(vmem_limit_bytes=VMEM_LIMIT),
        name="prepare",
    )(*(pltpu.with_memory_space_constraint(value, pltpu.HBM) for value in arguments))


def unpack(chunk_refs, wide, data, row_local):
    start = 0
    col_local = chunk_refs[0].shape[1]
    for ref in chunk_refs:
        count = ref.shape[0] // row_local
        wide[pl.ds(0, ref.shape[0]), :] = ref[...].astype(jnp.float32)
        for row in range(row_local):
            data[pl.ds(start, count), row * col_local : (row + 1) * col_local] = wide[
                pl.ds(row, count, stride=row_local), :
            ].astype(jnp.bfloat16)
        start += count


def gained(gain_top, gain_low, rows, columns, value):
    part = product(gain_top[rows, columns], value)
    if gain_low is not None:
        part = part + product(gain_low[rows, columns], value)
    return part


def early_kernel(*refs, row_local, start, end, late):
    *chunk_refs, gain_top, gain_low, data_ref, series_ref, wide = refs
    unpack(chunk_refs[:late], wide, data_ref, row_local)
    before = chunk_refs[late:]
    columns = pl.ds(start, end - start)
    value = data_ref[...]
    if before:
        held = before[0].shape[0] - start
        value = jnp.concatenate([before[0][pl.ds(start, held), :], value[: end - start - held]], axis=0)
    else:
        value = value[:end]
    half = series_ref.shape[0] // 2
    for first in (0, half):
        rows = pl.ds(first, half)
        part = gained(gain_top, gain_low, rows, columns, value)
        series_ref[rows, :] = part + before[1][rows, :] if before else part


def early_fit(chunks, before, gains, row_local, start, end):
    count = sum(chunk.shape[0] for chunk in chunks) // row_local
    pixel_count = chunks[0].shape[1] * row_local
    return pl.pallas_call(
        functools.partial(
            early_kernel, row_local=row_local, start=start, end=end, late=len(chunks)
        ),
        out_shape=[
            jax.ShapeDtypeStruct((count, pixel_count), jnp.bfloat16),
            jax.ShapeDtypeStruct((gains[0].shape[0], pixel_count), jnp.float32),
        ],
        scratch_shapes=[pltpu.VMEM(chunks[0].shape, jnp.float32)],
        compiler_params=pltpu.CompilerParams(vmem_limit_bytes=VMEM_LIMIT),
        name="early_fit",
    )(*chunks, *before, *gains)


def invert_kernel(*refs, row_local, date_total, late):
    (
        *chunk_refs, incidence, gain_top, gain_low, weighted_ref, basis_ref, series_ref,
        moments_ref, wide, data, residual, moved,
    ) = refs
    ifg_total, pixel_count = moved.shape
    date_rows = gain_top.shape[0]
    date_pad = incidence.shape[1] // 2
    late_refs, early_refs = chunk_refs[:late], chunk_refs[late:]
    done = 0
    pieces = []
    if early_refs:
        *early_data, early_series = early_refs
        for ref in early_data:
            count = ref.shape[0]
            used = min(count, (done + count) // 128 * 128 - done) if ref is early_data[-1] else count
            pieces.append((ref, done, used))
            done += used
        data[pl.ds(0, count - used), :] = early_data[-1][pl.ds(used, count - used), :]
        unpack(late_refs, wide, data.at[pl.ds(count - used, ifg_total - done - count + used)], row_local)
    else:
        unpack(late_refs, wide, data, row_local)
    pieces.append((data, done, ifg_total - done))

    def observed(rows):
        parts = []
        for ref, first, count in pieces:
            low, high = max(rows.start, first), min(rows.start + rows.size, first + count)
            if low < high:
                parts.append(ref[pl.ds(low - first, high - low), :])
        return parts[0] if len(parts) == 1 else jnp.concatenate(parts, axis=0)

    coherence = basis_ref[3:4, :]
    date_tiles = [pl.ds(start, date_rows // 2) for start in (0, date_rows // 2)]
    spare = [jnp.zeros((date_pad - date_rows, pixel_count), jnp.bfloat16)]
    ifg_tiles = [pl.ds(start, ROWS_A) for start in range(0, ifg_total, ROWS_A)]
    everything = slice(None)

    def folded(square):
        return jnp.sum(square.reshape(-1, 8, pixel_count), axis=0)

    def reweighted(total):
        scale = jnp.sum(total, axis=0, keepdims=True) / ifg_total + 1e-06
        strength = coherence * (scale * scale)
        for rows in ifg_tiles:
            left = residual[rows, :]
            inverse = pl.reciprocal(left * left + scale, approx=APPROX)
            moved[rows, :] = ((inverse * left) * (inverse * strength)).astype(jnp.bfloat16)

    left_columns = pl.ds(done, ifg_total - done)
    tops, lows = [], []
    for rows in date_tiles:
        part = gained(gain_top, gain_low, rows, left_columns, data[...])
        if early_refs:
            part = part + early_series[rows, :]
        series_ref[rows, :] = part
        top, low = halves(part)
        tops.append(top)
        lows.append(low)
    both = jnp.concatenate(tops + spare + lows + spare, axis=0)
    total = jnp.zeros((8, pixel_count), jnp.float32)
    for rows in ifg_tiles:
        left = observed(rows).astype(jnp.float32) - product(incidence[rows, :], both)
        residual[rows, :] = left
        total = total + folded(left * left)
    reweighted(total)
    for sweep in range(1, REWEIGHTS):
        steps = []
        for rows in date_tiles:
            part = gained(gain_top, None, rows, everything, moved[...])
            steps.append(part.astype(jnp.bfloat16))
            series_ref[rows, :] = series_ref[rows, :] + part
        step = jnp.concatenate(steps + spare, axis=0)
        total = jnp.zeros((8, pixel_count), jnp.float32)
        for rows in ifg_tiles:
            left = residual[rows, :] - product(incidence[rows, :date_pad], step)
            residual[rows, :] = left
            total = total + folded(left * left)
        held = moved[...]
        for rows in date_tiles:
            series_ref[rows, :] = series_ref[rows, :] + product(gain_low[rows, :], held)
        reweighted(total)
    for rows in date_tiles:
        part = gained(gain_top, None, rows, everything, moved[...])
        series_ref[rows, :] = series_ref[rows, :] + part
    series_ref[pl.ds(date_total, 8), :] = basis_ref[...]
    series_top, series_low = halves(series_ref[...])
    weighted_top, weighted_low = halves(weighted_ref[...])
    across = (((1,), (1,)), ((), ()))
    moments_ref[...] = product(weighted_top, series_top, across) + (
        product(weighted_low, series_top, across) + product(weighted_top, series_low, across)
    )


def invert(late_chunks, early, incidence, gains, weighted, basis, row_local, date_total):
    ifg_total = incidence.shape[0]
    kept = sum(value.shape[0] for value in early[:-1]) // 128 * 128
    date_rows = gains[0].shape[0]
    pixel_count = weighted.shape[1]
    return pl.pallas_call(
        functools.partial(
            invert_kernel, row_local=row_local, date_total=date_total, late=len(late_chunks)
        ),
        out_shape=[
            jax.ShapeDtypeStruct((date_rows, pixel_count), jnp.float32),
            jax.ShapeDtypeStruct((weighted.shape[0], date_rows), jnp.float32),
        ],
        scratch_shapes=[
            pltpu.VMEM(late_chunks[0].shape, jnp.float32),
            pltpu.VMEM((ifg_total - kept, pixel_count), jnp.bfloat16),
            pltpu.VMEM((ifg_total, pixel_count), jnp.float32),
            pltpu.VMEM((ifg_total, pixel_count), jnp.bfloat16),
        ],
        compiler_params=pltpu.CompilerParams(vmem_limit_bytes=VMEM_LIMIT),
        name="invert",
    )(*late_chunks, *early, incidence, *gains, weighted, basis)


def cut_kernel(source, *refs):
    *targets, sems = refs
    copies = [
        pltpu.make_async_copy(
            source.at[:, lax.axis_index("stack") ^ mask], target, sems.at[mask]
        )
        for mask, target in enumerate(targets)
    ]
    for copy in copies:
        copy.start()
    for copy in copies:
        copy.wait()


def cut(phases, col_local):
    ifg_local, row_local, col_range = phases.shape
    count = col_range // col_local
    view = phases.reshape(ifg_local, row_local, count, col_local).transpose(0, 2, 1, 3)
    return pl.pallas_call(
        cut_kernel,
        out_shape=[jax.ShapeDtypeStruct((ifg_local, row_local, col_local), phases.dtype)] * count,
        in_specs=[pl.BlockSpec(memory_space=pltpu.HBM)],
        out_specs=[pl.BlockSpec(memory_space=pltpu.VMEM)] * count,
        scratch_shapes=[pltpu.SemaphoreType.DMA((count,))],
        compiler_params=pltpu.CompilerParams(vmem_limit_bytes=8 * 1024 * 1024),
        name="cut",
    )(pltpu.with_memory_space_constraint(view, pltpu.HBM))


def exchange(phases, stack_size):
    ifg_local, row_local, col_range = phases.shape
    col_local = col_range // stack_size
    if stack_size != 8:
        blocks = phases.reshape(ifg_local, row_local, stack_size, col_local).transpose(2, 0, 1, 3)
        stacked = lax.all_to_all(blocks, "stack", split_axis=0, concat_axis=0, tiled=True)
        return [stacked.reshape(-1, col_local)], (0,)
    blocks = cut(phases, col_local)
    found = {0: blocks[0]}

    def send(mask, after=None):
        block = blocks[mask]
        if after is not None:
            block, found[after] = lax.optimization_barrier((block, found[after]))
        found[mask] = lax.ppermute(block, "stack", [(i, i ^ mask) for i in range(stack_size)])

    for mask, after in ((4, None), (5, None), (1, None), (6, None), (2, None), (7, 1), (3, 2)):
        send(mask, after)
    return [found[mask].reshape(-1, col_local) for mask in ARRIVAL], ARRIVAL


def plane_solve(gram_matrix, right_side):

    def entry(row_pos, col_pos):
        return gram_matrix[row_pos % 3][col_pos % 3]

    cofactors = [
        [
            entry(row_pos + 1, col_pos + 1) * entry(row_pos + 2, col_pos + 2)
            - entry(row_pos + 1, col_pos + 2) * entry(row_pos + 2, col_pos + 1)
            for col_pos in range(3)
        ]
        for row_pos in range(3)
    ]
    determinant = (
        entry(0, 0) * cofactors[0][0]
        + entry(0, 1) * cofactors[0][1]
        + entry(0, 2) * cofactors[0][2]
    )
    return [
        (
            (cofactors[0][col_pos] / determinant) * right_side[0]
            + (cofactors[1][col_pos] / determinant) * right_side[1]
            + (cofactors[2][col_pos] / determinant) * right_side[2]
        )
        for col_pos in range(3)
    ]


def deramp_kernel(first_ref, *refs, row_local, date_total):
    *others, series_ref, member_ref, out_ref, staged, sems = refs
    totals = first_ref[...]
    for other in others:
        totals = totals + other[...]
    sums = [
        jnp.concatenate([totals[2 * k : 2 * k + 2], totals[8 + 2 * k : 10 + 2 * k]], axis=0)
        for k in range(3)
    ]
    gram = [
        [sums[k][:, date_total + m : date_total + m + 1] + (1.0 if k == m else 0.0) for m in range(3)]
        for k in range(3)
    ]
    planes = plane_solve(gram, sums)
    planes.append(jnp.zeros_like(planes[0]))
    planes_top, planes_low = halves(jnp.concatenate(planes, axis=0))
    member_top, member_low = halves(member_ref[...])
    ramp = product(
        jnp.concatenate([planes_top, planes_low, planes_top], axis=0),
        jnp.concatenate([member_top, member_top, member_low], axis=0),
        (((0,), (0,)), ((), ())),
    )
    col_local = series_ref.shape[1] // row_local
    copies = []
    step = date_total // OUT_PARTS
    for part in range(OUT_PARTS):
        start = part * step
        flat = series_ref[pl.ds(start, step), :] - ramp[start : start + step]
        for row in range(row_local):
            staged[pl.ds(start * row_local + row, step, stride=row_local), :] = flat[
                :, row * col_local : (row + 1) * col_local
            ]
        rows = pl.ds(start * row_local, step * row_local)
        copy = pltpu.make_async_copy(staged.at[rows], out_ref.at[rows], sems.at[part])
        copy.start()
        copies.append(copy)
    for copy in copies:
        copy.wait()


def deramp(parts, series, member, row_local, date_total):
    col_local = series.shape[1] // row_local
    shape = (date_total * row_local, col_local)
    whole = pl.BlockSpec(memory_space=pltpu.VMEM)
    return pl.pallas_call(
        functools.partial(deramp_kernel, row_local=row_local, date_total=date_total),
        out_shape=jax.ShapeDtypeStruct(shape, jnp.float32),
        in_specs=[whole] * (len(parts) + 2),
        out_specs=pl.BlockSpec(memory_space=pl.ANY),
        scratch_shapes=[pltpu.VMEM(shape, jnp.float32), pltpu.SemaphoreType.DMA((OUT_PARTS,))],
        compiler_params=pltpu.CompilerParams(vmem_limit_bytes=VMEM_LIMIT),
        name="deramp",
    )(*parts, series, member)


def swap(value, axes, pairs):
    both = [(i, j) for i, j in pairs] + [(j, i) for i, j in pairs]
    return lax.ppermute(value, axes, both)


def local(phases, ifg_pairs, preconditioner, coherence, geo_tiles):
    stack_size = lax.axis_size("stack")
    range_size = lax.axis_size("range")
    azimuth_size = lax.axis_size("azimuth")
    ifg_local, row_local, col_range = phases.shape
    date_total = preconditioner.shape[0]
    date_rows = -(-(date_total + 8) // 32) * 32
    date_pad = -(-date_rows // LANES) * LANES

    chunks, order = exchange(phases, stack_size)
    incidence, *gains, member, weighted, basis = prepare(
        ifg_pairs.T, preconditioner, coherence, geo_tiles, date_pad, date_rows, order,
        col_range * range_size, row_local * azimuth_size,
    )
    early = []
    if len(chunks) > 1:
        first, second = EARLY
        count = ifg_local * first // 256 * 256
        data_a, series_a = early_fit(chunks[:first], [], gains, row_local, 0, count)
        data_b, series_b = early_fit(
            chunks[first:second], [data_a, series_a], gains, row_local, count,
            ifg_local * second // 128 * 128,
        )
        early = [data_a, data_b, series_b]
        chunks = chunks[second:]

    series, moments = invert(
        chunks, early, incidence, gains, weighted, basis, row_local, date_total
    )

    def place(block):
        return (block % stack_size) * range_size + block // stack_size

    block_count = stack_size * range_size
    inner = [
        (place(block), place(block + 2)) for block in range(block_count - 2) if block // 2 % 2 == 0
    ]
    outer = [
        (place(block), place(block + 2)) for block in range(block_count - 2) if block // 2 % 2 == 1
    ]
    axes = ("stack", "range")
    outer += [(place(0), place(1)), (place(block_count - 2), place(block_count - 1))]
    first = swap(moments[:8], axes, outer)
    node = (lax.axis_index("range") * stack_size + lax.axis_index("stack")) // 2
    first = jnp.where((node > 0) & (node < block_count // 2 - 1), first, 0.0)
    second = swap(moments[8:], axes, inner)
    moments = moments + jnp.concatenate([first, second], axis=0)
    pairs = [(i, i + 1) for i in range(0, stack_size, 2)]
    crossed = [
        (i * azimuth_size + a, (i + 1) * azimuth_size + (azimuth_size - 1 - a))
        for i in range(0, stack_size, 2)
        for a in range(azimuth_size)
    ]
    parts = [
        moments,
        swap(moments, ("stack", "azimuth"), crossed),
        swap(moments, "stack", pairs),
        swap(moments, "azimuth", [(0, 1)]),
    ]
    flat = deramp(parts, series, member, row_local, date_total)
    return flat.reshape(date_total, row_local, -1)


def solution(mesh):
    return jax.shard_map(
        local,
        mesh=mesh,
        in_specs=(
            P("stack", "azimuth", "range"),
            P(),
            P(),
            P("azimuth", ("range", "stack")),
            P("azimuth", ("range", "stack")),
        ),
        out_specs=P(None, "azimuth", ("range", "stack")),
        check_vma=False,
    )
```

```python
import functools

import jax
import jax.numpy as jnp
from jax import lax
from jax.experimental import pallas as pl
from jax.experimental.pallas import tpu as pltpu
from jax.sharding import PartitionSpec as P

REWEIGHTS = 2
LANES = 128
VMEM_LIMIT = 24 * 1024 * 1024
ROWS_A = 192
APPROX = False
ARRIVAL = (0, 1, 2, 4, 5, 6, 7, 3)
EARLY = (4, 6)
OUT_PARTS = 5


def halves(value):
    top = value.astype(jnp.bfloat16)
    return top, (value - top.astype(jnp.float32)).astype(jnp.bfloat16)


def product(left, right, dims=(((1,), (0,)), ((), ()))):
    return lax.dot_general(left, right, dims, preferred_element_type=jnp.float32)


def prepare_kernel(
    pairs_hbm, prec_hbm, coherence_hbm, tiles_hbm, incidence_ref, gain_top, gain_low, member_ref,
    weighted_ref, basis_ref, pairs_ref, prec_ref, coherence_ref, tiles_ref, pairs, sems, *, order,
    col_total, row_total,
):
    copies = [
        pltpu.make_async_copy(source, target, sems.at[index])
        for index, (source, target) in enumerate(
            (
                (pairs_hbm, pairs_ref),
                (prec_hbm, prec_ref),
                (coherence_hbm, coherence_ref),
                (tiles_hbm, tiles_ref),
            )
        )
    ]
    for copy in copies:
        copy.start()
    copies[0].wait()
    chunk = pairs_ref.shape[1] // len(order)
    date_total = prec_ref.shape[0]
    ifg_total = gain_top.shape[1]
    date_pad = incidence_ref.shape[1] // 2
    for position, mask in enumerate(order):
        moved = pairs_ref[...]
        if len(order) > 1:
            back = (len(order) - (lax.axis_index("stack") ^ mask)) % len(order)
            moved = pltpu.roll(moved, back * chunk, 1)
        pairs[:, position * chunk : (position + 1) * chunk] = moved[:, :chunk]
    date_ids = lax.broadcasted_iota(jnp.int32, (date_pad, ifg_total), 0)
    incidence_t = (
        jnp.where(date_ids == pairs[1:2, :], 1.0, 0.0)
        - jnp.where(date_ids == pairs[0:1, :], 1.0, 0.0)
    ).astype(jnp.bfloat16)
    incidence = incidence_t.T
    incidence_ref[:, :date_pad] = incidence
    incidence_ref[:, date_pad:] = incidence
    for copy in copies[1:]:
        copy.wait()
    prec = prec_ref[...]
    prec = prec - jnp.sum(prec, axis=1, keepdims=True) / date_total
    top, low = halves(prec)
    used = incidence_t[:date_total]
    gain_a, gain_b = halves(product(top, used) + product(low, used))
    zeros = jnp.zeros((gain_top.shape[0] - date_total, ifg_total), jnp.bfloat16)
    gain_top[...] = jnp.concatenate([gain_a, zeros], axis=0)
    gain_low[...] = jnp.concatenate([gain_b, zeros], axis=0)

    row_local, col_local = coherence_ref.shape
    pixel_count = row_local * col_local
    stack_size = lax.axis_size("stack")
    block = lax.axis_index("range") * stack_size + lax.axis_index("stack")
    node = block // 2
    even = node % 2 == 0

    def flat(ref):
        return jnp.concatenate([ref[row : row + 1, :] for row in range(row_local)], axis=1)

    coherence = flat(coherence_ref).astype(jnp.float32)
    tiles = flat(tiles_ref)
    pixel = lax.broadcasted_iota(jnp.int32, (1, pixel_count), 1)
    row = jnp.zeros_like(pixel)
    for step in range(1, row_local):
        row = row + (pixel >= step * col_local).astype(jnp.int32)
    column = block * col_local + (pixel - row * col_local)
    row = row + lax.axis_index("azimuth") * row_local
    coord_u = (row.astype(jnp.float32) + 0.5) / row_total - 0.5
    coord_v = (column.astype(jnp.float32) + 0.5) / col_total - 0.5
    basis = jnp.concatenate([jnp.ones_like(coord_u), coord_u, coord_v], axis=0)
    spare = jnp.zeros((2, pixel_count), jnp.float32)
    lines, inside = [], []
    for base in (jnp.where(even, 2 * node - 1, 2 * node + 1), jnp.where(even, 2 * node + 1, 2 * node - 1)):
        held = [(tiles == base + step).astype(jnp.float32) for step in range(2)]
        for line in range(3):
            lines += [basis[line : line + 1] * each for each in held]
        lines.append(spare)
        inside += held
    weighted_ref[...] = jnp.concatenate(lines, axis=0) * coherence
    member_ref[...] = jnp.concatenate(
        [basis[line : line + 1] * each for line in range(3) for each in inside] + [spare, spare], axis=0
    )
    basis_ref[...] = jnp.concatenate([basis, coherence, jnp.zeros((4, pixel_count), jnp.float32)], axis=0)


def prepare(pairs, preconditioner, coherence, tiles, date_pad, date_rows, order, col_total, row_total):
    ifg_total = pairs.shape[1]
    pixel_count = coherence.size
    arguments = (pairs, preconditioner, coherence, tiles)
    shapes = [((ifg_total, 2 * date_pad), jnp.bfloat16)]
    shapes += [((date_rows, ifg_total), jnp.bfloat16)] * 2
    shapes += [((rows, pixel_count), jnp.float32) for rows in (16, 16, 8)]
    whole = pl.BlockSpec(memory_space=pltpu.VMEM)
    return pl.pallas_call(
        functools.partial(prepare_kernel, order=order, col_total=col_total, row_total=row_total),
        out_shape=[jax.ShapeDtypeStruct(shape, dtype) for shape, dtype in shapes],
        in_specs=[pl.BlockSpec(memory_space=pltpu.HBM)] * 4,
        out_specs=[whole] * 6,
        scratch_shapes=[
            *(pltpu.VMEM(value.shape, value.dtype) for value in arguments),
            pltpu.VMEM(pairs.shape, jnp.int32),
            pltpu.SemaphoreType.DMA((4,)),
        ],
        compiler_params=pltpu.CompilerParams(vmem_limit_bytes=VMEM_LIMIT),
        name="prepare",
    )(*(pltpu.with_memory_space_constraint(value, pltpu.HBM) for value in arguments))


def unpack(chunk_refs, wide, data, row_local):
    start = 0
    col_local = chunk_refs[0].shape[1]
    for ref in chunk_refs:
        count = ref.shape[0] // row_local
        wide[pl.ds(0, ref.shape[0]), :] = ref[...].astype(jnp.float32)
        for row in range(row_local):
            data[pl.ds(start, count), row * col_local : (row + 1) * col_local] = wide[
                pl.ds(row, count, stride=row_local), :
            ].astype(jnp.bfloat16)
        start += count


def gained(gain_top, gain_low, rows, columns, value):
    part = product(gain_top[rows, columns], value)
    if gain_low is not None:
        part = part + product(gain_low[rows, columns], value)
    return part


def early_kernel(*refs, row_local, start, end, late):
    *chunk_refs, gain_top, gain_low, data_ref, series_ref, wide = refs
    unpack(chunk_refs[:late], wide, data_ref, row_local)
    before = chunk_refs[late:]
    columns = pl.ds(start, end - start)
    value = data_ref[...]
    if before:
        held = before[0].shape[0] - start
        value = jnp.concatenate([before[0][pl.ds(start, held), :], value[: end - start - held]], axis=0)
    else:
        value = value[:end]
    half = series_ref.shape[0] // 2
    for first in (0, half):
        rows = pl.ds(first, half)
        part = gained(gain_top, gain_low, rows, columns, value)
        series_ref[rows, :] = part + before[1][rows, :] if before else part


def early_fit(chunks, before, gains, row_local, start, end):
    count = sum(chunk.shape[0] for chunk in chunks) // row_local
    pixel_count = chunks[0].shape[1] * row_local
    return pl.pallas_call(
        functools.partial(
            early_kernel, row_local=row_local, start=start, end=end, late=len(chunks)
        ),
        out_shape=[
            jax.ShapeDtypeStruct((count, pixel_count), jnp.bfloat16),
            jax.ShapeDtypeStruct((gains[0].shape[0], pixel_count), jnp.float32),
        ],
        scratch_shapes=[pltpu.VMEM(chunks[0].shape, jnp.float32)],
        compiler_params=pltpu.CompilerParams(vmem_limit_bytes=VMEM_LIMIT),
        name="early_fit",
    )(*chunks, *before, *gains)


def invert_kernel(*refs, row_local, date_total, late):
    (
        *chunk_refs, incidence, gain_top, gain_low, weighted_ref, basis_ref, series_ref,
        moments_ref, wide, data, residual, moved,
    ) = refs
    ifg_total, pixel_count = moved.shape[1:]
    date_rows = gain_top.shape[0]
    date_pad = incidence.shape[1] // 2
    late_refs, early_refs = chunk_refs[:late], chunk_refs[late:]
    done = 0
    pieces = []
    if early_refs:
        *early_data, early_series = early_refs
        for ref in early_data:
            count = ref.shape[0]
            used = min(count, (done + count) // 128 * 128 - done) if ref is early_data[-1] else count
            pieces.append((ref, done, used))
            done += used
        data[pl.ds(0, count - used), :] = early_data[-1][pl.ds(used, count - used), :]
        unpack(late_refs, wide, data.at[pl.ds(count - used, ifg_total - done - count + used)], row_local)
    else:
        unpack(late_refs, wide, data, row_local)
    pieces.append((data, done, ifg_total - done))

    def observed(rows):
        parts = []
        for ref, first, count in pieces:
            low, high = max(rows.start, first), min(rows.start + rows.size, first + count)
            if low < high:
                parts.append(ref[pl.ds(low - first, high - low), :])
        return parts[0] if len(parts) == 1 else jnp.concatenate(parts, axis=0)

    coherence = basis_ref[3:4, :]
    date_tiles = [pl.ds(start, date_rows // 2) for start in (0, date_rows // 2)]
    spare = [jnp.zeros((date_pad - date_rows, pixel_count), jnp.bfloat16)]
    ifg_tiles = [pl.ds(start, ROWS_A) for start in range(0, ifg_total, ROWS_A)]
    everything = slice(None)

    def folded(square):
        return jnp.sum(square.reshape(-1, 8, pixel_count), axis=0)

    def reweighted(total, moved):
        scale = jnp.sum(total, axis=0, keepdims=True) / ifg_total + 1e-06
        strength = coherence * (scale * scale)
        for rows in ifg_tiles:
            left = residual[rows, :]
            inverse = pl.reciprocal(left * left + scale, approx=APPROX)
            moved[rows, :] = ((inverse * left) * (inverse * strength)).astype(jnp.bfloat16)

    left_columns = pl.ds(done, ifg_total - done)
    tops, lows = [], []
    for rows in date_tiles:
        part = gained(gain_top, gain_low, rows, left_columns, data[...])
        if early_refs:
            part = part + early_series[rows, :]
        series_ref[rows, :] = part
        top, low = halves(part)
        tops.append(top)
        lows.append(low)
    both = jnp.concatenate(tops + spare + lows + spare, axis=0)
    total = jnp.zeros((8, pixel_count), jnp.float32)
    for rows in ifg_tiles:
        left = observed(rows).astype(jnp.float32) - product(incidence[rows, :], both)
        residual[rows, :] = left
        total = total + folded(left * left)
    reweighted(total, moved.at[0])
    for sweep in range(1, REWEIGHTS):
        steps = []
        for rows in date_tiles:
            part = gained(gain_top, None, rows, everything, moved[sweep - 1])
            steps.append(part.astype(jnp.bfloat16))
            series_ref[rows, :] = series_ref[rows, :] + part
        step = jnp.concatenate(steps + spare, axis=0)
        total = jnp.zeros((8, pixel_count), jnp.float32)
        for rows in ifg_tiles:
            left = residual[rows, :] - product(incidence[rows, :date_pad], step)
            residual[rows, :] = left
            total = total + folded(left * left)
        reweighted(total, moved.at[sweep])
        for rows in date_tiles:
            series_ref[rows, :] = series_ref[rows, :] + product(gain_low[rows, :], moved[sweep - 1])
    for rows in date_tiles:
        part = gained(gain_top, None, rows, everything, moved[REWEIGHTS - 1])
        series_ref[rows, :] = series_ref[rows, :] + part
    series_ref[pl.ds(date_total, 8), :] = basis_ref[...]
    series_top, series_low = halves(series_ref[...])
    weighted_top, weighted_low = halves(weighted_ref[...])
    count = weighted_top.shape[0]
    across = (((1,), (1,)), ((), ()))
    first = product(jnp.concatenate([weighted_top, weighted_low], axis=0), series_top, across)
    moments_ref[...] = first[:count] + (first[count:] + product(weighted_top, series_low, across))


def invert(late_chunks, early, incidence, gains, weighted, basis, row_local, date_total):
    ifg_total = incidence.shape[0]
    kept = sum(value.shape[0] for value in early[:-1]) // 128 * 128
    date_rows = gains[0].shape[0]
    pixel_count = weighted.shape[1]
    return pl.pallas_call(
        functools.partial(
            invert_kernel, row_local=row_local, date_total=date_total, late=len(late_chunks)
        ),
        out_shape=[
            jax.ShapeDtypeStruct((date_rows, pixel_count), jnp.float32),
            jax.ShapeDtypeStruct((weighted.shape[0], date_rows), jnp.float32),
        ],
        scratch_shapes=[
            pltpu.VMEM(late_chunks[0].shape, jnp.float32),
            pltpu.VMEM((ifg_total - kept, pixel_count), jnp.bfloat16),
            pltpu.VMEM((ifg_total, pixel_count), jnp.float32),
            pltpu.VMEM((REWEIGHTS, ifg_total, pixel_count), jnp.bfloat16),
        ],
        compiler_params=pltpu.CompilerParams(vmem_limit_bytes=VMEM_LIMIT),
        name="invert",
    )(*late_chunks, *early, incidence, *gains, weighted, basis)


def cut_kernel(source, *refs):
    *targets, sems = refs
    copies = [
        pltpu.make_async_copy(
            source.at[:, lax.axis_index("stack") ^ mask], target, sems.at[mask]
        )
        for mask, target in enumerate(targets)
    ]
    for copy in copies:
        copy.start()
    for copy in copies:
        copy.wait()


def cut(phases, col_local):
    ifg_local, row_local, col_range = phases.shape
    count = col_range // col_local
    view = phases.reshape(ifg_local, row_local, count, col_local).transpose(0, 2, 1, 3)
    return pl.pallas_call(
        cut_kernel,
        out_shape=[jax.ShapeDtypeStruct((ifg_local, row_local, col_local), phases.dtype)] * count,
        in_specs=[pl.BlockSpec(memory_space=pltpu.HBM)],
        out_specs=[pl.BlockSpec(memory_space=pltpu.VMEM)] * count,
        scratch_shapes=[pltpu.SemaphoreType.DMA((count,))],
        compiler_params=pltpu.CompilerParams(vmem_limit_bytes=8 * 1024 * 1024),
        name="cut",
    )(pltpu.with_memory_space_constraint(view, pltpu.HBM))


def exchange(phases, stack_size):
    ifg_local, row_local, col_range = phases.shape
    col_local = col_range // stack_size
    if stack_size != 8:
        blocks = phases.reshape(ifg_local, row_local, stack_size, col_local).transpose(2, 0, 1, 3)
        stacked = lax.all_to_all(blocks, "stack", split_axis=0, concat_axis=0, tiled=True)
        return [stacked.reshape(-1, col_local)], (0,)
    blocks = cut(phases, col_local)
    found = {0: blocks[0]}

    def send(mask, after=None):
        block = blocks[mask]
        if after is not None:
            block, found[after] = lax.optimization_barrier((block, found[after]))
        found[mask] = lax.ppermute(block, "stack", [(i, i ^ mask) for i in range(stack_size)])

    for mask, after in ((4, None), (5, None), (1, None), (6, None), (2, None), (7, 1), (3, 2)):
        send(mask, after)
    return [found[mask].reshape(-1, col_local) for mask in ARRIVAL], ARRIVAL


def plane_weights(gram_matrix, basis):
    def entry(row_pos, col_pos):
        return gram_matrix[row_pos % 3][col_pos % 3]

    cofactors = [
        [
            entry(row_pos + 1, col_pos + 1) * entry(row_pos + 2, col_pos + 2)
            - entry(row_pos + 1, col_pos + 2) * entry(row_pos + 2, col_pos + 1)
            for col_pos in range(3)
        ]
        for row_pos in range(3)
    ]
    inverse = 1.0 / (
        entry(0, 0) * cofactors[0][0]
        + entry(0, 1) * cofactors[0][1]
        + entry(0, 2) * cofactors[0][2]
    )
    return [
        (cofactors[row_pos][0] * inverse) * basis[0]
        + (cofactors[row_pos][1] * inverse) * basis[1]
        + (cofactors[row_pos][2] * inverse) * basis[2]
        for row_pos in range(3)
    ]


def deramp_kernel(first_ref, *refs, row_local, date_total):
    *others, series_ref, member_ref, out_ref, staged, sems = refs
    totals = first_ref[...]
    for other in others:
        totals = totals + other[...]
    sums = [
        jnp.concatenate([totals[2 * k : 2 * k + 2], totals[8 + 2 * k : 10 + 2 * k]], axis=0)
        for k in range(3)
    ]
    wide = (sums[0].shape[0], member_ref.shape[1])
    gram = [
        [
            jnp.broadcast_to(sums[k][:, date_total + m : date_total + m + 1], wide)
            + (1.0 if k == m else 0.0)
            for m in range(3)
        ]
        for k in range(3)
    ]
    weights = plane_weights(gram, [member_ref[4 * k : 4 * k + 4, :] for k in range(3)])
    spare = 4
    weights_top, weights_low = halves(
        jnp.concatenate(weights + [jnp.zeros((spare, weights[0].shape[1]), jnp.float32)], axis=0)
    )
    sums_top, sums_low = halves(
        jnp.concatenate(sums + [jnp.zeros((spare, sums[0].shape[1]), jnp.float32)], axis=0)
    )
    ramp = product(
        jnp.concatenate([sums_top, sums_low, sums_top], axis=0),
        jnp.concatenate([weights_top, weights_top, weights_low], axis=0),
        (((0,), (0,)), ((), ())),
    )
    col_local = series_ref.shape[1] // row_local
    copies = []
    step = date_total // OUT_PARTS
    for part in range(OUT_PARTS):
        start = part * step
        flat = series_ref[pl.ds(start, step), :] - ramp[start : start + step]
        for row in range(row_local):
            staged[pl.ds(start * row_local + row, step, stride=row_local), :] = flat[
                :, row * col_local : (row + 1) * col_local
            ]
        rows = pl.ds(start * row_local, step * row_local)
        copy = pltpu.make_async_copy(staged.at[rows], out_ref.at[rows], sems.at[part])
        copy.start()
        copies.append(copy)
    for copy in copies:
        copy.wait()


def deramp(parts, series, member, row_local, date_total):
    col_local = series.shape[1] // row_local
    shape = (date_total * row_local, col_local)
    whole = pl.BlockSpec(memory_space=pltpu.VMEM)
    return pl.pallas_call(
        functools.partial(deramp_kernel, row_local=row_local, date_total=date_total),
        out_shape=jax.ShapeDtypeStruct(shape, jnp.float32),
        in_specs=[whole] * (len(parts) + 2),
        out_specs=pl.BlockSpec(memory_space=pl.ANY),
        scratch_shapes=[pltpu.VMEM(shape, jnp.float32), pltpu.SemaphoreType.DMA((OUT_PARTS,))],
        compiler_params=pltpu.CompilerParams(vmem_limit_bytes=VMEM_LIMIT),
        name="deramp",
    )(*parts, series, member)


def swap(value, axes, pairs):
    both = [(i, j) for i, j in pairs] + [(j, i) for i, j in pairs]
    return lax.ppermute(value, axes, both)


def local(phases, ifg_pairs, preconditioner, coherence, geo_tiles):
    stack_size = lax.axis_size("stack")
    range_size = lax.axis_size("range")
    azimuth_size = lax.axis_size("azimuth")
    ifg_local, row_local, col_range = phases.shape
    date_total = preconditioner.shape[0]
    date_rows = -(-(date_total + 8) // 32) * 32
    date_pad = -(-date_rows // LANES) * LANES

    chunks, order = exchange(phases, stack_size)
    incidence, *gains, member, weighted, basis = prepare(
        ifg_pairs.T, preconditioner, coherence, geo_tiles, date_pad, date_rows, order,
        col_range * range_size, row_local * azimuth_size,
    )
    early = []
    if len(chunks) > 1:
        first, second = EARLY
        count = ifg_local * first // 256 * 256
        data_a, series_a = early_fit(chunks[:first], [], gains, row_local, 0, count)
        data_b, series_b = early_fit(
            chunks[first:second], [data_a, series_a], gains, row_local, count,
            ifg_local * second // 128 * 128,
        )
        early = [data_a, data_b, series_b]
        chunks = chunks[second:]

    series, moments = invert(
        chunks, early, incidence, gains, weighted, basis, row_local, date_total
    )

    def place(block):
        return (block % stack_size) * range_size + block // stack_size

    block_count = stack_size * range_size
    inner = [
        (place(block), place(block + 2)) for block in range(block_count - 2) if block // 2 % 2 == 0
    ]
    outer = [
        (place(block), place(block + 2)) for block in range(block_count - 2) if block // 2 % 2 == 1
    ]
    axes = ("stack", "range")
    outer += [(place(0), place(1)), (place(block_count - 2), place(block_count - 1))]
    first = swap(moments[:8], axes, outer)
    node = (lax.axis_index("range") * stack_size + lax.axis_index("stack")) // 2
    first = jnp.where((node > 0) & (node < block_count // 2 - 1), first, 0.0)
    second = swap(moments[8:], axes, inner)
    moments = moments + jnp.concatenate([first, second], axis=0)
    pairs = [(i, i + 1) for i in range(0, stack_size, 2)]
    crossed = [
        (i * azimuth_size + a, (i + 1) * azimuth_size + (azimuth_size - 1 - a))
        for i in range(0, stack_size, 2)
        for a in range(azimuth_size)
    ]
    parts = [
        moments,
        swap(moments, ("stack", "azimuth"), crossed),
        swap(moments, "stack", pairs),
        swap(moments, "azimuth", [(0, 1)]),
    ]
    flat = deramp(parts, series, member, row_local, date_total)
    return flat.reshape(date_total, row_local, -1)


def solution(mesh):
    return jax.shard_map(
        local,
        mesh=mesh,
        in_specs=(
            P("stack", "azimuth", "range"),
            P(),
            P(),
            P("azimuth", ("range", "stack")),
            P("azimuth", ("range", "stack")),
        ),
        out_specs=P(None, "azimuth", ("range", "stack")),
        check_vma=False,
    )
```

```python
import functools

import jax
import jax.numpy as jnp
from jax import lax
from jax.experimental import pallas as pl
from jax.experimental.pallas import tpu as pltpu
from jax.sharding import PartitionSpec as P

REWEIGHTS = 2
LANES = 128
VMEM_LIMIT = 24 * 1024 * 1024
ROWS_A = 192
APPROX = False
ARRIVAL = (0, 7, 1, 6, 2, 5, 3, 4)
EARLY = (4, 6)
OUT_PARTS = 5


def halves(value):
    top = value.astype(jnp.bfloat16)
    return top, (value - top.astype(jnp.float32)).astype(jnp.bfloat16)


def product(left, right, dims=(((1,), (0,)), ((), ()))):
    return lax.dot_general(left, right, dims, preferred_element_type=jnp.float32)


def prepare_kernel(
    prec_hbm, pairs_ref, coherence_ref, tiles_ref, incidence_ref, gain_top, gain_low, member_ref,
    weighted_ref, basis_ref, prec_ref, pairs, sem, *, order, col_total, row_total,
):
    copy = pltpu.make_async_copy(prec_hbm, prec_ref, sem)
    copy.start()
    chunk = pairs_ref.shape[1] // len(order)
    date_total = prec_ref.shape[0]
    ifg_total = gain_top.shape[1]
    date_pad = incidence_ref.shape[1] // 2
    for position, mask in enumerate(order):
        moved = pairs_ref[...]
        if len(order) > 1:
            back = (len(order) - (lax.axis_index("stack") ^ mask)) % len(order)
            moved = pltpu.roll(moved, back * chunk, 1)
        pairs[:, position * chunk : (position + 1) * chunk] = moved[:, :chunk]
    date_ids = lax.broadcasted_iota(jnp.int32, (date_pad, ifg_total), 0)
    incidence_t = (
        jnp.where(date_ids == pairs[1:2, :], 1.0, 0.0)
        - jnp.where(date_ids == pairs[0:1, :], 1.0, 0.0)
    ).astype(jnp.bfloat16)
    copy.wait()
    incidence = incidence_t.T
    incidence_ref[:, :date_pad] = incidence
    incidence_ref[:, date_pad:] = incidence
    prec = prec_ref[...]
    prec = prec - jnp.sum(prec, axis=1, keepdims=True) / date_total
    top, low = halves(prec)
    used = incidence_t[:date_total]
    gain_a, gain_b = halves(product(top, used) + product(low, used))
    zeros = jnp.zeros((gain_top.shape[0] - date_total, ifg_total), jnp.bfloat16)
    gain_top[...] = jnp.concatenate([gain_a, zeros], axis=0)
    gain_low[...] = jnp.concatenate([gain_b, zeros], axis=0)

    row_local, col_local = coherence_ref.shape
    pixel_count = row_local * col_local
    stack_size = lax.axis_size("stack")
    block = lax.axis_index("range") * stack_size + lax.axis_index("stack")
    node = block // 2
    even = node % 2 == 0

    def flat(ref):
        return jnp.concatenate([ref[row : row + 1, :] for row in range(row_local)], axis=1)

    coherence = flat(coherence_ref).astype(jnp.float32)
    tiles = flat(tiles_ref)
    pixel = lax.broadcasted_iota(jnp.int32, (1, pixel_count), 1)
    row = jnp.zeros_like(pixel)
    for step in range(1, row_local):
        row = row + (pixel >= step * col_local).astype(jnp.int32)
    column = block * col_local + (pixel - row * col_local)
    row = row + lax.axis_index("azimuth") * row_local
    coord_u = (row.astype(jnp.float32) + 0.5) / row_total - 0.5
    coord_v = (column.astype(jnp.float32) + 0.5) / col_total - 0.5
    basis = jnp.concatenate([jnp.ones_like(coord_u), coord_u, coord_v], axis=0)
    spare = jnp.zeros((2, pixel_count), jnp.float32)
    lines, inside = [], []
    for base in (jnp.where(even, 2 * node - 1, 2 * node + 1), jnp.where(even, 2 * node + 1, 2 * node - 1)):
        held = [(tiles == base + step).astype(jnp.float32) for step in range(2)]
        for line in range(3):
            lines += [basis[line : line + 1] * each for each in held]
        lines.append(spare)
        inside += held
    weighted_ref[...] = jnp.concatenate(lines, axis=0) * coherence
    member_ref[...] = jnp.concatenate(
        [basis[line : line + 1] * each for line in range(3) for each in inside] + [spare, spare], axis=0
    )
    basis_ref[...] = jnp.concatenate([basis, coherence, jnp.zeros((4, pixel_count), jnp.float32)], axis=0)


def prepare(preconditioner, small, date_pad, date_rows, order, col_total, row_total):
    pairs, coherence, tiles = small
    ifg_total = pairs.shape[1]
    pixel_count = coherence.size
    shapes = [((ifg_total, 2 * date_pad), jnp.bfloat16)]
    shapes += [((date_rows, ifg_total), jnp.bfloat16)] * 2
    shapes += [((rows, pixel_count), jnp.float32) for rows in (16, 16, 8)]
    whole = pl.BlockSpec(memory_space=pltpu.VMEM)
    return pl.pallas_call(
        functools.partial(prepare_kernel, order=order, col_total=col_total, row_total=row_total),
        out_shape=[jax.ShapeDtypeStruct(shape, dtype) for shape, dtype in shapes],
        in_specs=[pl.BlockSpec(memory_space=pltpu.HBM)] + [whole] * 3,
        out_specs=[whole] * 6,
        scratch_shapes=[
            pltpu.VMEM(preconditioner.shape, jnp.float32),
            pltpu.VMEM(pairs.shape, jnp.int32),
            pltpu.SemaphoreType.DMA,
        ],
        compiler_params=pltpu.CompilerParams(vmem_limit_bytes=VMEM_LIMIT),
        name="prepare",
    )(pltpu.with_memory_space_constraint(preconditioner, pltpu.HBM), *small)


def unpack(chunk_refs, wide, data, row_local):
    start = 0
    col_local = chunk_refs[0].shape[1]
    for ref in chunk_refs:
        count = ref.shape[0] // row_local
        wide[pl.ds(0, ref.shape[0]), :] = ref[...].astype(jnp.float32)
        for row in range(row_local):
            data[pl.ds(start, count), row * col_local : (row + 1) * col_local] = wide[
                pl.ds(row, count, stride=row_local), :
            ].astype(jnp.bfloat16)
        start += count


def gained(gain_top, gain_low, rows, columns, value):
    part = product(gain_top[rows, columns], value)
    if gain_low is not None:
        part = part + product(gain_low[rows, columns], value)
    return part


def early_kernel(*refs, row_local, start, end, late):
    *chunk_refs, gain_top, gain_low, data_ref, series_ref, wide = refs
    unpack(chunk_refs[:late], wide, data_ref, row_local)
    before = chunk_refs[late:]
    columns = pl.ds(start, end - start)
    value = data_ref[...]
    if before:
        held = before[0].shape[0] - start
        value = jnp.concatenate([before[0][pl.ds(start, held), :], value[: end - start - held]], axis=0)
    else:
        value = value[:end]
    half = series_ref.shape[0] // 2
    for first in (0, half):
        rows = pl.ds(first, half)
        part = gained(gain_top, gain_low, rows, columns, value)
        series_ref[rows, :] = part + before[1][rows, :] if before else part


def early_fit(chunks, before, gains, row_local, start, end):
    count = sum(chunk.shape[0] for chunk in chunks) // row_local
    pixel_count = chunks[0].shape[1] * row_local
    return pl.pallas_call(
        functools.partial(
            early_kernel, row_local=row_local, start=start, end=end, late=len(chunks)
        ),
        out_shape=[
            jax.ShapeDtypeStruct((count, pixel_count), jnp.bfloat16),
            jax.ShapeDtypeStruct((gains[0].shape[0], pixel_count), jnp.float32),
        ],
        scratch_shapes=[pltpu.VMEM(chunks[0].shape, jnp.float32)],
        compiler_params=pltpu.CompilerParams(vmem_limit_bytes=VMEM_LIMIT),
        name="early_fit",
    )(*chunks, *before, *gains)


def invert_kernel(*refs, row_local, date_total, late):
    (
        *chunk_refs, incidence, gain_top, gain_low, weighted_ref, basis_ref, series_ref,
        moments_ref, wide, data, residual, moved,
    ) = refs
    ifg_total, pixel_count = moved.shape[1:]
    date_rows = gain_top.shape[0]
    date_pad = incidence.shape[1] // 2
    late_refs, early_refs = chunk_refs[:late], chunk_refs[late:]
    done = 0
    pieces = []
    if early_refs:
        *early_data, early_series = early_refs
        for ref in early_data:
            count = ref.shape[0]
            used = min(count, (done + count) // 128 * 128 - done) if ref is early_data[-1] else count
            pieces.append((ref, done, used))
            done += used
        data[pl.ds(0, count - used), :] = early_data[-1][pl.ds(used, count - used), :]
        unpack(late_refs, wide, data.at[pl.ds(count - used, ifg_total - done - count + used)], row_local)
    else:
        unpack(late_refs, wide, data, row_local)
    pieces.append((data, done, ifg_total - done))

    def observed(rows):
        parts = []
        for ref, first, count in pieces:
            low, high = max(rows.start, first), min(rows.start + rows.size, first + count)
            if low < high:
                parts.append(ref[pl.ds(low - first, high - low), :])
        return parts[0] if len(parts) == 1 else jnp.concatenate(parts, axis=0)

    coherence = basis_ref[3:4, :]
    date_tiles = [pl.ds(start, date_rows // 2) for start in (0, date_rows // 2)]
    spare = [jnp.zeros((date_pad - date_rows, pixel_count), jnp.bfloat16)]
    ifg_tiles = [pl.ds(start, ROWS_A) for start in range(0, ifg_total, ROWS_A)]
    everything = slice(None)

    def folded(square):
        return jnp.sum(square.reshape(-1, 8, pixel_count), axis=0)

    def reweighted(total, moved):
        scale = jnp.sum(total, axis=0, keepdims=True) / ifg_total + 1e-06
        strength = coherence * (scale * scale)
        for rows in ifg_tiles:
            left = residual[rows, :]
            inverse = pl.reciprocal(left * left + scale, approx=APPROX)
            moved[rows, :] = ((inverse * left) * (inverse * strength)).astype(jnp.bfloat16)

    left_columns = pl.ds(done, ifg_total - done)
    tops, lows = [], []
    for rows in date_tiles:
        part = gained(gain_top, gain_low, rows, left_columns, data[...])
        if early_refs:
            part = part + early_series[rows, :]
        series_ref[rows, :] = part
        top, low = halves(part)
        tops.append(top)
        lows.append(low)
    both = jnp.concatenate(tops + spare + lows + spare, axis=0)
    total = jnp.zeros((8, pixel_count), jnp.float32)
    for rows in ifg_tiles:
        left = observed(rows).astype(jnp.float32) - product(incidence[rows, :], both)
        residual[rows, :] = left
        total = total + folded(left * left)
    reweighted(total, moved.at[0])
    for sweep in range(1, REWEIGHTS):
        steps = []
        for rows in date_tiles:
            part = gained(gain_top, None, rows, everything, moved[sweep - 1])
            steps.append(part.astype(jnp.bfloat16))
            series_ref[rows, :] = series_ref[rows, :] + part
        step = jnp.concatenate(steps + spare, axis=0)
        total = jnp.zeros((8, pixel_count), jnp.float32)
        for rows in ifg_tiles:
            left = residual[rows, :] - product(incidence[rows, :date_pad], step)
            residual[rows, :] = left
            total = total + folded(left * left)
        reweighted(total, moved.at[sweep])
        for rows in date_tiles:
            series_ref[rows, :] = series_ref[rows, :] + product(gain_low[rows, :], moved[sweep - 1])
    for rows in date_tiles:
        part = gained(gain_top, None, rows, everything, moved[REWEIGHTS - 1])
        series_ref[rows, :] = series_ref[rows, :] + part
    series_ref[pl.ds(date_total, 8), :] = basis_ref[...]
    series_top, series_low = halves(series_ref[...])
    weighted_top, weighted_low = halves(weighted_ref[...])
    count = weighted_top.shape[0]
    across = (((1,), (1,)), ((), ()))
    first = product(jnp.concatenate([weighted_top, weighted_low], axis=0), series_top, across)
    moments_ref[...] = first[:count] + (first[count:] + product(weighted_top, series_low, across))


def invert(late_chunks, early, incidence, gains, weighted, basis, row_local, date_total):
    ifg_total = incidence.shape[0]
    kept = sum(value.shape[0] for value in early[:-1]) // 128 * 128
    date_rows = gains[0].shape[0]
    pixel_count = weighted.shape[1]
    return pl.pallas_call(
        functools.partial(
            invert_kernel, row_local=row_local, date_total=date_total, late=len(late_chunks)
        ),
        out_shape=[
            jax.ShapeDtypeStruct((date_rows, pixel_count), jnp.float32),
            jax.ShapeDtypeStruct((weighted.shape[0], date_rows), jnp.float32),
        ],
        scratch_shapes=[
            pltpu.VMEM(late_chunks[0].shape, jnp.float32),
            pltpu.VMEM((ifg_total - kept, pixel_count), jnp.bfloat16),
            pltpu.VMEM((ifg_total, pixel_count), jnp.float32),
            pltpu.VMEM((REWEIGHTS, ifg_total, pixel_count), jnp.bfloat16),
        ],
        compiler_params=pltpu.CompilerParams(vmem_limit_bytes=VMEM_LIMIT),
        name="invert",
    )(*late_chunks, *early, incidence, *gains, weighted, basis)


def cut_kernel(source, *refs):
    sems = refs[-1]
    extra = len(refs) - 1 - source.shape[1]
    extra //= 2
    small, targets, fetched = refs[:extra], refs[extra:-1 - extra], refs[-1 - extra : -1]
    place = lax.axis_index("stack")
    copies = [
        pltpu.make_async_copy(source.at[:, place ^ mask], target, sems.at[mask])
        for mask, target in enumerate(targets)
    ]
    copies += [
        pltpu.make_async_copy(value, target, sems.at[len(targets) + index])
        for index, (value, target) in enumerate(zip(small, fetched))
    ]
    for copy in copies:
        copy.start()
    for copy in copies:
        copy.wait()


def cut(phases, col_local, small):
    ifg_local, row_local, col_range = phases.shape
    count = col_range // col_local
    view = phases.reshape(ifg_local, row_local, count, col_local).transpose(0, 2, 1, 3)
    shapes = [jax.ShapeDtypeStruct((ifg_local, row_local, col_local), phases.dtype)] * count
    shapes += [jax.ShapeDtypeStruct(value.shape, value.dtype) for value in small]
    arguments = (view, *small)
    results = pl.pallas_call(
        cut_kernel,
        out_shape=shapes,
        in_specs=[pl.BlockSpec(memory_space=pltpu.HBM)] * len(arguments),
        out_specs=[pl.BlockSpec(memory_space=pltpu.VMEM)] * len(shapes),
        scratch_shapes=[pltpu.SemaphoreType.DMA((len(shapes),))],
        compiler_params=pltpu.CompilerParams(vmem_limit_bytes=8 * 1024 * 1024),
        name="cut",
    )(*(pltpu.with_memory_space_constraint(value, pltpu.HBM) for value in arguments))
    return results[:count], results[count:]


def exchange(phases, small, stack_size):
    ifg_local, row_local, col_range = phases.shape
    col_local = col_range // stack_size
    if stack_size != 8:
        blocks = phases.reshape(ifg_local, row_local, stack_size, col_local).transpose(2, 0, 1, 3)
        stacked = lax.all_to_all(blocks, "stack", split_axis=0, concat_axis=0, tiled=True)
        return [stacked.reshape(-1, col_local)], small, (0,)
    blocks, small = cut(phases, col_local, small)
    found = {0: blocks[0]}

    for mask in ARRIVAL[1:]:
        pairs = [(i, i ^ mask) for i in range(stack_size)]
        found[mask] = lax.ppermute(blocks[mask], "stack", pairs)
    return [found[mask].reshape(-1, col_local) for mask in ARRIVAL], small, ARRIVAL


def plane_weights(gram_matrix, basis):
    def entry(row_pos, col_pos):
        return gram_matrix[row_pos % 3][col_pos % 3]

    cofactors = [
        [
            entry(row_pos + 1, col_pos + 1) * entry(row_pos + 2, col_pos + 2)
            - entry(row_pos + 1, col_pos + 2) * entry(row_pos + 2, col_pos + 1)
            for col_pos in range(3)
        ]
        for row_pos in range(3)
    ]
    inverse = 1.0 / (
        entry(0, 0) * cofactors[0][0]
        + entry(0, 1) * cofactors[0][1]
        + entry(0, 2) * cofactors[0][2]
    )
    return [
        (cofactors[row_pos][0] * inverse) * basis[0]
        + (cofactors[row_pos][1] * inverse) * basis[1]
        + (cofactors[row_pos][2] * inverse) * basis[2]
        for row_pos in range(3)
    ]


def deramp_kernel(first_ref, *refs, row_local, date_total):
    *others, series_ref, member_ref, out_ref, staged, sems = refs
    totals = first_ref[...]
    for other in others:
        totals = totals + other[...]
    sums = [
        jnp.concatenate([totals[2 * k : 2 * k + 2], totals[8 + 2 * k : 10 + 2 * k]], axis=0)
        for k in range(3)
    ]
    wide = (sums[0].shape[0], member_ref.shape[1])
    gram = [
        [
            jnp.broadcast_to(sums[k][:, date_total + m : date_total + m + 1], wide)
            + (1.0 if k == m else 0.0)
            for m in range(3)
        ]
        for k in range(3)
    ]
    weights = plane_weights(gram, [member_ref[4 * k : 4 * k + 4, :] for k in range(3)])
    spare = 4
    weights_top, weights_low = halves(
        jnp.concatenate(weights + [jnp.zeros((spare, weights[0].shape[1]), jnp.float32)], axis=0)
    )
    sums_top, sums_low = halves(
        jnp.concatenate(sums + [jnp.zeros((spare, sums[0].shape[1]), jnp.float32)], axis=0)
    )
    ramp = product(
        jnp.concatenate([sums_top, sums_low, sums_top], axis=0),
        jnp.concatenate([weights_top, weights_top, weights_low], axis=0),
        (((0,), (0,)), ((), ())),
    )
    col_local = series_ref.shape[1] // row_local
    copies = []
    step = date_total // OUT_PARTS
    for part in range(OUT_PARTS):
        start = part * step
        flat = series_ref[pl.ds(start, step), :] - ramp[start : start + step]
        for row in range(row_local):
            staged[pl.ds(start * row_local + row, step, stride=row_local), :] = flat[
                :, row * col_local : (row + 1) * col_local
            ]
        rows = pl.ds(start * row_local, step * row_local)
        copy = pltpu.make_async_copy(staged.at[rows], out_ref.at[rows], sems.at[part])
        copy.start()
        copies.append(copy)
    for copy in copies:
        copy.wait()


def deramp(parts, series, member, row_local, date_total):
    col_local = series.shape[1] // row_local
    shape = (date_total * row_local, col_local)
    whole = pl.BlockSpec(memory_space=pltpu.VMEM)
    return pl.pallas_call(
        functools.partial(deramp_kernel, row_local=row_local, date_total=date_total),
        out_shape=jax.ShapeDtypeStruct(shape, jnp.float32),
        in_specs=[whole] * (len(parts) + 2),
        out_specs=pl.BlockSpec(memory_space=pl.ANY),
        scratch_shapes=[pltpu.VMEM(shape, jnp.float32), pltpu.SemaphoreType.DMA((OUT_PARTS,))],
        compiler_params=pltpu.CompilerParams(vmem_limit_bytes=VMEM_LIMIT),
        name="deramp",
    )(*parts, series, member)


def swap(value, axes, pairs):
    both = [(i, j) for i, j in pairs] + [(j, i) for i, j in pairs]
    return lax.ppermute(value, axes, both)


def local(phases, ifg_pairs, preconditioner, coherence, geo_tiles):
    stack_size = lax.axis_size("stack")
    range_size = lax.axis_size("range")
    azimuth_size = lax.axis_size("azimuth")
    ifg_local, row_local, col_range = phases.shape
    date_total = preconditioner.shape[0]
    date_rows = -(-(date_total + 8) // 32) * 32
    date_pad = -(-date_rows // LANES) * LANES

    small = (ifg_pairs.T, coherence, geo_tiles)
    chunks, small, order = exchange(phases, small, stack_size)
    incidence, *gains, member, weighted, basis = prepare(
        preconditioner, small, date_pad, date_rows, order,
        col_range * range_size, row_local * azimuth_size,
    )
    early = []
    if len(chunks) > 1:
        first, second = EARLY
        count = ifg_local * first // 256 * 256
        data_a, series_a = early_fit(chunks[:first], [], gains, row_local, 0, count)
        data_b, series_b = early_fit(
            chunks[first:second], [data_a, series_a], gains, row_local, count,
            ifg_local * second // 128 * 128,
        )
        early = [data_a, data_b, series_b]
        chunks = chunks[second:]

    series, moments = invert(
        chunks, early, incidence, gains, weighted, basis, row_local, date_total
    )

    def place(block):
        return (block % stack_size) * range_size + block // stack_size

    block_count = stack_size * range_size
    inner = [
        (place(block), place(block + 2)) for block in range(block_count - 2) if block // 2 % 2 == 0
    ]
    outer = [
        (place(block), place(block + 2)) for block in range(block_count - 2) if block // 2 % 2 == 1
    ]
    axes = ("stack", "range")
    outer += [(place(0), place(1)), (place(block_count - 2), place(block_count - 1))]
    first = swap(moments[:8], axes, outer)
    node = (lax.axis_index("range") * stack_size + lax.axis_index("stack")) // 2
    first = jnp.where((node > 0) & (node < block_count // 2 - 1), first, 0.0)
    second = swap(moments[8:], axes, inner)
    moments = moments + jnp.concatenate([first, second], axis=0)
    pairs = [(i, i + 1) for i in range(0, stack_size, 2)]
    crossed = [
        (i * azimuth_size + a, (i + 1) * azimuth_size + (azimuth_size - 1 - a))
        for i in range(0, stack_size, 2)
        for a in range(azimuth_size)
    ]
    parts = [
        moments,
        swap(moments, ("stack", "azimuth"), crossed),
        swap(moments, "stack", pairs),
        swap(moments, "azimuth", [(0, 1)]),
    ]
    flat = deramp(parts, series, member, row_local, date_total)
    return flat.reshape(date_total, row_local, -1)


def solution(mesh):
    return jax.shard_map(
        local,
        mesh=mesh,
        in_specs=(
            P("stack", "azimuth", "range"),
            P(),
            P(),
            P("azimuth", ("range", "stack")),
            P("azimuth", ("range", "stack")),
        ),
        out_specs=P(None, "azimuth", ("range", "stack")),
        check_vma=False,
    )
```

```python
import functools

import jax
import jax.numpy as jnp
from jax import lax
from jax.experimental import pallas as pl
from jax.experimental.pallas import tpu as pltpu
from jax.sharding import PartitionSpec as P

REWEIGHTS = 2
LANES = 128
VMEM_LIMIT = 24 * 1024 * 1024
ROWS_A = 192
APPROX = False
ARRIVAL = (0, 7, 1, 6, 2, 5, 3, 4)
EARLY = (4, 6)
OUT_PARTS = 5


def halves(value):
    top = value.astype(jnp.bfloat16)
    return top, (value - top.astype(jnp.float32)).astype(jnp.bfloat16)


def product(left, right, dims=(((1,), (0,)), ((), ()))):
    return lax.dot_general(left, right, dims, preferred_element_type=jnp.float32)


def prepare_kernel(
    prec_hbm, pairs_ref, coherence_ref, tiles_ref, incidence_ref, gain_top, gain_low, member_ref,
    weighted_ref, basis_ref, prec_ref, pairs, sem, *, order, col_total, row_total,
):
    copy = pltpu.make_async_copy(prec_hbm, prec_ref, sem)
    copy.start()
    chunk = pairs_ref.shape[1] // len(order)
    date_total = prec_ref.shape[0]
    ifg_total = gain_top.shape[1]
    date_pad = incidence_ref.shape[1] // 2
    for position, mask in enumerate(order):
        moved = pairs_ref[...]
        if len(order) > 1:
            back = (len(order) - (lax.axis_index("stack") ^ mask)) % len(order)
            moved = pltpu.roll(moved, back * chunk, 1)
        pairs[:, position * chunk : (position + 1) * chunk] = moved[:, :chunk]
    date_ids = lax.broadcasted_iota(jnp.int32, (date_pad, ifg_total), 0)
    incidence_t = (
        jnp.where(date_ids == pairs[1:2, :], 1.0, 0.0)
        - jnp.where(date_ids == pairs[0:1, :], 1.0, 0.0)
    ).astype(jnp.bfloat16)
    copy.wait()
    incidence = incidence_t.T
    incidence_ref[:, :date_pad] = incidence
    incidence_ref[:, date_pad:] = incidence
    prec = prec_ref[...]
    prec = prec - jnp.sum(prec, axis=1, keepdims=True) / date_total
    top, low = halves(prec)
    pad = jnp.zeros((date_total, date_pad - date_total), jnp.bfloat16)
    gain_a, gain_b = halves(
        product(
            jnp.concatenate([top, pad, low, pad], axis=1),
            jnp.concatenate([incidence_t, incidence_t], axis=0),
        )
    )
    zeros = jnp.zeros((gain_top.shape[0] - date_total, ifg_total), jnp.bfloat16)
    gain_top[...] = jnp.concatenate([gain_a, zeros], axis=0)
    gain_low[...] = jnp.concatenate([gain_b, zeros], axis=0)

    row_local, col_local = coherence_ref.shape
    pixel_count = row_local * col_local
    stack_size = lax.axis_size("stack")
    block = lax.axis_index("range") * stack_size + lax.axis_index("stack")
    node = block // 2
    even = node % 2 == 0

    def flat(ref):
        return jnp.concatenate([ref[row : row + 1, :] for row in range(row_local)], axis=1)

    coherence = flat(coherence_ref).astype(jnp.float32)
    tiles = flat(tiles_ref)
    pixel = lax.broadcasted_iota(jnp.int32, (1, pixel_count), 1)
    row = jnp.zeros_like(pixel)
    for step in range(1, row_local):
        row = row + (pixel >= step * col_local).astype(jnp.int32)
    column = block * col_local + (pixel - row * col_local)
    row = row + lax.axis_index("azimuth") * row_local
    coord_u = (row.astype(jnp.float32) + 0.5) / row_total - 0.5
    coord_v = (column.astype(jnp.float32) + 0.5) / col_total - 0.5
    basis = jnp.concatenate([jnp.ones_like(coord_u), coord_u, coord_v], axis=0)
    spare = jnp.zeros((2, pixel_count), jnp.float32)
    lines, inside = [], []
    for base in (jnp.where(even, 2 * node - 1, 2 * node + 1), jnp.where(even, 2 * node + 1, 2 * node - 1)):
        held = [(tiles == base + step).astype(jnp.float32) for step in range(2)]
        for line in range(3):
            lines += [basis[line : line + 1] * each for each in held]
        lines.append(spare)
        inside += held
    weighted_ref[...] = jnp.concatenate(lines, axis=0) * coherence
    member_ref[...] = jnp.concatenate(
        [basis[line : line + 1] * each for line in range(3) for each in inside] + [spare, spare], axis=0
    )
    basis_ref[...] = jnp.concatenate([basis, coherence, jnp.zeros((4, pixel_count), jnp.float32)], axis=0)


def prepare(preconditioner, small, date_pad, date_rows, order, col_total, row_total):
    pairs, coherence, tiles = small
    ifg_total = pairs.shape[1]
    pixel_count = coherence.size
    shapes = [((ifg_total, 2 * date_pad), jnp.bfloat16)]
    shapes += [((date_rows, ifg_total), jnp.bfloat16)] * 2
    shapes += [((rows, pixel_count), jnp.float32) for rows in (16, 16, 8)]
    whole = pl.BlockSpec(memory_space=pltpu.VMEM)
    return pl.pallas_call(
        functools.partial(prepare_kernel, order=order, col_total=col_total, row_total=row_total),
        out_shape=[jax.ShapeDtypeStruct(shape, dtype) for shape, dtype in shapes],
        in_specs=[pl.BlockSpec(memory_space=pltpu.HBM)] + [whole] * 3,
        out_specs=[whole] * 6,
        scratch_shapes=[
            pltpu.VMEM(preconditioner.shape, jnp.float32),
            pltpu.VMEM(pairs.shape, jnp.int32),
            pltpu.SemaphoreType.DMA,
        ],
        compiler_params=pltpu.CompilerParams(vmem_limit_bytes=VMEM_LIMIT),
        name="prepare",
    )(pltpu.with_memory_space_constraint(preconditioner, pltpu.HBM), *small)


def unpack(chunk_refs, wide, data, row_local):
    start = 0
    col_local = chunk_refs[0].shape[1]
    for ref in chunk_refs:
        count = ref.shape[0] // row_local
        wide[pl.ds(0, ref.shape[0]), :] = ref[...].astype(jnp.float32)
        for row in range(row_local):
            data[pl.ds(start, count), row * col_local : (row + 1) * col_local] = wide[
                pl.ds(row, count, stride=row_local), :
            ].astype(jnp.bfloat16)
        start += count


def gained(gain_top, gain_low, rows, columns, value):
    part = product(gain_top[rows, columns], value)
    if gain_low is not None:
        part = part + product(gain_low[rows, columns], value)
    return part


def early_kernel(*refs, row_local, start, end, late):
    *chunk_refs, gain_top, gain_low, data_ref, series_ref, wide = refs
    unpack(chunk_refs[:late], wide, data_ref, row_local)
    before = chunk_refs[late:]
    columns = pl.ds(start, end - start)
    value = data_ref[...]
    if before:
        held = before[0].shape[0] - start
        value = jnp.concatenate([before[0][pl.ds(start, held), :], value[: end - start - held]], axis=0)
    else:
        value = value[:end]
    half = series_ref.shape[0] // 2
    for first in (0, half):
        rows = pl.ds(first, half)
        part = gained(gain_top, gain_low, rows, columns, value)
        series_ref[rows, :] = part + before[1][rows, :] if before else part


def early_fit(chunks, before, gains, row_local, start, end):
    count = sum(chunk.shape[0] for chunk in chunks) // row_local
    pixel_count = chunks[0].shape[1] * row_local
    return pl.pallas_call(
        functools.partial(
            early_kernel, row_local=row_local, start=start, end=end, late=len(chunks)
        ),
        out_shape=[
            jax.ShapeDtypeStruct((count, pixel_count), jnp.bfloat16),
            jax.ShapeDtypeStruct((gains[0].shape[0], pixel_count), jnp.float32),
        ],
        scratch_shapes=[pltpu.VMEM(chunks[0].shape, jnp.float32)],
        compiler_params=pltpu.CompilerParams(vmem_limit_bytes=VMEM_LIMIT),
        name="early_fit",
    )(*chunks, *before, *gains)


def invert_kernel(*refs, row_local, date_total, late):
    (
        *chunk_refs, incidence, gain_top, gain_low, weighted_ref, basis_ref, series_ref,
        moments_ref, wide, data, residual, moved,
    ) = refs
    ifg_total, pixel_count = moved.shape[1:]
    date_rows = gain_top.shape[0]
    date_pad = incidence.shape[1] // 2
    late_refs, early_refs = chunk_refs[:late], chunk_refs[late:]
    done = 0
    pieces = []
    if early_refs:
        *early_data, early_series = early_refs
        for ref in early_data:
            count = ref.shape[0]
            used = min(count, (done + count) // 128 * 128 - done) if ref is early_data[-1] else count
            pieces.append((ref, done, used))
            done += used
        data[pl.ds(0, count - used), :] = early_data[-1][pl.ds(used, count - used), :]
        unpack(late_refs, wide, data.at[pl.ds(count - used, ifg_total - done - count + used)], row_local)
    else:
        unpack(late_refs, wide, data, row_local)
    pieces.append((data, done, ifg_total - done))

    def observed(rows):
        parts = []
        for ref, first, count in pieces:
            low, high = max(rows.start, first), min(rows.start + rows.size, first + count)
            if low < high:
                parts.append(ref[pl.ds(low - first, high - low), :])
        return parts[0] if len(parts) == 1 else jnp.concatenate(parts, axis=0)

    coherence = basis_ref[3:4, :]
    date_tiles = [pl.ds(start, date_rows // 2) for start in (0, date_rows // 2)]
    spare = [jnp.zeros((date_pad - date_rows, pixel_count), jnp.bfloat16)]
    ifg_tiles = [pl.ds(start, ROWS_A) for start in range(0, ifg_total, ROWS_A)]
    everything = slice(None)

    def folded(square):
        return jnp.sum(square.reshape(-1, 8, pixel_count), axis=0)

    def reweighted(total, moved):
        scale = jnp.sum(total, axis=0, keepdims=True) / ifg_total + 1e-06
        strength = coherence * (scale * scale)
        for rows in ifg_tiles:
            left = residual[rows, :]
            inverse = pl.reciprocal(left * left + scale, approx=APPROX)
            moved[rows, :] = ((inverse * left) * (inverse * strength)).astype(jnp.bfloat16)

    left_columns = pl.ds(done, ifg_total - done)
    tops, lows = [], []
    for rows in date_tiles:
        part = gained(gain_top, gain_low, rows, left_columns, data[...])
        if early_refs:
            part = part + early_series[rows, :]
        series_ref[rows, :] = part
        top, low = halves(part)
        tops.append(top)
        lows.append(low)
    both = jnp.concatenate(tops + spare + lows + spare, axis=0)
    total = jnp.zeros((8, pixel_count), jnp.float32)
    for rows in ifg_tiles:
        left = observed(rows).astype(jnp.float32) - product(incidence[rows, :], both)
        residual[rows, :] = left
        total = total + folded(left * left)
    reweighted(total, moved.at[0])
    for sweep in range(1, REWEIGHTS):
        steps = []
        for rows in date_tiles:
            part = gained(gain_top, None, rows, everything, moved[sweep - 1])
            steps.append(part.astype(jnp.bfloat16))
            series_ref[rows, :] = series_ref[rows, :] + part
        step = jnp.concatenate(steps + spare, axis=0)
        total = jnp.zeros((8, pixel_count), jnp.float32)
        for rows in ifg_tiles:
            left = residual[rows, :] - product(incidence[rows, :date_pad], step)
            residual[rows, :] = left
            total = total + folded(left * left)
        reweighted(total, moved.at[sweep])
        for rows in date_tiles:
            series_ref[rows, :] = series_ref[rows, :] + product(gain_low[rows, :], moved[sweep - 1])
    for rows in date_tiles:
        part = gained(gain_top, None, rows, everything, moved[REWEIGHTS - 1])
        series_ref[rows, :] = series_ref[rows, :] + part
    series_ref[pl.ds(date_total, 8), :] = basis_ref[...]
    series_top, series_low = halves(series_ref[...])
    weighted_top, weighted_low = halves(weighted_ref[...])
    count = weighted_top.shape[0]
    across = (((1,), (1,)), ((), ()))
    first = product(jnp.concatenate([weighted_top, weighted_low], axis=0), series_top, across)
    moments_ref[...] = first[:count] + (first[count:] + product(weighted_top, series_low, across))


def invert(late_chunks, early, incidence, gains, weighted, basis, row_local, date_total):
    ifg_total = incidence.shape[0]
    kept = sum(value.shape[0] for value in early[:-1]) // 128 * 128
    date_rows = gains[0].shape[0]
    pixel_count = weighted.shape[1]
    return pl.pallas_call(
        functools.partial(
            invert_kernel, row_local=row_local, date_total=date_total, late=len(late_chunks)
        ),
        out_shape=[
            jax.ShapeDtypeStruct((date_rows, pixel_count), jnp.float32),
            jax.ShapeDtypeStruct((weighted.shape[0], date_rows), jnp.float32),
        ],
        scratch_shapes=[
            pltpu.VMEM(late_chunks[0].shape, jnp.float32),
            pltpu.VMEM((ifg_total - kept, pixel_count), jnp.bfloat16),
            pltpu.VMEM((ifg_total, pixel_count), jnp.float32),
            pltpu.VMEM((REWEIGHTS, ifg_total, pixel_count), jnp.bfloat16),
        ],
        compiler_params=pltpu.CompilerParams(vmem_limit_bytes=VMEM_LIMIT),
        name="invert",
    )(*late_chunks, *early, incidence, *gains, weighted, basis)


def cut_kernel(source, *refs):
    sems = refs[-1]
    extra = len(refs) - 1 - source.shape[1]
    extra //= 2
    small, targets, fetched = refs[:extra], refs[extra:-1 - extra], refs[-1 - extra : -1]
    place = lax.axis_index("stack")
    copies = [
        pltpu.make_async_copy(source.at[:, place ^ mask], target, sems.at[mask])
        for mask, target in enumerate(targets)
    ]
    copies += [
        pltpu.make_async_copy(value, target, sems.at[len(targets) + index])
        for index, (value, target) in enumerate(zip(small, fetched))
    ]
    for copy in copies:
        copy.start()
    for copy in copies:
        copy.wait()


def cut(phases, col_local, small):
    ifg_local, row_local, col_range = phases.shape
    count = col_range // col_local
    view = phases.reshape(ifg_local, row_local, count, col_local).transpose(0, 2, 1, 3)
    shapes = [jax.ShapeDtypeStruct((ifg_local, row_local, col_local), phases.dtype)] * count
    shapes += [jax.ShapeDtypeStruct(value.shape, value.dtype) for value in small]
    arguments = (view, *small)
    results = pl.pallas_call(
        cut_kernel,
        out_shape=shapes,
        in_specs=[pl.BlockSpec(memory_space=pltpu.HBM)] * len(arguments),
        out_specs=[pl.BlockSpec(memory_space=pltpu.VMEM)] * len(shapes),
        scratch_shapes=[pltpu.SemaphoreType.DMA((len(shapes),))],
        compiler_params=pltpu.CompilerParams(vmem_limit_bytes=8 * 1024 * 1024),
        name="cut",
    )(*(pltpu.with_memory_space_constraint(value, pltpu.HBM) for value in arguments))
    return results[:count], results[count:]


def exchange(phases, small, stack_size):
    ifg_local, row_local, col_range = phases.shape
    col_local = col_range // stack_size
    if stack_size != 8:
        blocks = phases.reshape(ifg_local, row_local, stack_size, col_local).transpose(2, 0, 1, 3)
        stacked = lax.all_to_all(blocks, "stack", split_axis=0, concat_axis=0, tiled=True)
        return [stacked.reshape(-1, col_local)], small, (0,)
    blocks, small = cut(phases, col_local, small)
    found = {0: blocks[0]}

    for mask in ARRIVAL[1:]:
        pairs = [(i, i ^ mask) for i in range(stack_size)]
        found[mask] = lax.ppermute(blocks[mask], "stack", pairs)
    return [found[mask].reshape(-1, col_local) for mask in ARRIVAL], small, ARRIVAL


def plane_weights(gram_matrix, basis):
    def entry(row_pos, col_pos):
        return gram_matrix[row_pos % 3][col_pos % 3]

    cofactors = [
        [
            entry(row_pos + 1, col_pos + 1) * entry(row_pos + 2, col_pos + 2)
            - entry(row_pos + 1, col_pos + 2) * entry(row_pos + 2, col_pos + 1)
            for col_pos in range(3)
        ]
        for row_pos in range(3)
    ]
    inverse = 1.0 / (
        entry(0, 0) * cofactors[0][0]
        + entry(0, 1) * cofactors[0][1]
        + entry(0, 2) * cofactors[0][2]
    )
    return [
        (cofactors[row_pos][0] * inverse) * basis[0]
        + (cofactors[row_pos][1] * inverse) * basis[1]
        + (cofactors[row_pos][2] * inverse) * basis[2]
        for row_pos in range(3)
    ]


def deramp_kernel(first_ref, *refs, row_local, date_total):
    *others, series_ref, member_ref, out_ref, staged, sems = refs
    totals = first_ref[...]
    for other in others:
        totals = totals + other[...]
    sums = [
        jnp.concatenate([totals[2 * k : 2 * k + 2], totals[8 + 2 * k : 10 + 2 * k]], axis=0)
        for k in range(3)
    ]
    wide = (sums[0].shape[0], member_ref.shape[1])
    gram = [
        [
            jnp.broadcast_to(sums[k][:, date_total + m : date_total + m + 1], wide)
            + (1.0 if k == m else 0.0)
            for m in range(3)
        ]
        for k in range(3)
    ]
    weights = plane_weights(gram, [member_ref[4 * k : 4 * k + 4, :] for k in range(3)])
    spare = 4
    weights_top, weights_low = halves(
        jnp.concatenate(weights + [jnp.zeros((spare, weights[0].shape[1]), jnp.float32)], axis=0)
    )
    sums_top, sums_low = halves(
        jnp.concatenate(sums + [jnp.zeros((spare, sums[0].shape[1]), jnp.float32)], axis=0)
    )
    ramp = product(
        jnp.concatenate([sums_top, sums_low, sums_top], axis=0),
        jnp.concatenate([weights_top, weights_top, weights_low], axis=0),
        (((0,), (0,)), ((), ())),
    )
    col_local = series_ref.shape[1] // row_local
    copies = []
    step = date_total // OUT_PARTS
    for part in range(OUT_PARTS):
        start = part * step
        flat = series_ref[pl.ds(start, step), :] - ramp[start : start + step]
        for row in range(row_local):
            staged[pl.ds(start * row_local + row, step, stride=row_local), :] = flat[
                :, row * col_local : (row + 1) * col_local
            ]
        rows = pl.ds(start * row_local, step * row_local)
        copy = pltpu.make_async_copy(staged.at[rows], out_ref.at[rows], sems.at[part])
        copy.start()
        copies.append(copy)
    for copy in copies:
        copy.wait()


def deramp(parts, series, member, row_local, date_total):
    col_local = series.shape[1] // row_local
    shape = (date_total * row_local, col_local)
    whole = pl.BlockSpec(memory_space=pltpu.VMEM)
    return pl.pallas_call(
        functools.partial(deramp_kernel, row_local=row_local, date_total=date_total),
        out_shape=jax.ShapeDtypeStruct(shape, jnp.float32),
        in_specs=[whole] * (len(parts) + 2),
        out_specs=pl.BlockSpec(memory_space=pl.ANY),
        scratch_shapes=[pltpu.VMEM(shape, jnp.float32), pltpu.SemaphoreType.DMA((OUT_PARTS,))],
        compiler_params=pltpu.CompilerParams(vmem_limit_bytes=VMEM_LIMIT),
        name="deramp",
    )(*parts, series, member)


def swap(value, axes, pairs):
    both = [(i, j) for i, j in pairs] + [(j, i) for i, j in pairs]
    return lax.ppermute(value, axes, both)


def local(phases, ifg_pairs, preconditioner, coherence, geo_tiles):
    stack_size = lax.axis_size("stack")
    range_size = lax.axis_size("range")
    azimuth_size = lax.axis_size("azimuth")
    ifg_local, row_local, col_range = phases.shape
    date_total = preconditioner.shape[0]
    date_rows = -(-(date_total + 8) // 32) * 32
    date_pad = -(-date_rows // LANES) * LANES

    small = (ifg_pairs.T, coherence, geo_tiles)
    chunks, small, order = exchange(phases, small, stack_size)
    incidence, *gains, member, weighted, basis = prepare(
        preconditioner, small, date_pad, date_rows, order,
        col_range * range_size, row_local * azimuth_size,
    )
    early = []
    if len(chunks) > 1:
        first, second = EARLY
        count = ifg_local * first // 256 * 256
        data_a, series_a = early_fit(chunks[:first], [], gains, row_local, 0, count)
        data_b, series_b = early_fit(
            chunks[first:second], [data_a, series_a], gains, row_local, count,
            ifg_local * second // 128 * 128,
        )
        early = [data_a, data_b, series_b]
        chunks = chunks[second:]

    series, moments = invert(
        chunks, early, incidence, gains, weighted, basis, row_local, date_total
    )

    def place(block):
        return (block % stack_size) * range_size + block // stack_size

    block_count = stack_size * range_size
    inner = [
        (place(block), place(block + 2)) for block in range(block_count - 2) if block // 2 % 2 == 0
    ]
    outer = [
        (place(block), place(block + 2)) for block in range(block_count - 2) if block // 2 % 2 == 1
    ]
    axes = ("stack", "range")
    outer += [(place(0), place(1)), (place(block_count - 2), place(block_count - 1))]
    first = swap(moments[:8], axes, outer)
    node = (lax.axis_index("range") * stack_size + lax.axis_index("stack")) // 2
    first = jnp.where((node > 0) & (node < block_count // 2 - 1), first, 0.0)
    second = swap(moments[8:], axes, inner)
    moments = moments + jnp.concatenate([first, second], axis=0)
    pairs = [(i, i + 1) for i in range(0, stack_size, 2)]
    crossed = [
        (i * azimuth_size + a, (i + 1) * azimuth_size + (azimuth_size - 1 - a))
        for i in range(0, stack_size, 2)
        for a in range(azimuth_size)
    ]
    parts = [
        moments,
        swap(moments, ("stack", "azimuth"), crossed),
        swap(moments, "stack", pairs),
        swap(moments, "azimuth", [(0, 1)]),
    ]
    flat = deramp(parts, series, member, row_local, date_total)
    return flat.reshape(date_total, row_local, -1)


def solution(mesh):
    return jax.shard_map(
        local,
        mesh=mesh,
        in_specs=(
            P("stack", "azimuth", "range"),
            P(),
            P(),
            P("azimuth", ("range", "stack")),
            P("azimuth", ("range", "stack")),
        ),
        out_specs=P(None, "azimuth", ("range", "stack")),
        check_vma=False,
    )
```

```python
import functools

import jax
import jax.numpy as jnp
from jax import lax
from jax.experimental import pallas as pl
from jax.experimental.pallas import tpu as pltpu
from jax.sharding import PartitionSpec as P

REWEIGHTS = 2
LANES = 128
VMEM_LIMIT = 24 * 1024 * 1024
ROWS_A = 192
APPROX = False
ARRIVAL = (0, 7, 1, 6, 2, 5, 3, 4)
EARLY = (4, 6)
OUT_PARTS = 5


def halves(value):
    top = value.astype(jnp.bfloat16)
    return top, (value - top.astype(jnp.float32)).astype(jnp.bfloat16)


def product(left, right, dims=(((1,), (0,)), ((), ()))):
    return lax.dot_general(left, right, dims, preferred_element_type=jnp.float32)


def prepare_kernel(
    prec_hbm, pairs_ref, coherence_ref, tiles_ref, incidence_ref, gain_top, gain_low, member_ref,
    weighted_ref, basis_ref, prec_ref, pairs, sem, *, order, col_total, row_total,
):
    copy = pltpu.make_async_copy(prec_hbm, prec_ref, sem)
    copy.start()
    chunk = pairs_ref.shape[1] // len(order)
    date_total = prec_ref.shape[0]
    ifg_total = gain_top.shape[1]
    date_pad = incidence_ref.shape[1] // 2
    for position, mask in enumerate(order):
        moved = pairs_ref[...]
        if len(order) > 1:
            back = (len(order) - (lax.axis_index("stack") ^ mask)) % len(order)
            moved = pltpu.roll(moved, back * chunk, 1)
        pairs[:, position * chunk : (position + 1) * chunk] = moved[:, :chunk]
    date_ids = lax.broadcasted_iota(jnp.int32, (date_pad, ifg_total), 0)
    incidence_t = (
        jnp.where(date_ids == pairs[1:2, :], 1.0, 0.0)
        - jnp.where(date_ids == pairs[0:1, :], 1.0, 0.0)
    ).astype(jnp.bfloat16)
    copy.wait()
    incidence = incidence_t.T
    incidence_ref[:, :date_pad] = incidence
    incidence_ref[:, date_pad:] = incidence
    prec = prec_ref[...]
    prec = prec - jnp.sum(prec, axis=1, keepdims=True) / date_total
    top, low = halves(prec)
    pad = jnp.zeros((date_total, date_pad - date_total), jnp.bfloat16)
    gain_a, gain_b = halves(
        product(
            jnp.concatenate([top, pad, low, pad], axis=1),
            jnp.concatenate([incidence_t, incidence_t], axis=0),
        )
    )
    zeros = jnp.zeros((gain_top.shape[0] - date_total, ifg_total), jnp.bfloat16)
    gain_top[...] = jnp.concatenate([gain_a, zeros], axis=0)
    gain_low[...] = jnp.concatenate([gain_b, zeros], axis=0)

    row_local, col_local = coherence_ref.shape
    pixel_count = row_local * col_local
    stack_size = lax.axis_size("stack")
    block = lax.axis_index("range") * stack_size + lax.axis_index("stack")
    node = block // 2
    even = node % 2 == 0

    def flat(ref):
        return jnp.concatenate([ref[row : row + 1, :] for row in range(row_local)], axis=1)

    coherence = flat(coherence_ref).astype(jnp.float32)
    tiles = flat(tiles_ref)
    pixel = lax.broadcasted_iota(jnp.int32, (1, pixel_count), 1)
    row = jnp.zeros_like(pixel)
    for step in range(1, row_local):
        row = row + (pixel >= step * col_local).astype(jnp.int32)
    column = block * col_local + (pixel - row * col_local)
    row = row + lax.axis_index("azimuth") * row_local
    coord_u = (row.astype(jnp.float32) + 0.5) / row_total - 0.5
    coord_v = (column.astype(jnp.float32) + 0.5) / col_total - 0.5
    basis = jnp.concatenate([jnp.ones_like(coord_u), coord_u, coord_v], axis=0)
    spare = jnp.zeros((2, pixel_count), jnp.float32)
    lines, inside = [], []
    for base in (jnp.where(even, 2 * node - 1, 2 * node + 1), jnp.where(even, 2 * node + 1, 2 * node - 1)):
        held = [(tiles == base + step).astype(jnp.float32) for step in range(2)]
        for line in range(3):
            lines += [basis[line : line + 1] * each for each in held]
        lines.append(spare)
        inside += held
    weighted_ref[...] = jnp.concatenate(lines, axis=0) * coherence
    member_ref[...] = jnp.concatenate(
        [basis[line : line + 1] * each for line in range(3) for each in inside] + [spare, spare], axis=0
    )
    basis_ref[...] = jnp.concatenate([basis, coherence, jnp.zeros((4, pixel_count), jnp.float32)], axis=0)


def prepare(preconditioner, small, date_pad, date_rows, order, col_total, row_total):
    pairs, coherence, tiles = small
    ifg_total = pairs.shape[1]
    pixel_count = coherence.size
    shapes = [((ifg_total, 2 * date_pad), jnp.bfloat16)]
    shapes += [((date_rows, ifg_total), jnp.bfloat16)] * 2
    shapes += [((rows, pixel_count), jnp.float32) for rows in (16, 16, 8)]
    whole = pl.BlockSpec(memory_space=pltpu.VMEM)
    return pl.pallas_call(
        functools.partial(prepare_kernel, order=order, col_total=col_total, row_total=row_total),
        out_shape=[jax.ShapeDtypeStruct(shape, dtype) for shape, dtype in shapes],
        in_specs=[pl.BlockSpec(memory_space=pltpu.HBM)] + [whole] * 3,
        out_specs=[whole] * 6,
        scratch_shapes=[
            pltpu.VMEM(preconditioner.shape, jnp.float32),
            pltpu.VMEM(pairs.shape, jnp.int32),
            pltpu.SemaphoreType.DMA,
        ],
        compiler_params=pltpu.CompilerParams(vmem_limit_bytes=VMEM_LIMIT),
        name="prepare",
    )(pltpu.with_memory_space_constraint(preconditioner, pltpu.HBM), *small)


def unpack(chunk_refs, wide, data, row_local):
    start = 0
    col_local = chunk_refs[0].shape[1]
    for ref in chunk_refs:
        count = ref.shape[0] // row_local
        wide[pl.ds(0, ref.shape[0]), :] = ref[...].astype(jnp.float32)
        for row in range(row_local):
            data[pl.ds(start, count), row * col_local : (row + 1) * col_local] = wide[
                pl.ds(row, count, stride=row_local), :
            ].astype(jnp.bfloat16)
        start += count


def gained(gain_top, gain_low, rows, columns, value):
    part = product(gain_top[rows, columns], value)
    if gain_low is not None:
        part = part + product(gain_low[rows, columns], value)
    return part


def early_kernel(*refs, row_local, start, end, late):
    *chunk_refs, gain_top, gain_low, data_ref, series_ref, wide = refs
    unpack(chunk_refs[:late], wide, data_ref, row_local)
    before = chunk_refs[late:]
    columns = pl.ds(start, end - start)
    value = data_ref[...]
    if before:
        held = before[0].shape[0] - start
        value = jnp.concatenate([before[0][pl.ds(start, held), :], value[: end - start - held]], axis=0)
    else:
        value = value[:end]
    half = series_ref.shape[0] // 2
    for first in (0, half):
        rows = pl.ds(first, half)
        part = gained(gain_top, gain_low, rows, columns, value)
        series_ref[rows, :] = part + before[1][rows, :] if before else part


def early_fit(chunks, before, gains, row_local, start, end):
    count = sum(chunk.shape[0] for chunk in chunks) // row_local
    pixel_count = chunks[0].shape[1] * row_local
    return pl.pallas_call(
        functools.partial(
            early_kernel, row_local=row_local, start=start, end=end, late=len(chunks)
        ),
        out_shape=[
            jax.ShapeDtypeStruct((count, pixel_count), jnp.bfloat16),
            jax.ShapeDtypeStruct((gains[0].shape[0], pixel_count), jnp.float32),
        ],
        scratch_shapes=[pltpu.VMEM(chunks[0].shape, jnp.float32)],
        compiler_params=pltpu.CompilerParams(vmem_limit_bytes=VMEM_LIMIT),
        name="early_fit",
    )(*chunks, *before, *gains)


def invert_kernel(*refs, row_local, date_total, late):
    (
        *chunk_refs, incidence, gain_top, gain_low, weighted_ref, basis_ref, series_ref,
        moments_ref, wide, data, residual, moved,
    ) = refs
    ifg_total, pixel_count = moved.shape[1:]
    date_rows = gain_top.shape[0]
    date_pad = incidence.shape[1] // 2
    late_refs, early_refs = chunk_refs[:late], chunk_refs[late:]
    done = 0
    pieces = []
    if early_refs:
        *early_data, early_series = early_refs
        for ref in early_data:
            count = ref.shape[0]
            used = min(count, (done + count) // 128 * 128 - done) if ref is early_data[-1] else count
            pieces.append((ref, done, used))
            done += used
        data[pl.ds(0, count - used), :] = early_data[-1][pl.ds(used, count - used), :]
        unpack(late_refs, wide, data.at[pl.ds(count - used, ifg_total - done - count + used)], row_local)
    else:
        unpack(late_refs, wide, data, row_local)
    pieces.append((data, done, ifg_total - done))

    def observed(rows):
        parts = []
        for ref, first, count in pieces:
            low, high = max(rows.start, first), min(rows.start + rows.size, first + count)
            if low < high:
                parts.append(ref[pl.ds(low - first, high - low), :])
        return parts[0] if len(parts) == 1 else jnp.concatenate(parts, axis=0)

    coherence = basis_ref[3:4, :]
    date_tiles = [pl.ds(start, date_rows // 2) for start in (0, date_rows // 2)]
    spare = [jnp.zeros((date_pad - date_rows, pixel_count), jnp.bfloat16)]
    ifg_tiles = [pl.ds(start, ROWS_A) for start in range(0, ifg_total, ROWS_A)]
    everything = slice(None)

    def folded(square):
        return jnp.sum(square.reshape(-1, 8, pixel_count), axis=0)

    def reweighted(total, moved):
        scale = jnp.sum(total, axis=0, keepdims=True) / ifg_total + 1e-06
        strength = coherence * (scale * scale)
        for rows in ifg_tiles:
            left = residual[rows, :]
            inverse = pl.reciprocal(left * left + scale, approx=APPROX)
            moved[rows, :] = ((inverse * left) * (inverse * strength)).astype(jnp.bfloat16)

    left_columns = pl.ds(done, ifg_total - done)
    twice = jnp.concatenate([data[...], data[...]], axis=0)
    tops, lows = [], []
    for rows in date_tiles:
        parts = [gain_top[rows, left_columns], gain_low[rows, left_columns]]
        part = product(jnp.concatenate(parts, axis=1), twice)
        if early_refs:
            part = part + early_series[rows, :]
        series_ref[rows, :] = part
        top, low = halves(part)
        tops.append(top)
        lows.append(low)
    both = jnp.concatenate(tops + spare + lows + spare, axis=0)
    total = jnp.zeros((8, pixel_count), jnp.float32)
    for rows in ifg_tiles:
        left = observed(rows).astype(jnp.float32) - product(incidence[rows, :], both)
        residual[rows, :] = left
        total = total + folded(left * left)
    reweighted(total, moved.at[0])
    for sweep in range(1, REWEIGHTS):
        steps = []
        for rows in date_tiles:
            part = gained(gain_top, None, rows, everything, moved[sweep - 1])
            steps.append(part.astype(jnp.bfloat16))
            series_ref[rows, :] = series_ref[rows, :] + part
        step = jnp.concatenate(steps + spare, axis=0)
        total = jnp.zeros((8, pixel_count), jnp.float32)
        for rows in ifg_tiles:
            left = residual[rows, :] - product(incidence[rows, :date_pad], step)
            residual[rows, :] = left
            total = total + folded(left * left)
        reweighted(total, moved.at[sweep])
        for rows in date_tiles:
            series_ref[rows, :] = series_ref[rows, :] + product(gain_low[rows, :], moved[sweep - 1])
    for rows in date_tiles:
        part = gained(gain_top, None, rows, everything, moved[REWEIGHTS - 1])
        series_ref[rows, :] = series_ref[rows, :] + part
    series_ref[pl.ds(date_total, 8), :] = basis_ref[...]
    series_top, series_low = halves(series_ref[...])
    weighted_top, weighted_low = halves(weighted_ref[...])
    count = weighted_top.shape[0]
    across = (((1,), (1,)), ((), ()))
    first = product(jnp.concatenate([weighted_top, weighted_low], axis=0), series_top, across)
    moments_ref[...] = first[:count] + (first[count:] + product(weighted_top, series_low, across))


def invert(late_chunks, early, incidence, gains, weighted, basis, row_local, date_total):
    ifg_total = incidence.shape[0]
    kept = sum(value.shape[0] for value in early[:-1]) // 128 * 128
    date_rows = gains[0].shape[0]
    pixel_count = weighted.shape[1]
    return pl.pallas_call(
        functools.partial(
            invert_kernel, row_local=row_local, date_total=date_total, late=len(late_chunks)
        ),
        out_shape=[
            jax.ShapeDtypeStruct((date_rows, pixel_count), jnp.float32),
            jax.ShapeDtypeStruct((weighted.shape[0], date_rows), jnp.float32),
        ],
        scratch_shapes=[
            pltpu.VMEM(late_chunks[0].shape, jnp.float32),
            pltpu.VMEM((ifg_total - kept, pixel_count), jnp.bfloat16),
            pltpu.VMEM((ifg_total, pixel_count), jnp.float32),
            pltpu.VMEM((REWEIGHTS, ifg_total, pixel_count), jnp.bfloat16),
        ],
        compiler_params=pltpu.CompilerParams(vmem_limit_bytes=VMEM_LIMIT),
        name="invert",
    )(*late_chunks, *early, incidence, *gains, weighted, basis)


def cut_kernel(source, *refs):
    sems = refs[-1]
    extra = len(refs) - 1 - source.shape[1]
    extra //= 2
    small, targets, fetched = refs[:extra], refs[extra:-1 - extra], refs[-1 - extra : -1]
    place = lax.axis_index("stack")
    copies = [
        pltpu.make_async_copy(source.at[:, place ^ mask], target, sems.at[mask])
        for mask, target in enumerate(targets)
    ]
    copies += [
        pltpu.make_async_copy(value, target, sems.at[len(targets) + index])
        for index, (value, target) in enumerate(zip(small, fetched))
    ]
    for copy in copies:
        copy.start()
    for copy in copies:
        copy.wait()


def cut(phases, col_local, small):
    ifg_local, row_local, col_range = phases.shape
    count = col_range // col_local
    view = phases.reshape(ifg_local, row_local, count, col_local).transpose(0, 2, 1, 3)
    shapes = [jax.ShapeDtypeStruct((ifg_local, row_local, col_local), phases.dtype)] * count
    shapes += [jax.ShapeDtypeStruct(value.shape, value.dtype) for value in small]
    arguments = (view, *small)
    results = pl.pallas_call(
        cut_kernel,
        out_shape=shapes,
        in_specs=[pl.BlockSpec(memory_space=pltpu.HBM)] * len(arguments),
        out_specs=[pl.BlockSpec(memory_space=pltpu.VMEM)] * len(shapes),
        scratch_shapes=[pltpu.SemaphoreType.DMA((len(shapes),))],
        compiler_params=pltpu.CompilerParams(vmem_limit_bytes=8 * 1024 * 1024),
        name="cut",
    )(*(pltpu.with_memory_space_constraint(value, pltpu.HBM) for value in arguments))
    return results[:count], results[count:]


def exchange(phases, small, stack_size):
    ifg_local, row_local, col_range = phases.shape
    col_local = col_range // stack_size
    if stack_size != 8:
        blocks = phases.reshape(ifg_local, row_local, stack_size, col_local).transpose(2, 0, 1, 3)
        stacked = lax.all_to_all(blocks, "stack", split_axis=0, concat_axis=0, tiled=True)
        return [stacked.reshape(-1, col_local)], small, (0,)
    blocks, small = cut(phases, col_local, small)
    found = {0: blocks[0]}

    for mask in ARRIVAL[1:]:
        pairs = [(i, i ^ mask) for i in range(stack_size)]
        found[mask] = lax.ppermute(blocks[mask], "stack", pairs)
    return [found[mask].reshape(-1, col_local) for mask in ARRIVAL], small, ARRIVAL


def plane_weights(gram_matrix, basis):
    def entry(row_pos, col_pos):
        return gram_matrix[row_pos % 3][col_pos % 3]

    cofactors = [
        [
            entry(row_pos + 1, col_pos + 1) * entry(row_pos + 2, col_pos + 2)
            - entry(row_pos + 1, col_pos + 2) * entry(row_pos + 2, col_pos + 1)
            for col_pos in range(3)
        ]
        for row_pos in range(3)
    ]
    inverse = 1.0 / (
        entry(0, 0) * cofactors[0][0]
        + entry(0, 1) * cofactors[0][1]
        + entry(0, 2) * cofactors[0][2]
    )
    return [
        (cofactors[row_pos][0] * inverse) * basis[0]
        + (cofactors[row_pos][1] * inverse) * basis[1]
        + (cofactors[row_pos][2] * inverse) * basis[2]
        for row_pos in range(3)
    ]


def deramp_kernel(first_ref, *refs, row_local, date_total):
    *others, series_ref, member_ref, out_ref, staged, sems = refs
    totals = first_ref[...]
    for other in others:
        totals = totals + other[...]
    sums = [
        jnp.concatenate([totals[2 * k : 2 * k + 2], totals[8 + 2 * k : 10 + 2 * k]], axis=0)
        for k in range(3)
    ]
    wide = (sums[0].shape[0], member_ref.shape[1])
    gram = [
        [
            jnp.broadcast_to(sums[k][:, date_total + m : date_total + m + 1], wide)
            + (1.0 if k == m else 0.0)
            for m in range(3)
        ]
        for k in range(3)
    ]
    weights = plane_weights(gram, [member_ref[4 * k : 4 * k + 4, :] for k in range(3)])
    spare = 4
    weights_top, weights_low = halves(
        jnp.concatenate(weights + [jnp.zeros((spare, weights[0].shape[1]), jnp.float32)], axis=0)
    )
    sums_top, sums_low = halves(
        jnp.concatenate(sums + [jnp.zeros((spare, sums[0].shape[1]), jnp.float32)], axis=0)
    )
    ramp = product(
        jnp.concatenate([sums_top, sums_low, sums_top], axis=0),
        jnp.concatenate([weights_top, weights_top, weights_low], axis=0),
        (((0,), (0,)), ((), ())),
    )
    col_local = series_ref.shape[1] // row_local
    copies = []
    step = date_total // OUT_PARTS
    for part in range(OUT_PARTS):
        start = part * step
        flat = series_ref[pl.ds(start, step), :] - ramp[start : start + step]
        for row in range(row_local):
            staged[pl.ds(start * row_local + row, step, stride=row_local), :] = flat[
                :, row * col_local : (row + 1) * col_local
            ]
        rows = pl.ds(start * row_local, step * row_local)
        copy = pltpu.make_async_copy(staged.at[rows], out_ref.at[rows], sems.at[part])
        copy.start()
        copies.append(copy)
    for copy in copies:
        copy.wait()


def deramp(parts, series, member, row_local, date_total):
    col_local = series.shape[1] // row_local
    shape = (date_total * row_local, col_local)
    whole = pl.BlockSpec(memory_space=pltpu.VMEM)
    return pl.pallas_call(
        functools.partial(deramp_kernel, row_local=row_local, date_total=date_total),
        out_shape=jax.ShapeDtypeStruct(shape, jnp.float32),
        in_specs=[whole] * (len(parts) + 2),
        out_specs=pl.BlockSpec(memory_space=pl.ANY),
        scratch_shapes=[pltpu.VMEM(shape, jnp.float32), pltpu.SemaphoreType.DMA((OUT_PARTS,))],
        compiler_params=pltpu.CompilerParams(vmem_limit_bytes=VMEM_LIMIT),
        name="deramp",
    )(*parts, series, member)


def swap(value, axes, pairs):
    both = [(i, j) for i, j in pairs] + [(j, i) for i, j in pairs]
    return lax.ppermute(value, axes, both)


def local(phases, ifg_pairs, preconditioner, coherence, geo_tiles):
    stack_size = lax.axis_size("stack")
    range_size = lax.axis_size("range")
    azimuth_size = lax.axis_size("azimuth")
    ifg_local, row_local, col_range = phases.shape
    date_total = preconditioner.shape[0]
    date_rows = -(-(date_total + 8) // 32) * 32
    date_pad = -(-date_rows // LANES) * LANES

    small = (ifg_pairs.T, coherence, geo_tiles)
    chunks, small, order = exchange(phases, small, stack_size)
    incidence, *gains, member, weighted, basis = prepare(
        preconditioner, small, date_pad, date_rows, order,
        col_range * range_size, row_local * azimuth_size,
    )
    early = []
    if len(chunks) > 1:
        first, second = EARLY
        count = ifg_local * first // 256 * 256
        data_a, series_a = early_fit(chunks[:first], [], gains, row_local, 0, count)
        data_b, series_b = early_fit(
            chunks[first:second], [data_a, series_a], gains, row_local, count,
            ifg_local * second // 128 * 128,
        )
        early = [data_a, data_b, series_b]
        chunks = chunks[second:]

    series, moments = invert(
        chunks, early, incidence, gains, weighted, basis, row_local, date_total
    )

    def place(block):
        return (block % stack_size) * range_size + block // stack_size

    block_count = stack_size * range_size
    inner = [
        (place(block), place(block + 2)) for block in range(block_count - 2) if block // 2 % 2 == 0
    ]
    outer = [
        (place(block), place(block + 2)) for block in range(block_count - 2) if block // 2 % 2 == 1
    ]
    axes = ("stack", "range")
    outer += [(place(0), place(1)), (place(block_count - 2), place(block_count - 1))]
    first = swap(moments[:8], axes, outer)
    node = (lax.axis_index("range") * stack_size + lax.axis_index("stack")) // 2
    first = jnp.where((node > 0) & (node < block_count // 2 - 1), first, 0.0)
    second = swap(moments[8:], axes, inner)
    moments = moments + jnp.concatenate([first, second], axis=0)
    pairs = [(i, i + 1) for i in range(0, stack_size, 2)]
    crossed = [
        (i * azimuth_size + a, (i + 1) * azimuth_size + (azimuth_size - 1 - a))
        for i in range(0, stack_size, 2)
        for a in range(azimuth_size)
    ]
    parts = [
        moments,
        swap(moments, ("stack", "azimuth"), crossed),
        swap(moments, "stack", pairs),
        swap(moments, "azimuth", [(0, 1)]),
    ]
    flat = deramp(parts, series, member, row_local, date_total)
    return flat.reshape(date_total, row_local, -1)


def solution(mesh):
    return jax.shard_map(
        local,
        mesh=mesh,
        in_specs=(
            P("stack", "azimuth", "range"),
            P(),
            P(),
            P("azimuth", ("range", "stack")),
            P("azimuth", ("range", "stack")),
        ),
        out_specs=P(None, "azimuth", ("range", "stack")),
        check_vma=False,
    )
```

```python
import functools

import jax
import jax.numpy as jnp
from jax import lax
from jax.experimental import pallas as pl
from jax.experimental.pallas import tpu as pltpu
from jax.sharding import PartitionSpec as P

REWEIGHTS = 2
LANES = 128
VMEM_LIMIT = 24 * 1024 * 1024
ROWS_A = 192
APPROX = False
ARRIVAL = (0, 7, 1, 6, 2, 5, 3, 4)
EARLY = (4, 7)
OUT_PARTS = 5


def halves(value):
    top = value.astype(jnp.bfloat16)
    return top, (value - top.astype(jnp.float32)).astype(jnp.bfloat16)


def product(left, right, dims=(((1,), (0,)), ((), ()))):
    return lax.dot_general(left, right, dims, preferred_element_type=jnp.float32)


def prepare_kernel(
    prec_hbm, pairs_ref, coherence_ref, tiles_ref, incidence_ref, gain_top, gain_low, member_ref,
    weighted_ref, basis_ref, prec_ref, pairs, sem, *, order, col_total, row_total,
):
    copy = pltpu.make_async_copy(prec_hbm, prec_ref, sem)
    copy.start()
    chunk = pairs_ref.shape[1] // len(order)
    date_total = prec_ref.shape[0]
    ifg_total = gain_top.shape[1]
    date_pad = incidence_ref.shape[1] // 2
    for position, mask in enumerate(order):
        moved = pairs_ref[...]
        if len(order) > 1:
            back = (len(order) - (lax.axis_index("stack") ^ mask)) % len(order)
            moved = pltpu.roll(moved, back * chunk, 1)
        pairs[:, position * chunk : (position + 1) * chunk] = moved[:, :chunk]
    date_ids = lax.broadcasted_iota(jnp.int32, (date_pad, ifg_total), 0)
    incidence_t = (
        jnp.where(date_ids == pairs[1:2, :], 1.0, 0.0)
        - jnp.where(date_ids == pairs[0:1, :], 1.0, 0.0)
    ).astype(jnp.bfloat16)
    copy.wait()
    incidence = incidence_t.T
    incidence_ref[:, :date_pad] = incidence
    incidence_ref[:, date_pad:] = incidence
    prec = prec_ref[...]
    prec = prec - jnp.sum(prec, axis=1, keepdims=True) / date_total
    top, low = halves(prec)
    pad = jnp.zeros((date_total, date_pad - date_total), jnp.bfloat16)
    gain_a, gain_b = halves(
        product(
            jnp.concatenate([top, pad, low, pad], axis=1),
            jnp.concatenate([incidence_t, incidence_t], axis=0),
        )
    )
    zeros = jnp.zeros((gain_top.shape[0] - date_total, ifg_total), jnp.bfloat16)
    gain_top[...] = jnp.concatenate([gain_a, zeros], axis=0)
    gain_low[...] = jnp.concatenate([gain_b, zeros], axis=0)

    row_local, col_local = coherence_ref.shape
    pixel_count = row_local * col_local
    stack_size = lax.axis_size("stack")
    block = lax.axis_index("range") * stack_size + lax.axis_index("stack")
    node = block // 2
    even = node % 2 == 0

    def flat(ref):
        return jnp.concatenate([ref[row : row + 1, :] for row in range(row_local)], axis=1)

    coherence = flat(coherence_ref).astype(jnp.float32)
    tiles = flat(tiles_ref)
    pixel = lax.broadcasted_iota(jnp.int32, (1, pixel_count), 1)
    row = jnp.zeros_like(pixel)
    for step in range(1, row_local):
        row = row + (pixel >= step * col_local).astype(jnp.int32)
    column = block * col_local + (pixel - row * col_local)
    row = row + lax.axis_index("azimuth") * row_local
    coord_u = (row.astype(jnp.float32) + 0.5) / row_total - 0.5
    coord_v = (column.astype(jnp.float32) + 0.5) / col_total - 0.5
    basis = jnp.concatenate([jnp.ones_like(coord_u), coord_u, coord_v], axis=0)
    spare = jnp.zeros((2, pixel_count), jnp.float32)
    lines, inside = [], []
    for base in (jnp.where(even, 2 * node - 1, 2 * node + 1), jnp.where(even, 2 * node + 1, 2 * node - 1)):
        held = [(tiles == base + step).astype(jnp.float32) for step in range(2)]
        for line in range(3):
            lines += [basis[line : line + 1] * each for each in held]
        lines.append(spare)
        inside += held
    weighted_ref[...] = jnp.concatenate(lines, axis=0) * coherence
    member_ref[...] = jnp.concatenate(
        [basis[line : line + 1] * each for line in range(3) for each in inside] + [spare, spare], axis=0
    )
    basis_ref[...] = jnp.concatenate([basis, coherence, jnp.zeros((4, pixel_count), jnp.float32)], axis=0)


def prepare(preconditioner, small, date_pad, date_rows, order, col_total, row_total):
    pairs, coherence, tiles = small
    ifg_total = pairs.shape[1]
    pixel_count = coherence.size
    shapes = [((ifg_total, 2 * date_pad), jnp.bfloat16)]
    shapes += [((date_rows, ifg_total), jnp.bfloat16)] * 2
    shapes += [((rows, pixel_count), jnp.float32) for rows in (16, 16, 8)]
    whole = pl.BlockSpec(memory_space=pltpu.VMEM)
    return pl.pallas_call(
        functools.partial(prepare_kernel, order=order, col_total=col_total, row_total=row_total),
        out_shape=[jax.ShapeDtypeStruct(shape, dtype) for shape, dtype in shapes],
        in_specs=[pl.BlockSpec(memory_space=pltpu.HBM)] + [whole] * 3,
        out_specs=[whole] * 6,
        scratch_shapes=[
            pltpu.VMEM(preconditioner.shape, jnp.float32),
            pltpu.VMEM(pairs.shape, jnp.int32),
            pltpu.SemaphoreType.DMA,
        ],
        compiler_params=pltpu.CompilerParams(vmem_limit_bytes=VMEM_LIMIT),
        name="prepare",
    )(pltpu.with_memory_space_constraint(preconditioner, pltpu.HBM), *small)


def unpack(chunk_refs, wide, data, row_local):
    start = 0
    col_local = chunk_refs[0].shape[1]
    for ref in chunk_refs:
        count = ref.shape[0] // row_local
        wide[pl.ds(0, ref.shape[0]), :] = ref[...].astype(jnp.float32)
        for row in range(row_local):
            data[pl.ds(start, count), row * col_local : (row + 1) * col_local] = wide[
                pl.ds(row, count, stride=row_local), :
            ].astype(jnp.bfloat16)
        start += count


def gained(gain_top, gain_low, rows, columns, value):
    part = product(gain_top[rows, columns], value)
    if gain_low is not None:
        part = part + product(gain_low[rows, columns], value)
    return part


def early_kernel(*refs, row_local, start, end, late):
    *chunk_refs, gain_top, gain_low, data_ref, series_ref, wide = refs
    unpack(chunk_refs[:late], wide, data_ref, row_local)
    before = chunk_refs[late:]
    columns = pl.ds(start, end - start)
    value = data_ref[...]
    if before:
        held = before[0].shape[0] - start
        value = jnp.concatenate([before[0][pl.ds(start, held), :], value[: end - start - held]], axis=0)
    else:
        value = value[:end]
    half = series_ref.shape[0] // 2
    for first in (0, half):
        rows = pl.ds(first, half)
        part = gained(gain_top, gain_low, rows, columns, value)
        series_ref[rows, :] = part + before[1][rows, :] if before else part


def early_fit(chunks, before, gains, row_local, start, end):
    count = sum(chunk.shape[0] for chunk in chunks) // row_local
    pixel_count = chunks[0].shape[1] * row_local
    return pl.pallas_call(
        functools.partial(
            early_kernel, row_local=row_local, start=start, end=end, late=len(chunks)
        ),
        out_shape=[
            jax.ShapeDtypeStruct((count, pixel_count), jnp.bfloat16),
            jax.ShapeDtypeStruct((gains[0].shape[0], pixel_count), jnp.float32),
        ],
        scratch_shapes=[pltpu.VMEM(chunks[0].shape, jnp.float32)],
        compiler_params=pltpu.CompilerParams(vmem_limit_bytes=VMEM_LIMIT),
        name="early_fit",
    )(*chunks, *before, *gains)


def invert_kernel(*refs, row_local, date_total, late):
    (
        *chunk_refs, incidence, gain_top, gain_low, weighted_ref, basis_ref, series_ref,
        moments_ref, wide, data, residual, moved,
    ) = refs
    ifg_total, pixel_count = moved.shape[1:]
    date_rows = gain_top.shape[0]
    date_pad = incidence.shape[1] // 2
    late_refs, early_refs = chunk_refs[:late], chunk_refs[late:]
    done = 0
    pieces = []
    if early_refs:
        *early_data, early_series = early_refs
        for ref in early_data:
            count = ref.shape[0]
            used = min(count, (done + count) // 128 * 128 - done) if ref is early_data[-1] else count
            pieces.append((ref, done, used))
            done += used
        data[pl.ds(0, count - used), :] = early_data[-1][pl.ds(used, count - used), :]
        unpack(late_refs, wide, data.at[pl.ds(count - used, ifg_total - done - count + used)], row_local)
    else:
        unpack(late_refs, wide, data, row_local)
    pieces.append((data, done, ifg_total - done))

    def observed(rows):
        parts = []
        for ref, first, count in pieces:
            low, high = max(rows.start, first), min(rows.start + rows.size, first + count)
            if low < high:
                parts.append(ref[pl.ds(low - first, high - low), :])
        return parts[0] if len(parts) == 1 else jnp.concatenate(parts, axis=0)

    coherence = basis_ref[3:4, :]
    date_tiles = [pl.ds(start, date_rows // 2) for start in (0, date_rows // 2)]
    spare = [jnp.zeros((date_pad - date_rows, pixel_count), jnp.bfloat16)]
    ifg_tiles = [pl.ds(start, ROWS_A) for start in range(0, ifg_total, ROWS_A)]
    everything = slice(None)

    def folded(square):
        return jnp.sum(square.reshape(-1, 8, pixel_count), axis=0)

    def reweighted(total, moved):
        scale = jnp.sum(total, axis=0, keepdims=True) / ifg_total + 1e-06
        strength = coherence * (scale * scale)
        for rows in ifg_tiles:
            left = residual[rows, :]
            inverse = pl.reciprocal(left * left + scale, approx=APPROX)
            moved[rows, :] = ((inverse * left) * (inverse * strength)).astype(jnp.bfloat16)

    left_columns = pl.ds(done, ifg_total - done)
    twice = jnp.concatenate([data[...], data[...]], axis=0)
    tops, lows = [], []
    for rows in date_tiles:
        parts = [gain_top[rows, left_columns], gain_low[rows, left_columns]]
        part = product(jnp.concatenate(parts, axis=1), twice)
        if early_refs:
            part = part + early_series[rows, :]
        series_ref[rows, :] = part
        top, low = halves(part)
        tops.append(top)
        lows.append(low)
    both = jnp.concatenate(tops + spare + lows + spare, axis=0)
    total = jnp.zeros((8, pixel_count), jnp.float32)
    for rows in ifg_tiles:
        left = observed(rows).astype(jnp.float32) - product(incidence[rows, :], both)
        residual[rows, :] = left
        total = total + folded(left * left)
    reweighted(total, moved.at[0])
    for sweep in range(1, REWEIGHTS):
        steps = []
        for rows in date_tiles:
            part = gained(gain_top, None, rows, everything, moved[sweep - 1])
            steps.append(part.astype(jnp.bfloat16))
            series_ref[rows, :] = series_ref[rows, :] + part
        step = jnp.concatenate(steps + spare, axis=0)
        total = jnp.zeros((8, pixel_count), jnp.float32)
        for rows in ifg_tiles:
            left = residual[rows, :] - product(incidence[rows, :date_pad], step)
            residual[rows, :] = left
            total = total + folded(left * left)
        reweighted(total, moved.at[sweep])
        for rows in date_tiles:
            series_ref[rows, :] = series_ref[rows, :] + product(gain_low[rows, :], moved[sweep - 1])
    for rows in date_tiles:
        part = gained(gain_top, None, rows, everything, moved[REWEIGHTS - 1])
        series_ref[rows, :] = series_ref[rows, :] + part
    series_ref[pl.ds(date_total, 8), :] = basis_ref[...]
    series_top, series_low = halves(series_ref[...])
    weighted_top, weighted_low = halves(weighted_ref[...])
    count = weighted_top.shape[0]
    across = (((1,), (1,)), ((), ()))
    first = product(jnp.concatenate([weighted_top, weighted_low], axis=0), series_top, across)
    moments_ref[...] = first[:count] + (first[count:] + product(weighted_top, series_low, across))


def invert(late_chunks, early, incidence, gains, weighted, basis, row_local, date_total):
    ifg_total = incidence.shape[0]
    kept = sum(value.shape[0] for value in early[:-1]) // 128 * 128
    date_rows = gains[0].shape[0]
    pixel_count = weighted.shape[1]
    return pl.pallas_call(
        functools.partial(
            invert_kernel, row_local=row_local, date_total=date_total, late=len(late_chunks)
        ),
        out_shape=[
            jax.ShapeDtypeStruct((date_rows, pixel_count), jnp.float32),
            jax.ShapeDtypeStruct((weighted.shape[0], date_rows), jnp.float32),
        ],
        scratch_shapes=[
            pltpu.VMEM(late_chunks[0].shape, jnp.float32),
            pltpu.VMEM((ifg_total - kept, pixel_count), jnp.bfloat16),
            pltpu.VMEM((ifg_total, pixel_count), jnp.float32),
            pltpu.VMEM((REWEIGHTS, ifg_total, pixel_count), jnp.bfloat16),
        ],
        compiler_params=pltpu.CompilerParams(vmem_limit_bytes=VMEM_LIMIT),
        name="invert",
    )(*late_chunks, *early, incidence, *gains, weighted, basis)


def cut_kernel(source, *refs):
    sems = refs[-1]
    extra = len(refs) - 1 - source.shape[1]
    extra //= 2
    small, targets, fetched = refs[:extra], refs[extra:-1 - extra], refs[-1 - extra : -1]
    place = lax.axis_index("stack")
    copies = [
        pltpu.make_async_copy(source.at[:, place ^ mask], target, sems.at[mask])
        for mask, target in enumerate(targets)
    ]
    copies += [
        pltpu.make_async_copy(value, target, sems.at[len(targets) + index])
        for index, (value, target) in enumerate(zip(small, fetched))
    ]
    for copy in copies:
        copy.start()
    for copy in copies:
        copy.wait()


def cut(phases, col_local, small):
    ifg_local, row_local, col_range = phases.shape
    count = col_range // col_local
    view = phases.reshape(ifg_local, row_local, count, col_local).transpose(0, 2, 1, 3)
    shapes = [jax.ShapeDtypeStruct((ifg_local, row_local, col_local), phases.dtype)] * count
    shapes += [jax.ShapeDtypeStruct(value.shape, value.dtype) for value in small]
    arguments = (view, *small)
    results = pl.pallas_call(
        cut_kernel,
        out_shape=shapes,
        in_specs=[pl.BlockSpec(memory_space=pltpu.HBM)] * len(arguments),
        out_specs=[pl.BlockSpec(memory_space=pltpu.VMEM)] * len(shapes),
        scratch_shapes=[pltpu.SemaphoreType.DMA((len(shapes),))],
        compiler_params=pltpu.CompilerParams(vmem_limit_bytes=8 * 1024 * 1024),
        name="cut",
    )(*(pltpu.with_memory_space_constraint(value, pltpu.HBM) for value in arguments))
    return results[:count], results[count:]


def exchange(phases, small, stack_size):
    ifg_local, row_local, col_range = phases.shape
    col_local = col_range // stack_size
    if stack_size != 8:
        blocks = phases.reshape(ifg_local, row_local, stack_size, col_local).transpose(2, 0, 1, 3)
        stacked = lax.all_to_all(blocks, "stack", split_axis=0, concat_axis=0, tiled=True)
        return [stacked.reshape(-1, col_local)], small, (0,)
    blocks, small = cut(phases, col_local, small)
    found = {0: blocks[0]}

    for mask in ARRIVAL[1:]:
        pairs = [(i, i ^ mask) for i in range(stack_size)]
        found[mask] = lax.ppermute(blocks[mask], "stack", pairs)
    return [found[mask].reshape(-1, col_local) for mask in ARRIVAL], small, ARRIVAL


def plane_weights(gram_matrix, basis):
    def entry(row_pos, col_pos):
        return gram_matrix[row_pos % 3][col_pos % 3]

    cofactors = [
        [
            entry(row_pos + 1, col_pos + 1) * entry(row_pos + 2, col_pos + 2)
            - entry(row_pos + 1, col_pos + 2) * entry(row_pos + 2, col_pos + 1)
            for col_pos in range(3)
        ]
        for row_pos in range(3)
    ]
    inverse = 1.0 / (
        entry(0, 0) * cofactors[0][0]
        + entry(0, 1) * cofactors[0][1]
        + entry(0, 2) * cofactors[0][2]
    )
    return [
        (cofactors[row_pos][0] * inverse) * basis[0]
        + (cofactors[row_pos][1] * inverse) * basis[1]
        + (cofactors[row_pos][2] * inverse) * basis[2]
        for row_pos in range(3)
    ]


def deramp_kernel(first_ref, *refs, row_local, date_total):
    *others, series_ref, member_ref, out_ref, staged, sems = refs
    totals = first_ref[...]
    for other in others:
        totals = totals + other[...]
    sums = [
        jnp.concatenate([totals[2 * k : 2 * k + 2], totals[8 + 2 * k : 10 + 2 * k]], axis=0)
        for k in range(3)
    ]
    wide = (sums[0].shape[0], member_ref.shape[1])
    gram = [
        [
            jnp.broadcast_to(sums[k][:, date_total + m : date_total + m + 1], wide)
            + (1.0 if k == m else 0.0)
            for m in range(3)
        ]
        for k in range(3)
    ]
    weights = plane_weights(gram, [member_ref[4 * k : 4 * k + 4, :] for k in range(3)])
    spare = 4
    weights_top, weights_low = halves(
        jnp.concatenate(weights + [jnp.zeros((spare, weights[0].shape[1]), jnp.float32)], axis=0)
    )
    sums_top, sums_low = halves(
        jnp.concatenate(sums + [jnp.zeros((spare, sums[0].shape[1]), jnp.float32)], axis=0)
    )
    ramp = product(
        jnp.concatenate([sums_top, sums_low, sums_top], axis=0),
        jnp.concatenate([weights_top, weights_top, weights_low], axis=0),
        (((0,), (0,)), ((), ())),
    )
    col_local = series_ref.shape[1] // row_local
    copies = []
    step = date_total // OUT_PARTS
    for part in range(OUT_PARTS):
        start = part * step
        flat = series_ref[pl.ds(start, step), :] - ramp[start : start + step]
        for row in range(row_local):
            staged[pl.ds(start * row_local + row, step, stride=row_local), :] = flat[
                :, row * col_local : (row + 1) * col_local
            ]
        rows = pl.ds(start * row_local, step * row_local)
        copy = pltpu.make_async_copy(staged.at[rows], out_ref.at[rows], sems.at[part])
        copy.start()
        copies.append(copy)
    for copy in copies:
        copy.wait()


def deramp(parts, series, member, row_local, date_total):
    col_local = series.shape[1] // row_local
    shape = (date_total * row_local, col_local)
    whole = pl.BlockSpec(memory_space=pltpu.VMEM)
    return pl.pallas_call(
        functools.partial(deramp_kernel, row_local=row_local, date_total=date_total),
        out_shape=jax.ShapeDtypeStruct(shape, jnp.float32),
        in_specs=[whole] * (len(parts) + 2),
        out_specs=pl.BlockSpec(memory_space=pl.ANY),
        scratch_shapes=[pltpu.VMEM(shape, jnp.float32), pltpu.SemaphoreType.DMA((OUT_PARTS,))],
        compiler_params=pltpu.CompilerParams(vmem_limit_bytes=VMEM_LIMIT),
        name="deramp",
    )(*parts, series, member)


def swap(value, axes, pairs):
    both = [(i, j) for i, j in pairs] + [(j, i) for i, j in pairs]
    return lax.ppermute(value, axes, both)


def local(phases, ifg_pairs, preconditioner, coherence, geo_tiles):
    stack_size = lax.axis_size("stack")
    range_size = lax.axis_size("range")
    azimuth_size = lax.axis_size("azimuth")
    ifg_local, row_local, col_range = phases.shape
    date_total = preconditioner.shape[0]
    date_rows = -(-(date_total + 8) // 32) * 32
    date_pad = -(-date_rows // LANES) * LANES

    small = (ifg_pairs.T, coherence, geo_tiles)
    chunks, small, order = exchange(phases, small, stack_size)
    incidence, *gains, member, weighted, basis = prepare(
        preconditioner, small, date_pad, date_rows, order,
        col_range * range_size, row_local * azimuth_size,
    )
    early = []
    if len(chunks) > 1:
        first, second = EARLY
        count = ifg_local * first // 256 * 256
        data_a, series_a = early_fit(chunks[:first], [], gains, row_local, 0, count)
        data_b, series_b = early_fit(
            chunks[first:second], [data_a, series_a], gains, row_local, count,
            ifg_local * second // 128 * 128,
        )
        early = [data_a, data_b, series_b]
        chunks = chunks[second:]

    series, moments = invert(
        chunks, early, incidence, gains, weighted, basis, row_local, date_total
    )

    def place(block):
        return (block % stack_size) * range_size + block // stack_size

    block_count = stack_size * range_size
    inner = [
        (place(block), place(block + 2)) for block in range(block_count - 2) if block // 2 % 2 == 0
    ]
    outer = [
        (place(block), place(block + 2)) for block in range(block_count - 2) if block // 2 % 2 == 1
    ]
    axes = ("stack", "range")
    outer += [(place(0), place(1)), (place(block_count - 2), place(block_count - 1))]
    first = swap(moments[:8], axes, outer)
    node = (lax.axis_index("range") * stack_size + lax.axis_index("stack")) // 2
    first = jnp.where((node > 0) & (node < block_count // 2 - 1), first, 0.0)
    second = swap(moments[8:], axes, inner)
    moments = moments + jnp.concatenate([first, second], axis=0)
    pairs = [(i, i + 1) for i in range(0, stack_size, 2)]
    crossed = [
        (i * azimuth_size + a, (i + 1) * azimuth_size + (azimuth_size - 1 - a))
        for i in range(0, stack_size, 2)
        for a in range(azimuth_size)
    ]
    parts = [
        moments,
        swap(moments, ("stack", "azimuth"), crossed),
        swap(moments, "stack", pairs),
        swap(moments, "azimuth", [(0, 1)]),
    ]
    flat = deramp(parts, series, member, row_local, date_total)
    return flat.reshape(date_total, row_local, -1)


def solution(mesh):
    return jax.shard_map(
        local,
        mesh=mesh,
        in_specs=(
            P("stack", "azimuth", "range"),
            P(),
            P(),
            P("azimuth", ("range", "stack")),
            P("azimuth", ("range", "stack")),
        ),
        out_specs=P(None, "azimuth", ("range", "stack")),
        check_vma=False,
    )
```
